256 devices in a mesh: fft: 32 (over z, y), grp: 8 (over x, core).
Axes of the slice: x: 4, y: 4, z: 8, core: 2. Of those that a mesh axis runs over, the one named last changes fastest.
Arguments:
- root_density: float32 [768, 768, 128], P('fft', 'grp'), may hold values from -8 to 8
- patch_fluid: float32 [5, 12, 12, 12, 8192], P(None, None, None, None, ('fft', 'grp')), may hold values from -5 to 60, as said below
- ghost_list: int32 [2, 256, 64], P(None, ('fft', 'grp')), may hold values from -1 to 4607, as said below
Outputs:
- root_potential: float32 [768, 768, 128], P('fft', 'grp')
- fine_potential: float32 [8, 8, 8, 8192], P(None, None, None, ('fft', 'grp'))
- fluid_next: float32 [5, 8, 8, 8, 8192], P(None, None, None, None, ('fft', 'grp'))
The draws below stay inside these ranges and needn't reach their ends.
Inputs may be any that keep to these rules, and one draw needn't show every extreme that they name: `ghost_list`: in each used column (slot >= 0) field 0 names a corner as in the reference program, field 1 a slot of the receiving device; both fields are -1 in unused columns. Every slot of every device is named exactly once, no two patches share a corner, every device receives exactly 2 patches from some one sender, and every sending device uses its last corner in some column. `patch_fluid`: density and pressure are positive in every cell.
All inputs are finite; a program needn't handle non-finite values.
Results may differ from the reference program's by a relative error of at most 0.0003.
Values sent between devices are 32-bit elements; how exact they have to be, the bound alone decides.
A program may use at most 192 MiB of HBM per device.

```python
import math
import jax
import jax.numpy as jnp
import numpy as np
from jax import lax

CX = 24
CY = 96
NZ = 128
P_DEV = 32
SWEEPS = 8
NV = 5
NX = 768
NY = 768
PATCHES = 8192
GCAP = 2
SENDS = 64
N_FFT = 32
N_GRP = 8


GAMMA = 5.0 / 3.0


def draw_root_density(key, part):
    key = jax.random.fold_in(key, 5)
    shape = (NX, NY, NZ)
    return jnp.clip(jax.random.normal(key, shape, jnp.float32), -7.5, 7.5)


def draw_patch_fluid(key, part):
    key = jax.random.fold_in(key, 11)
    keys = jax.random.split(key, 3)
    shape = (12, 12, 12, PATCHES)
    rank = (jnp.arange(PATCHES, dtype=jnp.int32) // P_DEV).astype(jnp.float32)
    top = max(PATCHES // P_DEV - 1, 1)
    dens = jnp.exp(jax.random.uniform(keys[0], shape, jnp.float32, minval=math.log(0.5), maxval=math.log(2.0)))
    vel = jnp.clip(0.5 * jax.random.normal(keys[1], (3,) + shape, jnp.float32), -1.5, 1.5)
    pres = jnp.exp(jax.random.uniform(keys[2], shape, jnp.float32, minval=math.log(0.5), maxval=math.log(2.0)))
    pres = pres * (1.0 + 8.0 * rank / top)
    energy = pres / (GAMMA - 1.0) + 0.5 * dens * jnp.sum(vel * vel, axis=0)
    return jnp.concatenate([dens[None], dens * vel, energy[None]], axis=0).astype(jnp.float32)


def shuffle_row(row_key, length):
    return jax.random.permutation(row_key, length)


def partial_shuffle(length):

    def shuffled(row_key):
        return shuffle_row(row_key, length)
    return shuffled


def draw_ghost_list(key, part):
    key = jax.random.fold_in(key, 7)
    pick_key, forced_key, place_key = jax.random.split(key, 3)
    owners = N_FFT * N_GRP
    virtual = jnp.arange(SENDS, dtype=jnp.int32)
    source = virtual // GCAP
    ranks = jax.vmap(partial_shuffle(SENDS))(jax.random.split(pick_key, owners)).astype(jnp.int32)
    forced = jax.random.randint(forced_key, (owners, 1), 0, N_FFT, dtype=jnp.int32)
    priority = ranks + jnp.where(source[None, :] == forced, SENDS, 0)
    order = jnp.argsort(-priority, axis=1)
    chosen = order[:, :P_DEV]
    slots = jnp.full((owners, SENDS), -1, jnp.int32)
    slots = slots.at[jnp.arange(owners, dtype=jnp.int32)[:, None], chosen].set(jnp.arange(P_DEV, dtype=jnp.int32)[None, :])
    slots = slots.reshape(N_GRP, N_FFT, N_FFT, GCAP).transpose(2, 0, 1, 3).reshape(owners, SENDS)
    positions = CX // 4 * (CY // 4) * (NZ // 4)
    places = jax.vmap(partial_shuffle(positions))(jax.random.split(place_key, owners))[:, :SENDS].astype(jnp.int32)
    row_index = jnp.arange(owners, dtype=jnp.int32)
    first_used = jnp.argmax((slots >= 0).astype(jnp.int32), axis=1).astype(jnp.int32)
    held = places[row_index, first_used]
    places = jnp.where(places == positions - 1, held[:, None], places)
    places = places.at[row_index, first_used].set(positions - 1)
    corner = jnp.where(slots >= 0, places, -1)
    return jnp.stack([corner, slots]).astype(jnp.int32)


def setup_inputs(seed: int = 0) -> dict:
    key_of = jax.random.split(jax.random.key(seed), 4)
    root_density = draw_root_density(jax.random.fold_in(key_of[3], 71), 0)
    patch_fluid = draw_patch_fluid(jax.random.fold_in(key_of[3], 71), 0)
    ghost_list = draw_ghost_list(jax.random.fold_in(key_of[3], 71), 0)
    return {"root_density": root_density, "patch_fluid": patch_fluid, "ghost_list": ghost_list}


GAMMA = 5.0 / 3.0
SCREEN = 0.0006
OMEGA = 1.5
COURANT = 0.4
FINE_STEP = 0.5
HIGH = lax.Precision.HIGHEST

def sine_table(count):
    index = jnp.arange(count, dtype=jnp.int32) + 1
    phase = index[:, None] * index[None, :] % (2 * (count + 1))
    return math.sqrt(2.0 / (count + 1)) * jnp.sin(jnp.pi * phase.astype(jnp.float32) / (count + 1))

def eigen(count, index):
    half = jnp.sin(jnp.pi * (index + 1).astype(jnp.float32) / (2 * (count + 1)))
    return 4.0 * half * half

def spread_table():
    table = np.zeros((10, 6), np.float32)
    for fine in range(10):
        where_at = fine / 2.0 + 0.25
        lower = int(np.floor(where_at))
        frac = where_at - lower
        table[fine, lower] += 1.0 - frac
        table[fine, lower + 1] += frac
    return table

def block_offsets(stride_y, stride_z):
    cube = jnp.arange(6, dtype=jnp.int32)
    return ((cube[:, None, None] * stride_y + cube[None, :, None]) * stride_z + cube[None, None, :]).reshape(-1)

def primitives(fluid):
    dens = fluid[0]
    vel = fluid[1:4] / dens
    kinetic = 0.5 * lax.optimization_barrier(jnp.sum(fluid[1:4] * vel, axis=0))
    pres = (GAMMA - 1.0) * (fluid[4] - kinetic)
    return (dens, vel, pres)

def signal_speed(fluid):
    dens, vel, pres = primitives(fluid[:, 2:10, 2:10, 2:10])
    sound = jnp.sqrt(GAMMA * pres / dens)
    return jnp.max(lax.optimization_barrier(jnp.max(jnp.abs(vel), axis=0)) + sound)

def along(array, axis, start, stop):
    return lax.slice_in_dim(array, start, stop, axis=axis + 1)

def conserved_flux(state, axis):
    dens = state[0]
    vel = state[1:4]
    pres = state[4]
    normal = vel[axis]
    energy = pres / (GAMMA - 1.0) + 0.5 * dens * lax.optimization_barrier(jnp.sum(vel * vel, axis=0))
    cons = jnp.stack([dens, dens * vel[0], dens * vel[1], dens * vel[2], energy])
    moment = [dens * normal * vel[other] + (pres if other == axis else 0.0) for other in range(3)]
    flux = jnp.stack([dens * normal, moment[0], moment[1], moment[2], (energy + pres) * normal])
    speed = jnp.abs(normal) + jnp.sqrt(GAMMA * pres / dens)
    return (cons, flux, speed)

def flux_difference(prim, axis):
    for other in range(3):
        if other != axis:
            prim = along(prim, other, 2, 10)
    left_diff = along(prim, axis, 1, 11) - along(prim, axis, 0, 10)
    right_diff = along(prim, axis, 2, 12) - along(prim, axis, 1, 11)
    slope = 0.5 * (jnp.sign(left_diff) + jnp.sign(right_diff)) * jnp.minimum(jnp.abs(left_diff), jnp.abs(right_diff))
    centre = along(prim, axis, 1, 11)
    upper = centre + 0.5 * slope
    lower = centre - 0.5 * slope
    cons_left, flux_left, speed_left = conserved_flux(along(upper, axis, 0, 9), axis)
    cons_right, flux_right, speed_right = conserved_flux(along(lower, axis, 1, 10), axis)
    flux = 0.5 * (flux_left + flux_right) - 0.5 * jnp.maximum(speed_left, speed_right) * (cons_right - cons_left)
    return along(flux, axis, 1, 9) - along(flux, axis, 0, 8)

def advance(fluid, field, step):
    dens, vel, pres = primitives(fluid)
    prim = jnp.concatenate([dens[None], vel, pres[None]], axis=0)
    change = flux_difference(prim, 0) + flux_difference(prim, 1) + flux_difference(prim, 2)
    inner = fluid[:, 2:10, 2:10, 2:10]
    moved = inner - step / FINE_STEP * change
    pull = -jnp.stack([field[2:, 1:-1, 1:-1] - field[:-2, 1:-1, 1:-1], field[1:-1, 2:, 1:-1] - field[1:-1, :-2, 1:-1], field[1:-1, 1:-1, 2:] - field[1:-1, 1:-1, :-2]]) / (2.0 * FINE_STEP)
    momenta = moved[1:4] + step * inner[0] * pull
    energy = moved[4] + step * lax.optimization_barrier(jnp.sum(inner[1:4] * pull, axis=0))
    return jnp.concatenate([moved[0:1], momenta, energy[None]], axis=0)

def spread(coarse, count):
    table = jnp.asarray(spread_table())
    block = coarse.reshape(6, 6, 6, count)
    block = jnp.einsum('ia,abcp->ibcp', table, block, precision=HIGH)
    block = jnp.einsum('jb,ibcp->ijcp', table, block, precision=HIGH)
    return jnp.einsum('kc,ijcp->ijkp', table, block, precision=HIGH)

def relax(field, dens):
    index = jnp.arange(8, dtype=jnp.int32)
    parity = (index[:, None, None] + index[None, :, None] + index[None, None, :]) % 2
    scale = 1.0 / (6.0 + SCREEN * FINE_STEP * FINE_STEP)
    for sweep in range(SWEEPS):
        for colour in (0, 1):
            near = field[2:, 1:-1, 1:-1] + field[:-2, 1:-1, 1:-1] + field[1:-1, 2:, 1:-1] + field[1:-1, :-2, 1:-1] + field[1:-1, 1:-1, 2:] + field[1:-1, 1:-1, :-2]
            inner = field[1:-1, 1:-1, 1:-1]
            moved = (1.0 - OMEGA) * inner + OMEGA * scale * (near - FINE_STEP * FINE_STEP * dens)
            inner = jnp.where((parity == colour)[..., None], moved, inner)
            field = field.at[1:-1, 1:-1, 1:-1].set(inner)
    return field

def refine(fluid, coarse, step):
    count = fluid.shape[-1]
    field = relax(spread(coarse, count), fluid[0, 2:10, 2:10, 2:10])
    return (field[1:-1, 1:-1, 1:-1], advance(fluid, field, step))

def solve_root(density):
    table_x = sine_table(NX)
    table_y = sine_table(NY)
    table_z = sine_table(NZ)
    spec = jnp.einsum('xyz,kz->xyk', density, table_z, precision=HIGH)
    spec = jnp.einsum('kx,xyz->kyz', table_x, spec, precision=HIGH)
    spec = jnp.einsum('ky,xyz->xkz', table_y, spec, precision=HIGH)
    total = eigen(NX, jnp.arange(NX, dtype=jnp.int32))[:, None, None] + eigen(NY, jnp.arange(NY, dtype=jnp.int32))[None, :, None] + eigen(NZ, jnp.arange(NZ, dtype=jnp.int32))[None, None, :] + SCREEN
    spec = -spec / total
    spec = jnp.einsum('ky,xyz->xkz', table_y, spec, precision=HIGH)
    spec = jnp.einsum('kx,xyz->kyz', table_x, spec, precision=HIGH)
    return jnp.einsum('xyz,kz->xyk', spec, table_z, precision=HIGH)

def gather_coarse(potential, ghost_list):
    corner = ghost_list[0]
    slot = ghost_list[1]
    ranks = jnp.arange(N_FFT * N_GRP, dtype=jnp.int32)
    fft_of = ranks // N_GRP
    grp_of = ranks % N_GRP
    column = jnp.arange(SENDS, dtype=jnp.int32)
    owner = (column // GCAP)[None, :] * N_GRP + grp_of[:, None]
    patch = jnp.where(slot >= 0, owner * P_DEV + slot, PATCHES)
    code = jnp.maximum(corner, 0)
    per_z = NZ // 4
    per_y = CY // 4
    start_x = fft_of[:, None] * CX + 4 * (code // (per_y * per_z))
    start_y = grp_of[:, None] * CY + 4 * (code // per_z % per_y)
    start_z = 4 * (code % per_z)
    start = (start_x * (NY + 2) + start_y) * (NZ + 2) + start_z
    starts = jnp.zeros((PATCHES,), jnp.int32).at[patch.reshape(-1)].set(start.reshape(-1), mode='drop')
    flat = jnp.pad(potential, 1).reshape(-1)
    offsets = block_offsets(NY + 2, NZ + 2)
    return flat[starts[None, :] + offsets[:, None]]

def reference(root_density, patch_fluid, ghost_list):
    potential = solve_root(root_density)
    coarse = gather_coarse(potential, ghost_list)
    owners = PATCHES // P_DEV

    def block_speed(index):
        return signal_speed(lax.dynamic_slice_in_dim(patch_fluid, index * P_DEV, P_DEV, axis=4))
    speed = jnp.max(lax.map(block_speed, jnp.arange(owners, dtype=jnp.int32)))
    step = COURANT * FINE_STEP / speed

    def block_refine(index):
        fluid = lax.dynamic_slice_in_dim(patch_fluid, index * P_DEV, P_DEV, axis=4)
        piece = lax.dynamic_slice_in_dim(coarse, index * P_DEV, P_DEV, axis=1)
        return refine(fluid, piece, step)
    fields, fluids = lax.map(block_refine, jnp.arange(owners, dtype=jnp.int32))
    fine = jnp.moveaxis(fields, 0, 3).reshape(8, 8, 8, PATCHES)
    fluid_next = jnp.moveaxis(fluids, 0, 4).reshape(NV, 8, 8, 8, PATCHES)
    return (potential, fine, fluid_next)
```

```python
import functools

import jax
import jax.numpy as jnp
import ml_dtypes
import numpy as np
from jax import lax
from jax.experimental import pallas as pl
from jax.experimental.pallas import tpu as pltpu
from jax.sharding import PartitionSpec as P

SWEEPS = 8
GAMMA = 5.0 / 3.0
SCREEN = 0.0006
OMEGA = 1.5
COURANT = 0.4
FINE_STEP = 0.5
F32 = jnp.float32
BF16 = jnp.bfloat16


def sine(count):
    index = np.arange(1, count + 1)
    return np.sqrt(2.0 / (count + 1)) * np.sin(
        np.pi * (np.outer(index, index) % (2 * (count + 1))) / (count + 1)
    )


def eigen(count):
    return 4.0 * np.sin(np.pi * np.arange(1, count + 1) / (2 * (count + 1))) ** 2


def halves(table):
    high = table.astype(ml_dtypes.bfloat16)
    low = (table - high.astype(np.float64)).astype(ml_dtypes.bfloat16)
    return np.stack([high, low])


@functools.lru_cache(None)
def tables(nf, ng, cx, cy, nz):
    ny = ng * cy
    kz = nz // ng
    sz, sy, sx, full = sine(nz), sine(cy), sine(cx), sine(ny)
    lam = eigen(cy)[:, None] + eigen(nz)[None, :] + SCREEN
    steps = [1.0 / (2.0 + lam)]
    for _ in range(1, cx // 2):
        steps.append(1.0 / (2.0 + lam - steps[-1]))
    steps.append(1.0 / (1.0 - steps[-1] ** 2))
    edge = np.zeros((ng, 2, ny))
    wide = np.zeros((ng, 128, ny))
    back = np.zeros((ng, 128, ny))
    for d in range(ng):
        if d > 0:
            edge[d, 0] = full[d * cy - 1]
        if d < ng - 1:
            edge[d, 1] = full[(d + 1) * cy]
        wide[d, :cy] = sy @ full[d * cy : (d + 1) * cy]
        back[d, :cy] = wide[d, :cy]
        back[d, cy + cx] = edge[d, 0]
        back[d, cy + cx + 1] = edge[d, 1]
    repeated = np.repeat(edge.reshape(2 * ng, ny), kz, axis=0)
    denom = (
        eigen(cx)[None, :, None, None]
        + eigen(nz).reshape(ng, 1, kz, 1)
        + eigen(ny)[None, None, None, :]
        + SCREEN
    )
    phi = 2.0 * np.arcsinh(np.sqrt(eigen(ny)[None, :] + eigen(nz)[:, None] + SCREEN) / 2.0)

    def ratio(m, n):
        return np.exp(-(n - m) * phi) * np.expm1(-2 * m * phi) / np.expm1(-2 * n * phi)

    pair = np.zeros((ng, nf, 2, 8, 128))
    for i, values in enumerate((ratio(cx - 1, cx), ratio(1, cx))):
        pair[:, :, i, :3] = values.reshape(ng, nf, 3, 128)
    spread = np.zeros((10, 6))
    for j in range(10):
        at = j / 2 + 0.25
        low = int(np.floor(at))
        spread[j, low] += 1 - (at - low)
        spread[j, low + 1] += at - low
    inner = np.zeros((8, 8))
    inner[:, :6] = spread[1:9]
    outer = np.zeros((8, 8))
    outer[0, :6] = spread[0]
    outer[7, :6] = spread[9]
    weave = np.concatenate([np.kron(np.eye(16), inner), np.kron(np.eye(16), outer)])
    lanes = np.arange(128)
    fold = ((lanes[:, None] + 1) % 8 == lanes[None, :] % 8).astype(np.float64)
    column = np.broadcast_to(sy[0][:, None], (cy, 128))
    as32 = lambda t: np.ascontiguousarray(t, dtype=np.float32)
    szh, szl = halves(sz)
    return dict(
        sz=np.block([[szh, szl], [szh, np.zeros_like(szh)]]).astype(ml_dtypes.bfloat16),
        sy=halves(sy),
        sx=as32(sx),
        steps=as32(np.stack(steps)),
        wide=halves(wide.reshape(ng * 128, ny)),
        back=halves(np.ascontiguousarray(back.reshape(ng * 128, ny).T)),
        edge=halves(repeated),
        edget=halves(np.ascontiguousarray(repeated.T)),
        inv=as32(1.0 / denom),
        pair=as32(pair),
        weave=weave.astype(ml_dtypes.bfloat16),
        fold=np.concatenate([fold, fold]).astype(ml_dtypes.bfloat16),
        column=as32(column),
    )


NAMES = (
    "sz", "sy", "sx", "steps", "wide", "back", "edge", "edget", "inv", "pair", "weave", "fold", "column",
)


def split(value):
    high = value.astype(BF16)
    return high, (value - high.astype(F32)).astype(BF16)


def mm(a, b):
    return jnp.dot(a, b, preferred_element_type=F32)


def dot_right(value, high, low):
    a, b = split(value)
    return mm(a, high) + (mm(b, high) + mm(a, low))


def dot_left(high, low, value):
    a, b = split(value)
    return mm(high, a) + (mm(high, b) + mm(low, a))


def root_kernel(
    cfg,
    ghost, rho, speed, fluid, change,
    sz_h, sy_h, sx_h, steps_h, wide_h, back_h, edge_h, edget_h, inv_h, pair_h, weave_h, fold_h, column_h,
    pot_h, fine, moved,
    src, sz, sy, sx, steps, wide, back, edge, edget, inv, pair, weave, fold, column,
    block, solved, part, grid, hfield,
    s1, r1, s2, r2, s3, r3, s4, r4, s6, r6, chain, mults, field, ghosts, force,
    tsem, osem, s1s, r1s, s2s, r2s, s3s, r3s, s4s, r4s, s6s, r6s,
):
    nf, ng, cx, cy, nz = cfg
    kz = nz // ng
    ny = ng * cy
    half = cx // 2
    f = lax.axis_index("fft")
    g = lax.axis_index("grp")

    barrier = pltpu.get_barrier_semaphore()

    def hello(axis, pos, count):
        def body(k, _):
            pl.semaphore_signal(
                barrier, inc=1, device_id={axis: lax.rem(pos + k, count)},
                device_id_type=pl.DeviceIdType.MESH,
            )
            return 0
        lax.fori_loop(1, count, body, 0)

    hello("grp", g, ng)
    hello("fft", f, nf)

    loads = {}
    order = [
        ("rho", rho, src), ("sz", sz_h, sz), ("sy", sy_h, sy), ("steps", steps_h, steps),
        ("column", column_h, column), ("pair", pair_h.at[g, f], pair), ("wide", wide_h, wide),
        ("sx", sx_h, sx), ("edge", edge_h, edge), ("inv", inv_h.at[g], inv),
        ("edget", edget_h, edget), ("back", back_h, back), ("fold", fold_h, fold), ("weave", weave_h, weave),
    ]
    for i, (name, a, b) in enumerate(order):
        loads[name] = pltpu.make_async_copy(a, b, tsem.at[i])
        loads[name].start()

    sub = lax.broadcasted_iota(jnp.int32, (8, 128), 0)
    even = lax.rem(sub, 2) == 0

    loads["rho"].wait()
    loads["sz"].wait()
    loads["sy"].wait()

    def forward(i, _):
        rows = src[pl.ds(2 * i, 2)].reshape(2 * cy, nz)
        a, b = split(rows)
        both = mm(jnp.concatenate([a, b], axis=1), sz[...])
        both = both[:, :nz] + both[:, nz:]
        pair_x = jnp.concatenate([both[:cy], both[cy:]], axis=1)
        out = dot_left(sy[0], sy[1], pair_x)
        block[2 * i] = out[:, :nz]
        block[2 * i + 1] = out[:, nz:]
        return 0

    lax.fori_loop(0, half, forward, 0)

    loads["steps"].wait()
    loads["column"].wait()

    def solve(fetch, i):
        at = pl.ds(pl.multiple_of(16 * i, 16), 16)
        low, high = [], []
        for j in range(half):
            m = steps[j, at, :]
            a, b = fetch(j, at), fetch(cx - 1 - j, at)
            if j == 0:
                low.append(-m * a)
                high.append(-m * b)
            else:
                low.append(m * (low[-1] - a))
                high.append(m * (high[-1] - b))
        m, scale = steps[half - 1, at, :], steps[half, at, :]
        a, b = low[-1], high[-1]
        low[-1] = (a + m * b) * scale
        high[-1] = (b + m * a) * scale
        for j in range(half - 2, -1, -1):
            m = steps[j, at, :]
            low[j] = low[j] + m * low[j + 1]
            high[j] = high[j] + m * high[j + 1]
        return at, low + high[::-1]

    part[...] = jnp.zeros_like(part)

    def first(i, _):
        at, values = solve(lambda x, at: block[x, at, :], i)
        col = column[at, :]
        for x in range(cx):
            v = values[x] * col
            part[x] += v[:8] + v[8:]
        solved[0, at, :] = values[0]
        solved[1, at, :] = values[cx - 1]
        return 0

    lax.fori_loop(0, cy // 16, first, 0)
    sums = part[...]
    sign = jnp.where(even, 1.0, -1.0)
    edges = (jnp.sum(sums, axis=1), jnp.sum(sums * sign[None], axis=1))
    for e in range(2):
        solved[e, pl.ds(cy, cx), :] = edges[e]
        solved[e, pl.ds(cy + cx, 8), :] = speed[...]
        s1[e] = solved[e].T

    pl.semaphore_wait(barrier, ng + nf - 2)

    def send(axis, pos, count, source, target, sends, recvs):
        def body(k, _):
            to = lax.rem(pos + k, count)
            pltpu.make_async_remote_copy(
                source(to), target(pos), sends.at[k], recvs.at[k], device_id={axis: to},
                device_id_type=pl.DeviceIdType.MESH,
            ).start()
            return 0
        lax.fori_loop(1, count, body, 0)

    def receive(axis, pos, count, source, target, sends, recvs):
        def body(k, _):
            come = lax.rem(pos + (count - k), count)
            pltpu.make_async_remote_copy(
                source(come), target(come), sends.at[k], recvs.at[k], device_id={axis: come},
                device_id_type=pl.DeviceIdType.MESH,
            ).wait()
            return 0
        lax.fori_loop(1, count, body, 0)

    slice1 = lambda d: s1.at[:, pl.ds(pl.multiple_of(d * kz, kz), kz), :]
    ex1 = ("grp", g, ng, slice1, lambda d: r1.at[d], s1s, r1s)
    send(*ex1)
    r1[g] = s1[:, pl.ds(pl.multiple_of(g * kz, kz), kz), :]

    loads["pair"].wait()
    ca, cb = pair[0], pair[1]
    ca2, cb2 = ca * ca, cb * cb

    def coefficients(i, m):
        m0 = 1.0 / (1.0 - ca2 * m)
        mults[2 * i] = m0
        m1 = 1.0 / (1.0 - cb2 * m0)
        mults[2 * i + 1] = m1
        return m1

    lax.fori_loop(0, nf, coefficients, jnp.zeros((8, 128), F32))
    loads["wide"].wait()
    loads["sx"].wait()
    loads["edge"].wait()
    loads["inv"].wait()
    receive(*ex1)

    main = jnp.concatenate([r1[d].reshape(2 * kz, 128) for d in range(ng)], axis=1)
    main = dot_right(main, wide[0], wide[1])
    across = r1[...].reshape(ng * 2 * kz, 128).T
    edge_x = across[cy : cy + cx]
    most = across[cy + cx : cy + cx + 8]
    most = jnp.max(jnp.maximum(most[:, :128], most[:, 128:]), axis=0, keepdims=True)
    edge_k = jnp.dot(sx[...], edge_x, precision=lax.Precision.HIGHEST, preferred_element_type=F32)
    wide_lane = ng * 2 * kz
    diag = (
        lax.rem(lax.broadcasted_iota(jnp.int32, (kz, wide_lane), 1), kz)
        == lax.broadcasted_iota(jnp.int32, (kz, wide_lane), 0)
    )
    zero = jnp.zeros((kz, wide_lane), F32)
    sums = [jnp.zeros((kz, ny), F32), jnp.zeros((kz, ny), F32)]
    first_row = [float(v) for v in sine(cx)[0]]
    group = 4
    for x0 in range(0, cx, group):
        lhs = jnp.concatenate(
            [jnp.where(diag, jnp.broadcast_to(edge_k[x : x + 1], (kz, wide_lane)), zero) for x in range(x0, x0 + group)],
            axis=0,
        )
        out = dot_right(lhs, edge[0], edge[1])
        for x in range(x0, x0 + group):
            hd = out[(x - x0) * kz : (x - x0 + 1) * kz] * inv[x]
            hfield[x] = hd
            sums[x % 2] = sums[x % 2] + first_row[x] * hd
    rows = (main[:kz] + (sums[0] + sums[1]), main[kz:] + (sums[0] - sums[1]))
    for row in range(2):
        for j in range(6):
            s2[pl.ds((j // 3) * 8 + row * 3 + j % 3, kz, stride=16), :] = rows[row][:, j * 128 : (j + 1) * 128]
    for r in (6, 7):
        s2[pl.ds(r, nf, stride=8), :] = jnp.broadcast_to(most, (nf, 128))

    tile = lambda ref: lambda d: ref.at[pl.ds(pl.multiple_of(d * 8, 8), 8), :]
    ex2 = ("fft", f, nf, tile(s2), tile(r2), s2s, r2s)
    send(*ex2)
    mine = pl.ds(pl.multiple_of(f * 8, 8), 8)
    r2[mine, :] = s2[mine, :]
    receive(*ex2)
    most = jnp.max(r2[pl.ds(6, nf, stride=8), :])
    step = COURANT * FINE_STEP / most

    last = jnp.zeros((8, 128), F32)
    prev = last
    for d in range(nf):
        msg = r2[8 * d : 8 * d + 8, :]
        other = pltpu.roll(msg, 5, 0)
        m0, m1 = mults[2 * d], mults[2 * d + 1]
        prev = m0 * (msg - cb * other) + (m0 * ca) * prev
        chain[2 * d] = prev
        prev = m1 * (other - cb * msg) + (m1 * cb) * prev
        chain[2 * d + 1] = prev
    chain[2 * nf - 1] = prev
    for j in range(2 * nf - 2, -1, -1):
        prev = chain[j] + (mults[j] * (cb if j % 2 == 0 else ca)) * prev
        chain[j] = prev
    for d in range(nf):
        left = chain[2 * d - 1] if d > 0 else last
        right = chain[2 * d + 2] if d < nf - 1 else last
        s3[8 * d : 8 * d + 8, :] = jnp.where(sub < 3, left, pltpu.roll(right, 3, 0))

    ex3 = ("fft", f, nf, tile(s3), tile(r3), s3s, r3s)
    send(*ex3)
    r3[mine, :] = s3[mine, :]
    loads["edget"].wait()
    loads["back"].wait()
    receive(*ex3)
    around = [
        jnp.concatenate(
            [r3[pl.ds((j // 3) * 8 + row * 3 + j % 3, kz, stride=16), :] for j in range(6)], axis=1
        )
        for row in range(2)
    ]
    out_rows = dot_right(jnp.concatenate(around, axis=0), back[0], back[1])
    mixed = (around[0] + around[1], around[0] - around[1])
    corr = []
    for x0 in range(0, cx, group):
        lhs = jnp.concatenate(
            [hfield[x] + (first_row[x] * inv[x]) * mixed[x % 2] for x in range(x0, x0 + group)], axis=0
        )
        out = dot_right(lhs, edget[0], edget[1])
        for x in range(group):
            corr.append(jnp.sum(jnp.where(diag, out[x * kz : (x + 1) * kz], zero), axis=0, keepdims=True))
    corr = jnp.concatenate(corr, axis=0)
    corr = jnp.dot(sx[...], corr, precision=lax.Precision.HIGHEST, preferred_element_type=F32)
    blank = jnp.zeros((cx, kz), F32)
    from_left = jnp.concatenate([blank, edge_x[:, :-kz]], axis=1)
    from_right = jnp.concatenate([edge_x[:, kz:], blank], axis=1)
    second = lax.rem(lax.broadcasted_iota(jnp.int32, (cx, wide_lane), 1) // kz, 2) == 1
    sides = corr + jnp.where(second, from_right, from_left)
    sides = jnp.concatenate(
        [jnp.zeros((cy, wide_lane), F32), sides, jnp.zeros((128 - cy - cx, wide_lane), F32)], axis=0
    ).T
    for d in range(ng):
        s4[d] = (out_rows[:, 128 * d : 128 * d + 128] + sides[2 * kz * d : 2 * kz * (d + 1)]).reshape(2, kz, 128)

    ex4 = ("grp", g, ng, lambda d: s4.at[d], lambda d: r4.at[:, d], s4s, r4s)
    send(*ex4)
    r4[:, g] = s4[g]
    receive(*ex4)
    for e in range(2):
        solved[e] = r4[e].reshape(nz, 128).T

    def second_solve(i, _):
        def fetch(x, at):
            va = solved[0, pl.ds(cy + x, 1), :]
            vb = solved[1, pl.ds(cy + x, 1), :]
            w = jnp.where(even, va + vb, va - vb)
            value = block[x, at, :] - column[at, :] * jnp.concatenate([w, w], axis=0)
            if x == 0:
                value = value - solved[0, at, :]
            if x == cx - 1:
                value = value - solved[1, at, :]
            return value

        at, values = solve(fetch, i)
        for x in range(cx):
            block[x, at, :] = values[x]
        return 0

    lax.fori_loop(0, cy // 16, second_solve, 0)

    def inverse_z(rows):
        a, b = split(rows)
        both = mm(jnp.concatenate([a, b], axis=1), sz[...])
        return both[:, :nz] + both[:, nz:]

    def backward(i, _):
        pair_x = jnp.concatenate([block[2 * i], block[2 * i + 1]], axis=1)
        out = dot_left(sy[0], sy[1], pair_x)
        out = inverse_z(jnp.concatenate([out[:, :nz], out[:, nz:]], axis=0))
        grid[2 * i + 1, pl.ds(8, cy), :] = out[:cy]
        grid[2 * i + 2, pl.ds(8, cy), :] = out[cy:]
        return 0

    lax.fori_loop(0, half, backward, 0)
    copy_out = pltpu.make_async_copy(grid.at[pl.ds(1, cx), pl.ds(8, cy), :], pot_h, osem)
    copy_out.start()
    pair_x = jnp.concatenate([solved[0, :cy], solved[1, :cy]], axis=1)
    out = dot_left(sy[0], sy[1], pair_x)
    rest = jnp.concatenate([out[:, :nz], out[:, nz:], solved[0, cy:], solved[1, cy:]], axis=0)
    rest = inverse_z(rest)
    grid[0, pl.ds(8, cy), :] = rest[:cy]
    grid[cx + 1, pl.ds(8, cy), :] = rest[cy : 2 * cy]
    pad = 128 - cy
    for e in range(2):
        lines = rest[2 * cy + pad * e : 2 * cy + pad * (e + 1)]
        at = pl.ds(7 if e == 0 else 8 + cy, 1)
        for x in range(cx):
            grid[x + 1, at, :] = lines[x : x + 1]
    for e in range(2):
        lines = rest[2 * cy + pad * e : 2 * cy + pad * (e + 1)]
        for s in range(2):
            grid[(cx + 1) * e, pl.ds(7 if s == 0 else 8 + cy, 1), :] = lines[cx + s : cx + s + 1]

    loads["fold"].wait()
    loads["weave"].wait()
    per_y, per_z = cy // 4, nz // 4
    lanes8 = lax.broadcasted_iota(jnp.int32, (8, 128), 1)
    pick = (
        lax.broadcasted_iota(jnp.int32, (16, 128), 1) // 8 == lax.broadcasted_iota(jnp.int32, (16, 128), 0)
    )
    lane6 = lax.rem(lax.broadcasted_iota(jnp.int32, (6, 128), 1), 8)
    row6 = lax.broadcasted_iota(jnp.int32, (6, 128), 0)
    some = 4

    def gather(i, _):
        cut, odd = [], []
        for c in range(2 * some):
            code = jnp.maximum(ghost[0, 2 * some * i + c], 0)
            ix = code // (per_y * per_z)
            iy = lax.rem(code // per_z, per_y)
            iz = lax.rem(code, per_z)
            rows = grid[pl.ds(4 * ix, 6), pl.ds(7 + 4 * iy, 8), :]
            inside = (lanes8 >= 4 * iz - 1) & (lanes8 <= 4 * iz + 4) & (sub < 6)
            cut.append(jnp.where(inside[None], rows, 0.0).reshape(48, 128))
            odd.append(lax.rem(iz, 2))
        a, b = split(jnp.concatenate(cut, axis=0))
        out = mm(jnp.concatenate([a, b], axis=1), fold[...]).reshape(2 * some * 3, 16, 128)
        out = jnp.sum(jnp.where(pick[None], out, 0.0), axis=1)
        for k in range(some):
            d = some * i + k
            mini = out[6 * k : 6 * k + 6]
            turned = jnp.where(lane6 < 4, pltpu.roll(mini, 124, 1), pltpu.roll(mini, 4, 1))
            which = jnp.where(row6 < 3, odd[2 * k], odd[2 * k + 1])
            mini = jnp.where(which == 1, turned, mini)
            slots = [
                jnp.full((1, 128), ghost[1, 2 * d + c].astype(F32), F32) for c in range(2)
            ]
            s6[pl.ds(pl.multiple_of(8 * d, 8), 8), :] = jnp.concatenate([mini] + slots, axis=0)
        return 0

    lax.fori_loop(0, nf // some, gather, 0)

    ex6 = ("fft", f, nf, tile(s6), tile(r6), s6s, r6s)
    send(*ex6)
    r6[mine, :] = s6[mine, :]
    receive(*ex6)
    lanes = lax.broadcasted_iota(jnp.int32, (nf, 128), 1)
    hot = jnp.concatenate(
        [
            jnp.where(r6[pl.ds(6 + c, nf, stride=8), :] == lanes.astype(F32), 1.0, 0.0)
            for c in range(2)
        ],
        axis=0,
    ).astype(BF16)
    within, outside = [], []
    for t in range(3):
        came = jnp.concatenate([r6[pl.ds(c * 3 + t, nf, stride=8), :] for c in range(2)], axis=0)
        a, b = split(came.T)
        placed = mm(a, hot) + mm(b, hot)
        a, b = split(placed)
        woven = mm(weave[...], a) + mm(weave[...], b)
        woven = woven.reshape(2, 2, 8, 8, 128)[..., : fine.shape[-1]]
        within += [woven[0, 0], woven[0, 1]]
        outside += [woven[1, 0], woven[1, 1]]

    def between(values, j):
        low = j // 2
        return (
            0.75 * values[low] + 0.25 * values[low + 1]
            if j % 2 == 0
            else 0.25 * values[low] + 0.75 * values[low + 1]
        )

    scale = 1.0 / (6.0 + SCREEN * FINE_STEP * FINE_STEP)
    for jx in range(10):
        plane = between(within, jx)
        for jy in range(10):
            field[jx, jy] = between(plane, jy)
        if 1 <= jx <= 8:
            plane = between(outside, jx)
            for jy in range(1, 9):
                layer = between(plane, jy)
                ghosts[jx - 1, jy - 1] = layer
                force[jx - 1, jy - 1] = (OMEGA * scale) * (
                    layer - FINE_STEP * FINE_STEP * fluid[0, jx - 1, jy - 1]
                )

    width = fine.shape[-1]
    z = lax.broadcasted_iota(jnp.int32, (8, width), 0)
    bottom, top, zeven = z == 0, z == 7, lax.rem(z, 2) == 0
    zodd = jnp.logical_not(zeven)

    def sweep(_, carry):
        for colour in (0, 1):
            def planes(i, c, colour=colour):
                for k in range(2):
                    x = 2 * i + k + 1
                    for y in range(1, 9):
                        v = field[x, y]
                        near = (
                            (field[x - 1, y] + field[x + 1, y])
                            + (field[x, y - 1] + field[x, y + 1])
                            + (
                                jnp.where(bottom, 0.0, pltpu.roll(v, 1, 0))
                                + jnp.where(top, 0.0, pltpu.roll(v, 7, 0))
                            )
                        )
                        new = (1.0 - OMEGA) * v + ((OMEGA * scale) * near + force[x - 1, y - 1])
                        mask = zeven if (k + y - 1 + colour) % 2 == 0 else zodd
                        field[x, y] = jnp.where(mask, new, v)
                return c
            lax.fori_loop(0, 4, planes, 0)
        return carry

    lax.fori_loop(0, SWEEPS, sweep, 0)

    def update(x, _):
        for y in range(8):
            v = field[x + 1, y + 1]
            layer = ghosts[x, y]
            fine[x, y] = v
            pull = (
                field[x, y + 1] - field[x + 2, y + 1],
                field[x + 1, y] - field[x + 1, y + 2],
                jnp.where(bottom, layer, pltpu.roll(v, 1, 0)) - jnp.where(top, layer, pltpu.roll(v, 7, 0)),
            )
            dens = fluid[0, x, y]
            rate = step / FINE_STEP
            work = 0.0
            moved[0, x, y] = dens - rate * change[0, x, y]
            for n in range(3):
                mom = fluid[1 + n, x, y]
                moved[1 + n, x, y] = mom - rate * change[1 + n, x, y] + step * dens * pull[n]
                work = work + mom * pull[n]
            moved[4, x, y] = fluid[4, x, y] - rate * change[4, x, y] + step * work
        return 0

    lax.fori_loop(0, 8, update, 0)
    copy_out.wait()


def root_call(ghost, rho, speed, fluid, change, nf, ng):
    cx, cy, nz = rho.shape
    kz = nz // ng
    ny = ng * cy
    count = fluid.shape[-1]
    tab = tables(nf, ng, cx, cy, nz)
    consts = [jnp.asarray(tab[n]) for n in NAMES]
    vm = lambda shape, dtype=F32: pltpu.VMEM(shape, dtype)
    anyspace = pl.BlockSpec(memory_space=pl.ANY)
    vspace = pl.BlockSpec(memory_space=pltpu.VMEM)
    dma = pltpu.SemaphoreType.DMA
    local = {n: tab[n].shape for n in NAMES}
    local["inv"] = local["inv"][1:]
    local["pair"] = local["pair"][2:]
    return pl.pallas_call(
        functools.partial(root_kernel, (nf, ng, cx, cy, nz)),
        out_shape=(
            jax.ShapeDtypeStruct((cx, cy, nz), F32),
            jax.ShapeDtypeStruct((8, 8, 8, count), F32),
            jax.ShapeDtypeStruct((5, 8, 8, 8, count), F32),
        ),
        in_specs=[pl.BlockSpec(memory_space=pltpu.SMEM), anyspace, vspace, vspace, vspace]
        + [anyspace] * len(NAMES),
        out_specs=(anyspace, vspace, vspace),
        scratch_shapes=[vm((cx, cy, nz))]
        + [vm(local[n], consts[i].dtype) for i, n in enumerate(NAMES)]
        + [
            vm((cx, cy, nz)),
            vm((2, 128, nz)),
            vm((cx, 8, nz)),
            vm((cx + 2, cy + 16, nz)),
            vm((cx, kz, ny)),
            vm((2, nz, 128)), vm((ng, 2, kz, 128)),
            vm((nf * 8, 128)), vm((nf * 8, 128)),
            vm((nf * 8, 128)), vm((nf * 8, 128)),
            vm((ng, 2, kz, 128)), vm((2, ng, kz, 128)),
            vm((nf * 8, 128)), vm((nf * 8, 128)),
            vm((2 * nf, 8, 128)), vm((2 * nf, 8, 128)),
            vm((10, 10, 8, count)), vm((8, 8, 8, count)), vm((8, 8, 8, count)),
            dma((14,)), dma,
            dma((ng,)), dma((ng,)),
            dma((nf,)), dma((nf,)),
            dma((nf,)), dma((nf,)),
            dma((ng,)), dma((ng,)),
            dma((nf,)), dma((nf,)),
        ],
        compiler_params=pltpu.CompilerParams(
            collective_id=0, has_side_effects=True, vmem_limit_bytes=56 * 1024 * 1024
        ),
    )(ghost, rho, speed, fluid, change, *consts)


def primitives(fluid):
    dens = fluid[0]
    vel = fluid[1:4] / dens
    kinetic = 0.5 * jnp.sum(fluid[1:4] * vel, axis=0)
    pres = (GAMMA - 1.0) * (fluid[4] - kinetic)
    return (dens, vel, pres)


def signal_speed(fluid):
    dens, vel, pres = primitives(fluid[:, 2:10, 2:10, 2:10])
    sound = jnp.sqrt(GAMMA * pres / dens)
    return jnp.max(jnp.max(jnp.abs(vel), axis=0) + sound)


def along(array, axis, start, stop):
    return lax.slice_in_dim(array, start, stop, axis=axis + 1)


def conserved_flux(state, axis):
    dens = state[0]
    vel = state[1:4]
    pres = state[4]
    normal = vel[axis]
    energy = pres / (GAMMA - 1.0) + 0.5 * dens * jnp.sum(vel * vel, axis=0)
    cons = jnp.stack([dens, dens * vel[0], dens * vel[1], dens * vel[2], energy])
    moment = [dens * normal * vel[other] + (pres if other == axis else 0.0) for other in range(3)]
    flux = jnp.stack([dens * normal, moment[0], moment[1], moment[2], (energy + pres) * normal])
    speed = jnp.abs(normal) + jnp.sqrt(GAMMA * pres / dens)
    return (cons, flux, speed)


def flux_difference(prim, axis):
    for other in range(3):
        if other != axis:
            prim = along(prim, other, 2, 10)
    left_diff = along(prim, axis, 1, 11) - along(prim, axis, 0, 10)
    right_diff = along(prim, axis, 2, 12) - along(prim, axis, 1, 11)
    slope = (
        0.5
        * (jnp.sign(left_diff) + jnp.sign(right_diff))
        * jnp.minimum(jnp.abs(left_diff), jnp.abs(right_diff))
    )
    centre = along(prim, axis, 1, 11)
    upper = centre + 0.5 * slope
    lower = centre - 0.5 * slope
    cons_left, flux_left, speed_left = conserved_flux(along(upper, axis, 0, 9), axis)
    cons_right, flux_right, speed_right = conserved_flux(along(lower, axis, 1, 10), axis)
    flux = 0.5 * (flux_left + flux_right) - 0.5 * jnp.maximum(speed_left, speed_right) * (
        cons_right - cons_left
    )
    return along(flux, axis, 1, 9) - along(flux, axis, 0, 8)


def per_device(root_density, patch_fluid, ghost_list):
    nf = lax.axis_size("fft")
    ng = lax.axis_size("grp")
    speed = jnp.broadcast_to(signal_speed(patch_fluid), (8, 128))
    dens, vel, pres = primitives(patch_fluid)
    prim = jnp.concatenate([dens[None], vel, pres[None]], axis=0)
    change = flux_difference(prim, 0) + flux_difference(prim, 1) + flux_difference(prim, 2)
    inner = patch_fluid[:, 2:10, 2:10, 2:10]
    return root_call(ghost_list[:, 0], root_density, speed, inner, change, nf, ng)


def solution(mesh):
    return jax.shard_map(
        per_device,
        mesh=mesh,
        in_specs=(
            P("fft", "grp", None),
            P(None, None, None, None, ("fft", "grp")),
            P(None, ("fft", "grp"), None),
        ),
        out_specs=(
            P("fft", "grp", None),
            P(None, None, None, ("fft", "grp")),
            P(None, None, None, None, ("fft", "grp")),
        ),
        check_vma=False,
    )
```

```python
import functools

import jax
import jax.numpy as jnp
import ml_dtypes
import numpy as np
from jax import lax
from jax.experimental import pallas as pl
from jax.experimental.pallas import tpu as pltpu
from jax.sharding import PartitionSpec as P

SWEEPS = 8
GAMMA = 5.0 / 3.0
SCREEN = 0.0006
OMEGA = 1.5
COURANT = 0.4
FINE_STEP = 0.5
F32 = jnp.float32
BF16 = jnp.bfloat16


def sine(count):
    index = np.arange(1, count + 1)
    return np.sqrt(2.0 / (count + 1)) * np.sin(
        np.pi * (np.outer(index, index) % (2 * (count + 1))) / (count + 1)
    )


def eigen(count):
    return 4.0 * np.sin(np.pi * np.arange(1, count + 1) / (2 * (count + 1))) ** 2


def halves(table):
    high = table.astype(ml_dtypes.bfloat16)
    low = (table - high.astype(np.float64)).astype(ml_dtypes.bfloat16)
    return np.stack([high, low])


@functools.lru_cache(None)
def tables(nf, ng, cx, cy, nz):
    ny = ng * cy
    kz = nz // ng
    sz, sy, sx, full = sine(nz), sine(cy), sine(cx), sine(ny)
    lam = eigen(cy)[:, None] + eigen(nz)[None, :] + SCREEN
    steps = [1.0 / (2.0 + lam)]
    for _ in range(1, cx // 2):
        steps.append(1.0 / (2.0 + lam - steps[-1]))
    steps.append(1.0 / (1.0 - steps[-1] ** 2))
    edge = np.zeros((ng, 2, ny))
    wide = np.zeros((ng, 128, ny))
    back = np.zeros((ng, 128, ny))
    for d in range(ng):
        if d > 0:
            edge[d, 0] = full[d * cy - 1]
        if d < ng - 1:
            edge[d, 1] = full[(d + 1) * cy]
        wide[d, :cy] = sy @ full[d * cy : (d + 1) * cy]
        back[d, :cy] = wide[d, :cy]
        back[d, cy + cx] = edge[d, 0]
        back[d, cy + cx + 1] = edge[d, 1]
    repeated = np.repeat(edge.reshape(2 * ng, ny), kz, axis=0)
    denom = (
        eigen(cx)[None, :, None, None]
        + eigen(nz).reshape(ng, 1, kz, 1)
        + eigen(ny)[None, None, None, :]
        + SCREEN
    )
    phi = 2.0 * np.arcsinh(np.sqrt(eigen(ny)[None, :] + eigen(nz)[:, None] + SCREEN) / 2.0)

    def ratio(m, n):
        return np.exp(-(n - m) * phi) * np.expm1(-2 * m * phi) / np.expm1(-2 * n * phi)

    pair = np.zeros((ng, nf, 2, 8, 128))
    for i, values in enumerate((ratio(cx - 1, cx), ratio(1, cx))):
        pair[:, :, i, :3] = values.reshape(ng, nf, 3, 128)
    spread = np.zeros((10, 6))
    for j in range(10):
        at = j / 2 + 0.25
        low = int(np.floor(at))
        spread[j, low] += 1 - (at - low)
        spread[j, low + 1] += at - low
    inner = np.zeros((8, 8))
    inner[:, :6] = spread[1:9]
    outer = np.zeros((8, 8))
    outer[0, :6] = spread[0]
    outer[7, :6] = spread[9]
    weave = np.concatenate([np.kron(np.eye(16), inner), np.kron(np.eye(16), outer)])
    lanes = np.arange(128)
    fold = ((lanes[:, None] + 1) % 8 == lanes[None, :] % 8).astype(np.float64)
    column = np.broadcast_to(sy[0][:, None], (cy, 128))
    as32 = lambda t: np.ascontiguousarray(t, dtype=np.float32)
    szh, szl = halves(sz)
    return dict(
        sz=np.block([[szh, szl], [szh, np.zeros_like(szh)]]).astype(ml_dtypes.bfloat16),
        sy=halves(sy),
        sx=as32(sx),
        steps=as32(np.stack(steps)),
        wide=halves(wide.reshape(ng * 128, ny)),
        back=halves(np.ascontiguousarray(back.reshape(ng * 128, ny).T)),
        edge=halves(repeated),
        edget=halves(np.ascontiguousarray(repeated.T)),
        inv=as32(1.0 / denom),
        pair=as32(pair),
        weave=weave.astype(ml_dtypes.bfloat16),
        fold=np.concatenate([fold, fold]).astype(ml_dtypes.bfloat16),
        column=as32(column),
    )


NAMES = (
    "sz", "sy", "sx", "steps", "wide", "back", "edge", "edget", "inv", "pair", "fold", "column",
)


def split(value):
    high = value.astype(BF16)
    return high, (value - high.astype(F32)).astype(BF16)


def mm(a, b):
    return jnp.dot(a, b, preferred_element_type=F32)


def dot_right(value, high, low):
    a, b = split(value)
    return mm(a, high) + (mm(b, high) + mm(a, low))


def dot_left(high, low, value):
    a, b = split(value)
    return mm(high, a) + (mm(high, b) + mm(low, a))


def root_kernel(
    cfg,
    ghost, rho, fluid_h,
    sz_h, sy_h, sx_h, steps_h, wide_h, back_h, edge_h, edget_h, inv_h, pair_h, fold_h, column_h,
    pot_h, blocks, most_out, change,
    src, sz, sy, sx, steps, wide, back, edge, edget, inv, pair, fold, column, fluid, prim,
    block, solved, part, grid, hfield,
    s1, r1, s2, r2, s3, r3, s4, r4, s6, r6, chain, mults, last_face,
    tsem, osem, s1s, r1s, s2s, r2s, s3s, r3s, s4s, r4s, s6s, r6s,
):
    nf, ng, cx, cy, nz = cfg
    kz = nz // ng
    ny = ng * cy
    half = cx // 2
    f = lax.axis_index("fft")
    g = lax.axis_index("grp")

    ny_chips = 4 if nf % 4 == 0 else 1
    nz_chips = nf // ny_chips
    barrier = pltpu.get_barrier_semaphore()

    def hello(axis, pos, count):
        def body(k, _):
            pl.semaphore_signal(
                barrier, inc=1, device_id={axis: lax.rem(pos + k, count)},
                device_id_type=pl.DeviceIdType.MESH,
            )
            return 0
        lax.fori_loop(1, count, body, 0)

    hello("grp", g, ng)
    hello("fft", f, nf)

    loads = {}
    order = [
        ("rho", rho, src), ("sz", sz_h, sz), ("sy", sy_h, sy), ("steps", steps_h, steps),
        ("column", column_h, column), ("pair", pair_h.at[g, f], pair), ("wide", wide_h, wide),
        ("sx", sx_h, sx), ("edge", edge_h, edge), ("inv", inv_h.at[g], inv),
        ("fluid", fluid_h, fluid), ("edget", edget_h, edget), ("back", back_h, back), ("fold", fold_h, fold),
    ]
    for i, (name, a, b) in enumerate(order):
        loads[name] = pltpu.make_async_copy(a, b, tsem.at[i])
        loads[name].start()

    sub = lax.broadcasted_iota(jnp.int32, (8, 128), 0)
    even = lax.rem(sub, 2) == 0

    loads["rho"].wait()
    loads["sz"].wait()
    loads["sy"].wait()

    def forward(i, _):
        rows = src[pl.ds(2 * i, 2)].reshape(2 * cy, nz)
        a, b = split(rows)
        both = mm(jnp.concatenate([a, b], axis=1), sz[...])
        both = both[:, :nz] + both[:, nz:]
        pair_x = jnp.concatenate([both[:cy], both[cy:]], axis=1)
        out = dot_left(sy[0], sy[1], pair_x)
        block[2 * i] = out[:, :nz]
        block[2 * i + 1] = out[:, nz:]
        return 0

    lax.fori_loop(0, half, forward, 0)

    loads["steps"].wait()
    loads["column"].wait()

    def solve(fetch, i):
        at = pl.ds(pl.multiple_of(16 * i, 16), 16)
        low, high = [], []
        for j in range(half):
            m = steps[j, at, :]
            a, b = fetch(j, at), fetch(cx - 1 - j, at)
            if j == 0:
                low.append(-m * a)
                high.append(-m * b)
            else:
                low.append(m * (low[-1] - a))
                high.append(m * (high[-1] - b))
        m, scale = steps[half - 1, at, :], steps[half, at, :]
        a, b = low[-1], high[-1]
        low[-1] = (a + m * b) * scale
        high[-1] = (b + m * a) * scale
        for j in range(half - 2, -1, -1):
            m = steps[j, at, :]
            low[j] = low[j] + m * low[j + 1]
            high[j] = high[j] + m * high[j + 1]
        return at, low + high[::-1]

    part[...] = jnp.zeros_like(part)

    def first(i, _):
        at, values = solve(lambda x, at: block[x, at, :], i)
        col = column[at, :]
        for x in range(cx):
            v = values[x] * col
            part[x] += v[:8] + v[8:]
        solved[0, at, :] = values[0]
        solved[1, at, :] = values[cx - 1]
        return 0

    lax.fori_loop(0, cy // 16, first, 0)
    sums = part[...]
    sign = jnp.where(even, 1.0, -1.0)
    edges = (jnp.sum(sums, axis=1), jnp.sum(sums * sign[None], axis=1))
    for e in range(2):
        solved[e, pl.ds(cy, cx), :] = edges[e]
        solved[e, pl.ds(cy + cx, 8), :] = jnp.zeros((8, 128), F32)
        s1[e] = solved[e].T


    cells = pl.ds(2, 8)

    def cell_values(cons):
        dens = cons[0]
        over = 1.0 / dens
        vel = [m * over for m in cons[1:4]]
        kinetic = 0.5 * (cons[1] * vel[0] + cons[2] * vel[1] + cons[3] * vel[2])
        return [dens] + vel + [(GAMMA - 1.0) * (cons[4] - kinetic)]

    def sound(dens, pres):
        return jnp.sqrt(GAMMA * pres) * lax.rsqrt(dens)

    def make_cells(x, _):
        for y in range(12):
            w = cell_values([fluid[v, x, y, cells, :] for v in range(5)])
            for v in range(5):
                prim[v, x, y] = w[v]
        return 0

    def top_speed():
        def body(x, top):
            for y in range(2, 10):
                w = [prim[v, x + 2, y] for v in range(5)]
                fast = jnp.maximum(jnp.maximum(jnp.abs(w[1]), jnp.abs(w[2])), jnp.abs(w[3]))
                top = jnp.maximum(top, fast + sound(w[0], w[4]))
            return top
        return jnp.max(lax.fori_loop(0, 8, body, jnp.zeros((8, fluid.shape[-1]), F32)))

    def states(before, here, after):
        low, high = [], []
        for a, b, c in zip(before, here, after):
            p, q = b - a, c - b
            half_slope = 0.5 * (
                jnp.maximum(0.0, jnp.minimum(p, q)) + jnp.minimum(0.0, jnp.maximum(p, q))
            )
            low.append(b - half_slope)
            high.append(b + half_slope)
        return low, high

    def side(w, n):
        dens, vel, pres = w[0], w[1:4], w[4]
        energy = pres * (1.0 / (GAMMA - 1.0)) + 0.5 * dens * (
            vel[0] * vel[0] + vel[1] * vel[1] + vel[2] * vel[2]
        )
        mom = [dens * v for v in vel]
        flux = [mom[n]] + [mom[n] * v for v in vel] + [(energy + pres) * vel[n]]
        flux[1 + n] = flux[1 + n] + pres
        return [dens] + mom + [energy], flux, jnp.abs(vel[n]) + sound(dens, pres)

    def face(left, right, n):
        cl, fl, al = side(left, n)
        cr, fr, ar = side(right, n)
        top = jnp.maximum(al, ar)
        return [0.5 * ((a + b) - top * (d - c)) for a, b, c, d in zip(fl, fr, cl, cr)]

    def sweep_line(get, put, n):
        w = [get(0), get(1), get(2)]
        _, high = states(*w)
        flux = None
        for i in range(2, 11):
            w = [w[1], w[2], get(i + 1)]
            low, high_next = states(*w)
            now = face(high, low, n)
            if flux is not None:
                put(i - 3, [b - a for a, b in zip(flux, now)])
            flux, high = now, high_next

    def lines_x(y, _):
        def get(i):
            return [prim[v, i, y + 2] for v in range(5)]

        def put(i, values):
            for v in range(5):
                change[v, i, y] = values[v]

        sweep_line(get, put, 0)
        return 0

    def lines_y(x, _):
        def get(i):
            return [prim[v, x + 2, i] for v in range(5)]

        def put(i, values):
            for v in range(5):
                change[v, x, i] += values[v]

        sweep_line(get, put, 1)
        return 0

    def last_faces(x, _):
        w = [
            cell_values([fluid[v, x + 2, cells, k, :] for v in range(5)]) for k in (8, 9, 10, 11)
        ]
        _, high = states(w[0], w[1], w[2])
        low, _ = states(w[1], w[2], w[3])
        flux = face(high, low, 2)
        for v in range(5):
            last_face[v, x] = flux[v]
        return 0

    def lines_z(x, _):
        row = lax.broadcasted_iota(jnp.int32, (8, fluid.shape[-1]), 0)
        for y in range(8):
            w = [
                cell_values([fluid[v, x + 2, y + 2, pl.ds(k, 8), :] for v in range(5)]) if k != 2
                else [prim[v, x + 2, y + 2] for v in range(5)]
                for k in range(4)
            ]
            _, high = states(w[0], w[1], w[2])
            low, _ = states(w[1], w[2], w[3])
            flux = face(high, low, 2)
            for v in range(5):
                after = jnp.where(row == 7, last_face[v, x, pl.ds(y, 1), :], pltpu.roll(flux[v], 7, 0))
                change[v, x, y] += after - flux[v]
        return 0

    pl.semaphore_wait(barrier, ng + nf - 2)

    def grp_partner(i, way):
        return lax.rem(g + way * i + ng, ng), i

    def fft_partner(i, way):
        a, b = i // ny_chips, lax.rem(i, ny_chips)
        dz = nz_chips // 2 + ((a + 1) // 2) * (1 - 2 * lax.rem(a, 2))
        dy = ny_chips // 2 + ((b + 1) // 2) * (1 - 2 * lax.rem(b, 2))
        z = lax.rem(f // ny_chips + way * dz + nz_chips, nz_chips)
        y = lax.rem(lax.rem(f, ny_chips) + way * dy + ny_chips, ny_chips)
        return z * ny_chips + y, i

    ways = {"grp": (1, ng, grp_partner, g), "fft": (0, nf - 1, fft_partner, f)}

    def send(axis, source, target, sends, recvs):
        begin, end, partner, pos = ways[axis]

        def body(k, _):
            to, at = partner(k, 1)
            pltpu.make_async_remote_copy(
                source(to), target(pos), sends.at[at], recvs.at[at], device_id={axis: to},
                device_id_type=pl.DeviceIdType.MESH,
            ).start()
            return 0

        lax.fori_loop(begin, end, body, 0)

    def receive(axis, source, target, sends, recvs):
        begin, end, partner, pos = ways[axis]

        def body(k, _):
            come, at = partner(k, -1)
            pltpu.make_async_remote_copy(
                source(come), target(come), sends.at[at], recvs.at[at], device_id={axis: come},
                device_id_type=pl.DeviceIdType.MESH,
            ).wait_recv()
            return 0

        lax.fori_loop(begin, end, body, 0)

    def sent(axis, source, target, sends, recvs):
        begin, end, partner, pos = ways[axis]

        def body(k, _):
            to, at = partner(k, 1)
            pltpu.make_async_remote_copy(
                source(to), target(pos), sends.at[at], recvs.at[at], device_id={axis: to},
                device_id_type=pl.DeviceIdType.MESH,
            ).wait_send()
            return 0

        lax.fori_loop(begin, end, body, 0)

    slice1 = lambda d: s1.at[:, pl.ds(pl.multiple_of(d * kz, kz), kz), :]
    ex1 = ("grp", slice1, lambda d: r1.at[d], s1s, r1s)
    send(*ex1)
    r1[g] = s1[:, pl.ds(pl.multiple_of(g * kz, kz), kz), :]

    loads["pair"].wait()
    ca, cb = pair[0], pair[1]
    ca2, cb2 = ca * ca, cb * cb

    def coefficients(i, m):
        m0 = 1.0 / (1.0 - ca2 * m)
        mults[2 * i] = m0
        m1 = 1.0 / (1.0 - cb2 * m0)
        mults[2 * i + 1] = m1
        return m1

    lax.fori_loop(0, nf, coefficients, jnp.zeros((8, 128), F32))
    loads["fluid"].wait()
    lax.fori_loop(0, 12, make_cells, 0)
    most = jnp.full((1, 128), top_speed(), F32)
    loads["wide"].wait()
    loads["sx"].wait()
    loads["edge"].wait()
    loads["inv"].wait()
    receive(*ex1)

    main = jnp.concatenate([r1[d].reshape(2 * kz, 128) for d in range(ng)], axis=1)
    main = dot_right(main, wide[0], wide[1])
    across = r1[...].reshape(ng * 2 * kz, 128).T
    edge_x = across[cy : cy + cx]
    edge_k = jnp.dot(sx[...], edge_x, precision=lax.Precision.HIGHEST, preferred_element_type=F32)
    wide_lane = ng * 2 * kz
    diag = (
        lax.rem(lax.broadcasted_iota(jnp.int32, (kz, wide_lane), 1), kz)
        == lax.broadcasted_iota(jnp.int32, (kz, wide_lane), 0)
    )
    zero = jnp.zeros((kz, wide_lane), F32)
    sums = [jnp.zeros((kz, ny), F32), jnp.zeros((kz, ny), F32)]
    first_row = [float(v) for v in sine(cx)[0]]
    group = 4
    for x0 in range(0, cx, group):
        lhs = jnp.concatenate(
            [jnp.where(diag, jnp.broadcast_to(edge_k[x : x + 1], (kz, wide_lane)), zero) for x in range(x0, x0 + group)],
            axis=0,
        )
        out = dot_right(lhs, edge[0], edge[1])
        for x in range(x0, x0 + group):
            hd = out[(x - x0) * kz : (x - x0 + 1) * kz] * inv[x]
            hfield[x] = hd
            sums[x % 2] = sums[x % 2] + first_row[x] * hd
    rows = (main[:kz] + (sums[0] + sums[1]), main[kz:] + (sums[0] - sums[1]))
    for row in range(2):
        for j in range(6):
            s2[pl.ds((j // 3) * 8 + row * 3 + j % 3, kz, stride=16), :] = rows[row][:, j * 128 : (j + 1) * 128]
    for r in (6, 7):
        s2[pl.ds(r, nf, stride=8), :] = jnp.broadcast_to(most, (nf, 128))

    tile = lambda ref: lambda d: ref.at[pl.ds(pl.multiple_of(d * 8, 8), 8), :]
    ex2 = ("fft", tile(s2), tile(r2), s2s, r2s)
    send(*ex2)
    mine = pl.ds(pl.multiple_of(f * 8, 8), 8)
    r2[mine, :] = s2[mine, :]
    lax.fori_loop(0, 8, lines_x, 0)
    lax.fori_loop(0, 8, lines_y, 0)
    receive(*ex2)
    most = jnp.max(r2[pl.ds(6, nf, stride=8), :], axis=0, keepdims=True)

    last = jnp.zeros((8, 128), F32)
    prev = last
    for d in range(nf):
        msg = r2[8 * d : 8 * d + 8, :]
        other = pltpu.roll(msg, 5, 0)
        m0, m1 = mults[2 * d], mults[2 * d + 1]
        prev = m0 * (msg - cb * other) + (m0 * ca) * prev
        chain[2 * d] = prev
        prev = m1 * (other - cb * msg) + (m1 * cb) * prev
        chain[2 * d + 1] = prev
    chain[2 * nf - 1] = prev
    for j in range(2 * nf - 2, -1, -1):
        prev = chain[j] + (mults[j] * (cb if j % 2 == 0 else ca)) * prev
        chain[j] = prev
    for d in range(nf):
        left = chain[2 * d - 1] if d > 0 else last
        right = chain[2 * d + 2] if d < nf - 1 else last
        s3[8 * d : 8 * d + 8, :] = jnp.where(sub < 3, left, pltpu.roll(right, 3, 0))

    ex3 = ("fft", tile(s3), tile(r3), s3s, r3s)
    send(*ex3)
    r3[mine, :] = s3[mine, :]
    loads["edget"].wait()
    loads["back"].wait()
    lax.fori_loop(0, 8, last_faces, 0)
    lax.fori_loop(0, 8, lines_z, 0)
    receive(*ex3)
    around = [
        jnp.concatenate(
            [r3[pl.ds((j // 3) * 8 + row * 3 + j % 3, kz, stride=16), :] for j in range(6)], axis=1
        )
        for row in range(2)
    ]
    out_rows = dot_right(jnp.concatenate(around, axis=0), back[0], back[1])
    mixed = (around[0] + around[1], around[0] - around[1])
    corr = []
    for x0 in range(0, cx, group):
        lhs = jnp.concatenate(
            [hfield[x] + (first_row[x] * inv[x]) * mixed[x % 2] for x in range(x0, x0 + group)], axis=0
        )
        out = dot_right(lhs, edget[0], edget[1])
        for x in range(group):
            corr.append(jnp.sum(jnp.where(diag, out[x * kz : (x + 1) * kz], zero), axis=0, keepdims=True))
    corr = jnp.concatenate(corr, axis=0)
    corr = jnp.dot(sx[...], corr, precision=lax.Precision.HIGHEST, preferred_element_type=F32)
    blank = jnp.zeros((cx, kz), F32)
    from_left = jnp.concatenate([blank, edge_x[:, :-kz]], axis=1)
    from_right = jnp.concatenate([edge_x[:, kz:], blank], axis=1)
    second = lax.rem(lax.broadcasted_iota(jnp.int32, (cx, wide_lane), 1) // kz, 2) == 1
    sides = corr + jnp.where(second, from_right, from_left)
    sides = jnp.concatenate(
        [jnp.zeros((cy, wide_lane), F32), sides, jnp.zeros((128 - cy - cx, wide_lane), F32)], axis=0
    ).T
    sides = jnp.where(
        lax.broadcasted_iota(jnp.int32, (wide_lane, 128), 1) == 127, jnp.broadcast_to(most, (wide_lane, 128)), sides
    )
    for d in range(ng):
        s4[d] = (out_rows[:, 128 * d : 128 * d + 128] + sides[2 * kz * d : 2 * kz * (d + 1)]).reshape(2, kz, 128)

    ex4 = ("grp", lambda d: s4.at[d], lambda d: r4.at[:, d], s4s, r4s)
    send(*ex4)
    r4[:, g] = s4[g]
    sent(*ex1)
    sent(*ex2)
    sent(*ex3)
    receive(*ex4)
    for e in range(2):
        solved[e] = r4[e].reshape(nz, 128).T
    most_out[...] = jnp.full((8, 128), jnp.max(solved[0, pl.ds(127, 1), :]), F32)

    def second_solve(i, _):
        def fetch(x, at):
            va = solved[0, pl.ds(cy + x, 1), :]
            vb = solved[1, pl.ds(cy + x, 1), :]
            w = jnp.where(even, va + vb, va - vb)
            value = block[x, at, :] - column[at, :] * jnp.concatenate([w, w], axis=0)
            if x == 0:
                value = value - solved[0, at, :]
            if x == cx - 1:
                value = value - solved[1, at, :]
            return value

        at, values = solve(fetch, i)
        for x in range(cx):
            block[x, at, :] = values[x]
        return 0

    lax.fori_loop(0, cy // 16, second_solve, 0)

    def inverse_z(rows):
        a, b = split(rows)
        both = mm(jnp.concatenate([a, b], axis=1), sz[...])
        return both[:, :nz] + both[:, nz:]

    def backward(i, _):
        pair_x = jnp.concatenate([block[2 * i], block[2 * i + 1]], axis=1)
        out = dot_left(sy[0], sy[1], pair_x)
        out = inverse_z(jnp.concatenate([out[:, :nz], out[:, nz:]], axis=0))
        grid[2 * i + 1, pl.ds(8, cy), :] = out[:cy]
        grid[2 * i + 2, pl.ds(8, cy), :] = out[cy:]
        return 0

    lax.fori_loop(0, half, backward, 0)
    copy_out = pltpu.make_async_copy(grid.at[pl.ds(1, cx), pl.ds(8, cy), :], pot_h, osem)
    copy_out.start()
    pair_x = jnp.concatenate([solved[0, :cy], solved[1, :cy]], axis=1)
    out = dot_left(sy[0], sy[1], pair_x)
    rest = jnp.concatenate([out[:, :nz], out[:, nz:], solved[0, cy:], solved[1, cy:]], axis=0)
    rest = inverse_z(rest)
    grid[0, pl.ds(8, cy), :] = rest[:cy]
    grid[cx + 1, pl.ds(8, cy), :] = rest[cy : 2 * cy]
    pad = 128 - cy
    for e in range(2):
        lines = rest[2 * cy + pad * e : 2 * cy + pad * (e + 1)]
        at = pl.ds(7 if e == 0 else 8 + cy, 1)
        for x in range(cx):
            grid[x + 1, at, :] = lines[x : x + 1]
    for e in range(2):
        lines = rest[2 * cy + pad * e : 2 * cy + pad * (e + 1)]
        for s in range(2):
            grid[(cx + 1) * e, pl.ds(7 if s == 0 else 8 + cy, 1), :] = lines[cx + s : cx + s + 1]

    loads["fold"].wait()
    per_y, per_z = cy // 4, nz // 4
    lanes8 = lax.broadcasted_iota(jnp.int32, (8, 128), 1)
    pick = (
        lax.broadcasted_iota(jnp.int32, (16, 128), 1) // 8 == lax.broadcasted_iota(jnp.int32, (16, 128), 0)
    )
    lane6 = lax.rem(lax.broadcasted_iota(jnp.int32, (6, 128), 1), 8)
    row6 = lax.broadcasted_iota(jnp.int32, (6, 128), 0)
    some = 4

    def gather(i, _):
        cut, odd = [], []
        for c in range(2 * some):
            code = jnp.maximum(ghost[0, 2 * some * i + c], 0)
            ix = code // (per_y * per_z)
            iy = lax.rem(code // per_z, per_y)
            iz = lax.rem(code, per_z)
            rows = grid[pl.ds(4 * ix, 6), pl.ds(7 + 4 * iy, 8), :]
            inside = (lanes8 >= 4 * iz - 1) & (lanes8 <= 4 * iz + 4) & (sub < 6)
            cut.append(jnp.where(inside[None], rows, 0.0).reshape(48, 128))
            odd.append(lax.rem(iz, 2))
        a, b = split(jnp.concatenate(cut, axis=0))
        out = mm(jnp.concatenate([a, b], axis=1), fold[...]).reshape(2 * some * 3, 16, 128)
        out = jnp.sum(jnp.where(pick[None], out, 0.0), axis=1)
        for k in range(some):
            d = some * i + k
            mini = out[6 * k : 6 * k + 6]
            turned = jnp.where(lane6 < 4, pltpu.roll(mini, 124, 1), pltpu.roll(mini, 4, 1))
            which = jnp.where(row6 < 3, odd[2 * k], odd[2 * k + 1])
            mini = jnp.where(which == 1, turned, mini)
            slots = [
                jnp.full((1, 128), ghost[1, 2 * d + c].astype(F32), F32) for c in range(2)
            ]
            s6[pl.ds(pl.multiple_of(8 * d, 8), 8), :] = jnp.concatenate([mini] + slots, axis=0)
        return 0

    lax.fori_loop(0, nf // some, gather, 0)

    ex6 = ("fft", tile(s6), tile(r6), s6s, r6s)
    send(*ex6)
    r6[mine, :] = s6[mine, :]
    sent(*ex4)
    copy_out.wait()
    receive(*ex6)
    blocks[...] = r6[...]
    sent(*ex6)


def patch_kernel(
    blocks, most, change_h, fluid_h, pot_in, weave,
    fine, moved, pot_out,
    fluid, change, force, state, hold, sems,
):
    count = fine.shape[-1]
    nf = blocks.shape[0] // 8
    copies = [
        pltpu.make_async_copy(fluid_h.at[0], fluid.at[0], sems.at[0]),
        pltpu.make_async_copy(pot_in, hold, sems.at[1]),
        pltpu.make_async_copy(change_h, change, sems.at[2]),
        pltpu.make_async_copy(fluid_h.at[pl.ds(1, 4)], fluid.at[pl.ds(1, 4)], sems.at[3]),
    ]
    for c in copies:
        c.start()
    copy_out = pltpu.make_async_copy(hold, pot_out, sems.at[4])
    groups = 128 // count

    lanes = lax.rem(lax.broadcasted_iota(jnp.int32, (nf, 128), 1), count)
    hot = jnp.concatenate(
        [
            jnp.where(blocks[pl.ds(6 + c, nf, stride=8), :] == lanes.astype(F32), 1.0, 0.0)
            for c in range(2)
        ],
        axis=0,
    ).astype(BF16)
    within, outside = [], []
    for t in range(3):
        came = jnp.concatenate([blocks[pl.ds(c * 3 + t, nf, stride=8), :] for c in range(2)], axis=0)
        a, b = split(came.T)
        placed = mm(a, hot) + mm(b, hot)
        a, b = split(placed)
        woven = mm(weave[...], a) + mm(weave[...], b)
        woven = woven.reshape(2, 2, 8, 8, 128)
        within += [woven[0, 0], woven[0, 1]]
        outside += [woven[1, 0], woven[1, 1]]

    z = lax.broadcasted_iota(jnp.int32, (8, 128), 0)
    q = lax.broadcasted_iota(jnp.int32, (8, 128), 1) // count
    bottom, top, zeven = z == 0, z == 7, lax.rem(z, 2) == 0
    zodd = jnp.logical_not(zeven)
    first, final = q == 0, q == 3

    def choose(values, shift, y):
        out = values[shift + 3][y]
        for i in (2, 1, 0):
            out = jnp.where(q == i, values[shift + i][y], out)
        return out

    def along_x(values, r, y):
        if r == 0:
            return 0.25 * choose(values, 0, y) + 0.75 * choose(values, 1, y)
        return 0.75 * choose(values, 1, y) + 0.25 * choose(values, 2, y)

    def between(values, j):
        low = j // 2
        return (
            0.75 * values[low] + 0.25 * values[low + 1]
            if j % 2 == 0
            else 0.25 * values[low] + 0.75 * values[low + 1]
        )

    copies[0].wait()
    scale = 1.0 / (6.0 + SCREEN * FINE_STEP * FINE_STEP)
    layers = {}
    rims = {}
    for r in range(2):
        plane = [along_x(within, r, y) for y in range(6)]
        for jy in range(10):
            value = between(plane, jy)
            if 1 <= jy <= 8:
                state[r, jy - 1] = value
            else:
                rims[r, jy] = value
        plane = [along_x(outside, r, y) for y in range(6)]
        for jy in range(1, 9):
            layers[r, jy - 1] = between(plane, jy)
    ends = (
        [0.75 * within[0][y] + 0.25 * within[1][y] for y in range(6)],
        [0.25 * within[4][y] + 0.75 * within[5][y] for y in range(6)],
    )
    for r in range(2):
        for y in range(8):
            rho = jnp.concatenate(
                [fluid[0, 2 * i + r + 2, y + 2, pl.ds(2, 8), :] for i in range(groups)], axis=1
            )
            side = jnp.where(first if r == 0 else final, between(ends[r], y + 1), 0.0)
            ghost = layers[r, y] + side
            if y == 0:
                ghost = ghost + rims[r, 0]
            if y == 7:
                ghost = ghost + rims[r, 9]
            force[r, y] = (OMEGA * scale) * (ghost - FINE_STEP * FINE_STEP * rho)

    copies[1].wait()
    copy_out.start()

    def beside(r, y, v):
        other = state[1 - r, y]
        if r == 0:
            far = jnp.where(first, 0.0, pltpu.roll(other, count, 1))
        else:
            far = jnp.where(final, 0.0, pltpu.roll(other, 128 - count, 1))
        return other, far

    def sweep(_, carry):
        for colour in (0, 1):
            for r in range(2):
                for y in range(8):
                    v = state[r, y]
                    other, far = beside(r, y, v)
                    near = (other + far) + (
                        jnp.where(bottom, 0.0, pltpu.roll(v, 1, 0)) + jnp.where(top, 0.0, pltpu.roll(v, 7, 0))
                    )
                    if y > 0:
                        near = near + state[r, y - 1]
                    if y < 7:
                        near = near + state[r, y + 1]
                    new = (1.0 - OMEGA) * v + ((OMEGA * scale) * near + force[r, y])
                    mask = zeven if (r + y + colour) % 2 == 0 else zodd
                    state[r, y] = jnp.where(mask, new, v)
        return carry

    lax.fori_loop(0, SWEEPS, sweep, 0)

    copies[2].wait()
    copies[3].wait()
    step = COURANT * FINE_STEP / most[pl.ds(0, 1), pl.ds(0, count)]
    rate = step / FINE_STEP
    for r in range(2):
        for y in range(8):
            v = state[r, y]
            other, far = beside(r, y, v)
            far = far + jnp.where(first if r == 0 else final, between(ends[r], y + 1), 0.0)
            layer = layers[r, y]
            down = state[r, y - 1] if y > 0 else rims[r, 0]
            up = state[r, y + 1] if y < 7 else rims[r, 9]
            pull = (
                far - other if r == 0 else other - far,
                down - up,
                jnp.where(bottom, layer, pltpu.roll(v, 1, 0)) - jnp.where(top, layer, pltpu.roll(v, 7, 0)),
            )
            for i in range(groups):
                x = 2 * i + r
                at = slice(count * i, count * (i + 1))
                fine[x, y] = v[:, at]
                cons = [fluid[k, x + 2, y + 2, pl.ds(2, 8), :] for k in range(5)]
                work = 0.0
                moved[0, x, y] = cons[0] - rate * change[0, x, y]
                for n in range(3):
                    force_n = pull[n][:, at]
                    moved[1 + n, x, y] = cons[1 + n] - rate * change[1 + n, x, y] + step * cons[0] * force_n
                    work = work + cons[1 + n] * force_n
                moved[4, x, y] = cons[4] - rate * change[4, x, y] + step * work
    copy_out.wait()


def root_call(ghost, rho, fluid, nf, ng):
    cx, cy, nz = rho.shape
    kz = nz // ng
    ny = ng * cy
    count = fluid.shape[-1]
    tab = tables(nf, ng, cx, cy, nz)
    consts = [jnp.asarray(tab[n]) for n in NAMES]
    vm = lambda shape, dtype=F32: pltpu.VMEM(shape, dtype)
    anyspace = pl.BlockSpec(memory_space=pl.ANY)
    vspace = pl.BlockSpec(memory_space=pltpu.VMEM)
    dma = pltpu.SemaphoreType.DMA
    local = {n: tab[n].shape for n in NAMES}
    local["inv"] = local["inv"][1:]
    local["pair"] = local["pair"][2:]
    limit = 56 * 1024 * 1024
    potential, blocks, most, change = pl.pallas_call(
        functools.partial(root_kernel, (nf, ng, cx, cy, nz)),
        out_shape=(
            jax.ShapeDtypeStruct((cx, cy, nz), F32),
            jax.ShapeDtypeStruct((nf * 8, 128), F32),
            jax.ShapeDtypeStruct((8, 128), F32),
            jax.ShapeDtypeStruct((5, 8, 8, 8, count), F32),
        ),
        in_specs=[pl.BlockSpec(memory_space=pltpu.SMEM)] + [anyspace] * (2 + len(NAMES)),
        out_specs=(anyspace, vspace, vspace, vspace),
        scratch_shapes=[vm((cx, cy, nz))]
        + [vm(local[n], consts[i].dtype) for i, n in enumerate(NAMES)]
        + [
            vm(fluid.shape), vm((5, 12, 12, 8, count)),
            vm((cx, cy, nz)),
            vm((2, 128, nz)),
            vm((cx, 8, nz)),
            vm((cx + 2, cy + 16, nz)),
            vm((cx, kz, ny)),
            vm((2, nz, 128)), vm((ng, 2, kz, 128)),
            vm((nf * 8, 128)), vm((nf * 8, 128)),
            vm((nf * 8, 128)), vm((nf * 8, 128)),
            vm((ng, 2, kz, 128)), vm((2, ng, kz, 128)),
            vm((nf * 8, 128)), vm((nf * 8, 128)),
            vm((2 * nf, 8, 128)), vm((2 * nf, 8, 128)),
            vm((5, 8, 8, count)),
            dma((14,)), dma,
            dma((ng,)), dma((ng,)),
            dma((nf,)), dma((nf,)),
            dma((nf,)), dma((nf,)),
            dma((ng,)), dma((ng,)),
            dma((nf,)), dma((nf,)),
        ],
        compiler_params=pltpu.CompilerParams(
            collective_id=0, has_side_effects=True, vmem_limit_bytes=limit
        ),
    )(ghost, rho, fluid, *consts)
    fine, moved, potential = pl.pallas_call(
        patch_kernel,
        out_shape=(
            jax.ShapeDtypeStruct((8, 8, 8, count), F32),
            jax.ShapeDtypeStruct((5, 8, 8, 8, count), F32),
            jax.ShapeDtypeStruct((cx, cy, nz), F32),
        ),
        in_specs=[vspace, vspace, anyspace, anyspace, anyspace, vspace],
        out_specs=(vspace, vspace, anyspace),
        scratch_shapes=[
            vm(fluid.shape), vm((5, 8, 8, 8, count)),
            vm((2, 8, 8, 128)), vm((2, 8, 8, 128)), vm((cx, cy, nz)),
            dma((5,)),
        ],
        compiler_params=pltpu.CompilerParams(vmem_limit_bytes=limit),
    )(blocks, most, change, fluid, potential, jnp.asarray(tab["weave"]))
    return potential, fine, moved


def per_device(root_density, patch_fluid, ghost_list):
    nf = lax.axis_size("fft")
    ng = lax.axis_size("grp")
    return root_call(ghost_list[:, 0], root_density, patch_fluid, nf, ng)


def solution(mesh):
    return jax.shard_map(
        per_device,
        mesh=mesh,
        in_specs=(
            P("fft", "grp", None),
            P(None, None, None, None, ("fft", "grp")),
            P(None, ("fft", "grp"), None),
        ),
        out_specs=(
            P("fft", "grp", None),
            P(None, None, None, ("fft", "grp")),
            P(None, None, None, None, ("fft", "grp")),
        ),
        check_vma=False,
    )
```

```python
import functools

import jax
import jax.numpy as jnp
import ml_dtypes
import numpy as np
from jax import lax
from jax.experimental import pallas as pl
from jax.experimental.pallas import tpu as pltpu
from jax.sharding import PartitionSpec as P

SWEEPS = 8
GAMMA = 5.0 / 3.0
SCREEN = 0.0006
OMEGA = 1.5
COURANT = 0.4
FINE_STEP = 0.5
F32 = jnp.float32
BF16 = jnp.bfloat16


def sine(count):
    index = np.arange(1, count + 1)
    return np.sqrt(2.0 / (count + 1)) * np.sin(
        np.pi * (np.outer(index, index) % (2 * (count + 1))) / (count + 1)
    )


def eigen(count):
    return 4.0 * np.sin(np.pi * np.arange(1, count + 1) / (2 * (count + 1))) ** 2


def halves(table):
    high = table.astype(ml_dtypes.bfloat16)
    low = (table - high.astype(np.float64)).astype(ml_dtypes.bfloat16)
    return np.stack([high, low])


@functools.lru_cache(None)
def tables(nf, ng, cx, cy, nz):
    ny = ng * cy
    kz = nz // ng
    sz, sy, sx, full = sine(nz), sine(cy), sine(cx), sine(ny)
    lam = eigen(cy)[:, None] + eigen(nz)[None, :] + SCREEN
    steps = [1.0 / (2.0 + lam)]
    for _ in range(1, cx // 2):
        steps.append(1.0 / (2.0 + lam - steps[-1]))
    steps.append(1.0 / (1.0 - steps[-1] ** 2))
    edge = np.zeros((ng, 2, ny))
    wide = np.zeros((ng, 128, ny))
    back = np.zeros((ng, 128, ny))
    for d in range(ng):
        if d > 0:
            edge[d, 0] = full[d * cy - 1]
        if d < ng - 1:
            edge[d, 1] = full[(d + 1) * cy]
        wide[d, :cy] = sy @ full[d * cy : (d + 1) * cy]
        back[d, :cy] = wide[d, :cy]
        back[d, cy + cx] = edge[d, 0]
        back[d, cy + cx + 1] = edge[d, 1]
    repeated = np.repeat(edge.reshape(2 * ng, ny), kz, axis=0)
    denom = (
        eigen(cx)[None, :, None, None]
        + eigen(nz).reshape(ng, 1, kz, 1)
        + eigen(ny)[None, None, None, :]
        + SCREEN
    )
    phi = 2.0 * np.arcsinh(np.sqrt(eigen(ny)[None, :] + eigen(nz)[:, None] + SCREEN) / 2.0)

    def ratio(m, n):
        return np.exp(-(n - m) * phi) * np.expm1(-2 * m * phi) / np.expm1(-2 * n * phi)

    pair = np.zeros((ng, nf, 2, 8, 128))
    for i, values in enumerate((ratio(cx - 1, cx), ratio(1, cx))):
        pair[:, :, i, :3] = values.reshape(ng, nf, 3, 128)
    spread = np.zeros((10, 6))
    for j in range(10):
        at = j / 2 + 0.25
        low = int(np.floor(at))
        spread[j, low] += 1 - (at - low)
        spread[j, low + 1] += at - low
    inner = np.zeros((8, 8))
    inner[:, :6] = spread[1:9]
    outer = np.zeros((8, 8))
    outer[0, :6] = spread[0]
    outer[7, :6] = spread[9]
    weave = np.concatenate([np.kron(np.eye(16), inner), np.kron(np.eye(16), outer)])
    lanes = np.arange(128)
    fold = ((lanes[:, None] + 1) % 8 == lanes[None, :] % 8).astype(np.float64)
    column = np.broadcast_to(sy[0][:, None], (cy, 128))
    as32 = lambda t: np.ascontiguousarray(t, dtype=np.float32)
    szh, szl = halves(sz)
    return dict(
        sz=np.block([[szh, szl], [szh, np.zeros_like(szh)]]).astype(ml_dtypes.bfloat16),
        sy=np.concatenate(halves(sy)),
        sx=as32(sx),
        steps=as32(np.stack(steps)),
        wide=halves(wide.reshape(ng * 128, ny)),
        back=halves(np.ascontiguousarray(back.reshape(ng * 128, ny).T)),
        edge=halves(repeated),
        edget=halves(np.ascontiguousarray(repeated.T)),
        inv=as32(1.0 / denom),
        pair=as32(pair),
        weave=weave.astype(ml_dtypes.bfloat16),
        fold=np.concatenate([fold, fold]).astype(ml_dtypes.bfloat16),
        column=as32(column),
    )


NAMES = (
    "sz", "sy", "sx", "steps", "wide", "back", "edge", "edget", "inv", "pair", "fold", "column",
)


def split(value):
    high = value.astype(BF16)
    return high, (value - high.astype(F32)).astype(BF16)


def mm(a, b):
    return jnp.dot(a, b, preferred_element_type=F32)


def dot_right(value, high, low):
    a, b = split(value)
    return mm(a, high) + (mm(b, high) + mm(a, low))


def dot_left(both, value):
    rows = both.shape[0] // 2
    a, b = split(value)
    main = mm(both, a)
    return main[:rows] + (main[rows:] + mm(both[:rows], b))


def root_kernel(
    cfg,
    ghost, rho, fluid_h,
    sz_h, sy_h, sx_h, steps_h, wide_h, back_h, edge_h, edget_h, inv_h, pair_h, fold_h, column_h,
    pot_h, blocks, most_out, change,
    src, sz, sy, sx, steps, wide, back, edge, edget, inv, pair, fold, column, fluid, prim,
    block, solved, part, grid, hfield,
    s1, r1, s2, r2, s3, r3, s4, r4, s6, r6, chain, mults, last_face,
    tsem, osem, x1, x2, x3, x4, x6,
):
    nf, ng, cx, cy, nz = cfg
    kz = nz // ng
    ny = ng * cy
    half = cx // 2
    f = lax.axis_index("fft")
    g = lax.axis_index("grp")

    ny_chips = 4 if nf % 4 == 0 else 1
    nz_chips = nf // ny_chips
    barrier = pltpu.get_barrier_semaphore()

    def grp_partner(k):
        return lax.rem(g + k, ng)

    def fft_partner(k):
        a, b = k // ny_chips, lax.rem(k, ny_chips)
        dz = nz_chips // 2 + ((a + 1) // 2) * (1 - 2 * lax.rem(a, 2))
        dy = ny_chips // 2 + ((b + 1) // 2) * (1 - 2 * lax.rem(b, 2))
        return lax.rem(f // ny_chips + dz, nz_chips) * ny_chips + lax.rem(lax.rem(f, ny_chips) + dy, ny_chips)

    ways = {"grp": (1, ng, grp_partner, g), "fft": (0, nf - 1, fft_partner, f)}

    def hello(axis):
        begin, end, partner, _ = ways[axis]

        def body(k, _):
            pl.semaphore_signal(
                barrier, inc=1, device_id={axis: partner(k)}, device_id_type=pl.DeviceIdType.MESH
            )
            return 0

        lax.fori_loop(begin, end, body, 0, unroll=True)

    hello("fft")
    hello("grp")

    loads = {}
    order = [
        ("rho", rho, src), ("sz", sz_h, sz), ("sy", sy_h, sy), ("steps", steps_h, steps),
        ("column", column_h, column), ("pair", pair_h.at[g, f], pair), ("wide", wide_h, wide),
        ("sx", sx_h, sx), ("edge", edge_h, edge), ("inv", inv_h.at[g], inv),
        ("fluid", fluid_h, fluid), ("edget", edget_h, edget), ("back", back_h, back), ("fold", fold_h, fold),
    ]
    for i, (name, a, b) in enumerate(order):
        loads[name] = pltpu.make_async_copy(a, b, tsem.at[i])
        loads[name].start()

    sub = lax.broadcasted_iota(jnp.int32, (8, 128), 0)
    even = lax.rem(sub, 2) == 0

    loads["rho"].wait()
    loads["sz"].wait()
    loads["sy"].wait()

    def forward(i, _):
        rows = src[pl.ds(2 * i, 2)].reshape(2 * cy, nz)
        a, b = split(rows)
        both = mm(jnp.concatenate([a, b], axis=1), sz[...])
        both = both[:, :nz] + both[:, nz:]
        pair_x = jnp.concatenate([both[:cy], both[cy:]], axis=1)
        out = dot_left(sy[...], pair_x)
        block[2 * i] = out[:, :nz]
        block[2 * i + 1] = out[:, nz:]
        return 0

    lax.fori_loop(0, half, forward, 0, unroll=3)

    loads["steps"].wait()
    loads["column"].wait()

    def solve(fetch, i):
        at = pl.ds(pl.multiple_of(16 * i, 16), 16)
        low, high = [], []
        for j in range(half):
            m = steps[j, at, :]
            a, b = fetch(j, at), fetch(cx - 1 - j, at)
            if j == 0:
                low.append(-m * a)
                high.append(-m * b)
            else:
                low.append(m * (low[-1] - a))
                high.append(m * (high[-1] - b))
        m, scale = steps[half - 1, at, :], steps[half, at, :]
        a, b = low[-1], high[-1]
        low[-1] = (a + m * b) * scale
        high[-1] = (b + m * a) * scale
        for j in range(half - 2, -1, -1):
            m = steps[j, at, :]
            low[j] = low[j] + m * low[j + 1]
            high[j] = high[j] + m * high[j + 1]
        return at, low + high[::-1]

    part[...] = jnp.zeros_like(part)

    def first(i, _):
        at, values = solve(lambda x, at: block[x, at, :], i)
        col = column[at, :]
        for x in range(cx):
            v = values[x] * col
            part[x] += v[:8] + v[8:]
        solved[0, at, :] = values[0]
        solved[1, at, :] = values[cx - 1]
        return 0

    lax.fori_loop(0, cy // 16, first, 0)
    sums = part[...]
    sign = jnp.where(even, 1.0, -1.0)
    edges = (jnp.sum(sums, axis=1), jnp.sum(sums * sign[None], axis=1))
    for e in range(2):
        solved[e, pl.ds(cy, cx), :] = edges[e]
        solved[e, pl.ds(cy + cx, 8), :] = jnp.zeros((8, 128), F32)
        s1[e] = solved[e].T


    cells = pl.ds(2, 8)

    def cell_values(cons):
        dens = cons[0]
        over = 1.0 / dens
        vel = [m * over for m in cons[1:4]]
        kinetic = 0.5 * (cons[1] * vel[0] + cons[2] * vel[1] + cons[3] * vel[2])
        return [dens] + vel + [(GAMMA - 1.0) * (cons[4] - kinetic)]

    def sound(dens, pres):
        return jnp.sqrt(GAMMA * pres) * lax.rsqrt(dens)

    def make_cells(x, _):
        for y in range(12):
            w = cell_values([fluid[v, x, y, cells, :] for v in range(5)])
            for v in range(5):
                prim[v, x, y] = w[v]
        return 0

    def top_speed():
        def body(x, top):
            for y in range(2, 10):
                w = [prim[v, x + 2, y] for v in range(5)]
                fast = jnp.maximum(jnp.maximum(jnp.abs(w[1]), jnp.abs(w[2])), jnp.abs(w[3]))
                top = jnp.maximum(top, fast + sound(w[0], w[4]))
            return top
        return jnp.max(lax.fori_loop(0, 8, body, jnp.zeros((8, fluid.shape[-1]), F32)))

    def states(before, here, after):
        low, high = [], []
        for a, b, c in zip(before, here, after):
            p, q = b - a, c - b
            half_slope = 0.5 * (
                jnp.maximum(0.0, jnp.minimum(p, q)) + jnp.minimum(0.0, jnp.maximum(p, q))
            )
            low.append(b - half_slope)
            high.append(b + half_slope)
        return low, high

    def side(w, n):
        dens, vel, pres = w[0], w[1:4], w[4]
        energy = pres * (1.0 / (GAMMA - 1.0)) + 0.5 * dens * (
            vel[0] * vel[0] + vel[1] * vel[1] + vel[2] * vel[2]
        )
        mom = [dens * v for v in vel]
        flux = [mom[n]] + [mom[n] * v for v in vel] + [(energy + pres) * vel[n]]
        flux[1 + n] = flux[1 + n] + pres
        return [dens] + mom + [energy], flux, jnp.abs(vel[n]) + sound(dens, pres)

    def face(left, right, n):
        cl, fl, al = side(left, n)
        cr, fr, ar = side(right, n)
        top = jnp.maximum(al, ar)
        return [0.5 * ((a + b) - top * (d - c)) for a, b, c, d in zip(fl, fr, cl, cr)]

    def sweep_line(get, put, n):
        w = [get(0), get(1), get(2)]
        _, high = states(*w)
        flux = None
        for i in range(2, 11):
            w = [w[1], w[2], get(i + 1)]
            low, high_next = states(*w)
            now = face(high, low, n)
            if flux is not None:
                put(i - 3, [b - a for a, b in zip(flux, now)])
            flux, high = now, high_next

    def lines_x(y, _):
        def get(i):
            return [prim[v, i, y + 2] for v in range(5)]

        def put(i, values):
            for v in range(5):
                change[v, i, y] = values[v]

        sweep_line(get, put, 0)
        return 0

    def lines_y(x, _):
        def get(i):
            return [prim[v, x + 2, i] for v in range(5)]

        def put(i, values):
            for v in range(5):
                change[v, x, i] += values[v]

        sweep_line(get, put, 1)
        return 0

    def last_faces(x, _):
        w = [
            cell_values([fluid[v, x + 2, cells, k, :] for v in range(5)]) for k in (8, 9, 10, 11)
        ]
        _, high = states(w[0], w[1], w[2])
        low, _ = states(w[1], w[2], w[3])
        flux = face(high, low, 2)
        for v in range(5):
            last_face[v, x] = flux[v]
        return 0

    def lines_z(x, _):
        row = lax.broadcasted_iota(jnp.int32, (8, fluid.shape[-1]), 0)
        for y in range(8):
            w = [
                cell_values([fluid[v, x + 2, y + 2, pl.ds(k, 8), :] for v in range(5)]) if k != 2
                else [prim[v, x + 2, y + 2] for v in range(5)]
                for k in range(4)
            ]
            _, high = states(w[0], w[1], w[2])
            low, _ = states(w[1], w[2], w[3])
            flux = face(high, low, 2)
            for v in range(5):
                after = jnp.where(row == 7, last_face[v, x, pl.ds(y, 1), :], pltpu.roll(flux[v], 7, 0))
                change[v, x, y] += after - flux[v]
        return 0

    pl.semaphore_wait(barrier, ng + nf - 2)

    def send(axis, source, target, every, sems):
        begin, end, partner, pos = ways[axis]

        def body(k, _):
            to = partner(k)
            pltpu.make_async_remote_copy(
                source(to), target(pos), sems.at[0], sems.at[1], device_id={axis: to},
                device_id_type=pl.DeviceIdType.MESH,
            ).start()
            return 0

        lax.fori_loop(begin, end, body, 0, unroll=True)

    def whole(axis, source, target, every, sems):
        return pltpu.make_async_remote_copy(
            every, every, sems.at[0], sems.at[1], device_id={axis: ways[axis][2](1)},
            device_id_type=pl.DeviceIdType.MESH,
        )

    def receive(*exchange):
        whole(*exchange).wait_recv()

    def sent(*exchange):
        whole(*exchange).wait_send()

    slice1 = lambda d: s1.at[:, pl.ds(pl.multiple_of(d * kz, kz), kz), :]
    ex1 = ("grp", slice1, lambda d: r1.at[d], r1.at[pl.ds(0, ng - 1)], x1)
    send(*ex1)
    r1[g] = s1[:, pl.ds(pl.multiple_of(g * kz, kz), kz), :]

    loads["pair"].wait()
    ca, cb = pair[0], pair[1]
    ca2, cb2 = ca * ca, cb * cb

    def coefficients(i, m):
        m0 = 1.0 / (1.0 - ca2 * m)
        mults[2 * i] = m0
        m1 = 1.0 / (1.0 - cb2 * m0)
        mults[2 * i + 1] = m1
        return m1

    lax.fori_loop(0, nf, coefficients, jnp.zeros((8, 128), F32))
    loads["fluid"].wait()
    lax.fori_loop(0, 12, make_cells, 0)
    most = jnp.full((1, 128), top_speed(), F32)
    loads["wide"].wait()
    loads["sx"].wait()
    loads["edge"].wait()
    loads["inv"].wait()
    receive(*ex1)

    main = jnp.concatenate([r1[d].reshape(2 * kz, 128) for d in range(ng)], axis=1)
    main = dot_right(main, wide[0], wide[1])
    across = r1[...].reshape(ng * 2 * kz, 128).T
    edge_x = across[cy : cy + cx]
    edge_k = jnp.dot(sx[...], edge_x, precision=lax.Precision.HIGHEST, preferred_element_type=F32)
    wide_lane = ng * 2 * kz
    diag = (
        lax.rem(lax.broadcasted_iota(jnp.int32, (kz, wide_lane), 1), kz)
        == lax.broadcasted_iota(jnp.int32, (kz, wide_lane), 0)
    )
    zero = jnp.zeros((kz, wide_lane), F32)
    sums = [jnp.zeros((kz, ny), F32), jnp.zeros((kz, ny), F32)]
    first_row = [float(v) for v in sine(cx)[0]]
    group = 4
    for x0 in range(0, cx, group):
        lhs = jnp.concatenate(
            [jnp.where(diag, jnp.broadcast_to(edge_k[x : x + 1], (kz, wide_lane)), zero) for x in range(x0, x0 + group)],
            axis=0,
        )
        out = dot_right(lhs, edge[0], edge[1])
        for x in range(x0, x0 + group):
            hd = out[(x - x0) * kz : (x - x0 + 1) * kz] * inv[x]
            hfield[x] = hd
            sums[x % 2] = sums[x % 2] + first_row[x] * hd
    rows = (main[:kz] + (sums[0] + sums[1]), main[kz:] + (sums[0] - sums[1]))
    for row in range(2):
        for j in range(6):
            s2[pl.ds((j // 3) * 8 + row * 3 + j % 3, kz, stride=16), :] = rows[row][:, j * 128 : (j + 1) * 128]
    for r in (6, 7):
        s2[pl.ds(r, nf, stride=8), :] = jnp.broadcast_to(most, (nf, 128))

    most_rows = lambda ref: ref.at[pl.ds(0, (nf - 1) * 8), :]
    tile = lambda ref: lambda d: ref.at[pl.ds(pl.multiple_of(d * 8, 8), 8), :]
    ex2 = ("fft", tile(s2), tile(r2), most_rows(r2), x2)
    send(*ex2)
    mine = pl.ds(pl.multiple_of(f * 8, 8), 8)
    r2[mine, :] = s2[mine, :]
    lax.fori_loop(0, 8, lines_x, 0)
    lax.fori_loop(0, 8, lines_y, 0)
    receive(*ex2)
    most = jnp.max(r2[pl.ds(6, nf, stride=8), :], axis=0, keepdims=True)

    last = jnp.zeros((8, 128), F32)
    prev = last
    for d in range(nf):
        msg = r2[8 * d : 8 * d + 8, :]
        other = pltpu.roll(msg, 5, 0)
        m0, m1 = mults[2 * d], mults[2 * d + 1]
        prev = m0 * (msg - cb * other) + (m0 * ca) * prev
        chain[2 * d] = prev
        prev = m1 * (other - cb * msg) + (m1 * cb) * prev
        chain[2 * d + 1] = prev
    chain[2 * nf - 1] = prev
    for j in range(2 * nf - 2, -1, -1):
        prev = chain[j] + (mults[j] * (cb if j % 2 == 0 else ca)) * prev
        chain[j] = prev
    for d in range(nf):
        left = chain[2 * d - 1] if d > 0 else last
        right = chain[2 * d + 2] if d < nf - 1 else last
        s3[8 * d : 8 * d + 8, :] = jnp.where(sub < 3, left, pltpu.roll(right, 3, 0))

    ex3 = ("fft", tile(s3), tile(r3), most_rows(r3), x3)
    send(*ex3)
    r3[mine, :] = s3[mine, :]
    loads["edget"].wait()
    loads["back"].wait()
    lax.fori_loop(0, 8, last_faces, 0)
    lax.fori_loop(0, 8, lines_z, 0)
    receive(*ex3)
    around = [
        jnp.concatenate(
            [r3[pl.ds((j // 3) * 8 + row * 3 + j % 3, kz, stride=16), :] for j in range(6)], axis=1
        )
        for row in range(2)
    ]
    out_rows = dot_right(jnp.concatenate(around, axis=0), back[0], back[1])
    mixed = (around[0] + around[1], around[0] - around[1])
    corr = []
    for x0 in range(0, cx, group):
        lhs = jnp.concatenate(
            [hfield[x] + (first_row[x] * inv[x]) * mixed[x % 2] for x in range(x0, x0 + group)], axis=0
        )
        out = dot_right(lhs, edget[0], edget[1])
        for x in range(group):
            corr.append(jnp.sum(jnp.where(diag, out[x * kz : (x + 1) * kz], zero), axis=0, keepdims=True))
    corr = jnp.concatenate(corr, axis=0)
    corr = jnp.dot(sx[...], corr, precision=lax.Precision.HIGHEST, preferred_element_type=F32)
    blank = jnp.zeros((cx, kz), F32)
    from_left = jnp.concatenate([blank, edge_x[:, :-kz]], axis=1)
    from_right = jnp.concatenate([edge_x[:, kz:], blank], axis=1)
    second = lax.rem(lax.broadcasted_iota(jnp.int32, (cx, wide_lane), 1) // kz, 2) == 1
    sides = corr + jnp.where(second, from_right, from_left)
    sides = jnp.concatenate(
        [jnp.zeros((cy, wide_lane), F32), sides, jnp.zeros((128 - cy - cx, wide_lane), F32)], axis=0
    ).T
    sides = jnp.where(
        lax.broadcasted_iota(jnp.int32, (wide_lane, 128), 1) == 127, jnp.broadcast_to(most, (wide_lane, 128)), sides
    )
    for d in range(ng):
        s4[d] = (out_rows[:, 128 * d : 128 * d + 128] + sides[2 * kz * d : 2 * kz * (d + 1)]).reshape(2, kz, 128)

    ex4 = ("grp", lambda d: s4.at[d], lambda d: r4.at[:, d], r4.at[:, pl.ds(0, ng - 1)], x4)
    send(*ex4)
    r4[:, g] = s4[g]
    sent(*ex1)
    sent(*ex2)
    sent(*ex3)
    receive(*ex4)
    for e in range(2):
        solved[e] = r4[e].reshape(nz, 128).T
    most_out[...] = jnp.full((8, 128), jnp.max(solved[0, pl.ds(127, 1), :]), F32)

    def second_solve(i, _):
        def fetch(x, at):
            va = solved[0, pl.ds(cy + x, 1), :]
            vb = solved[1, pl.ds(cy + x, 1), :]
            w = jnp.where(even, va + vb, va - vb)
            value = block[x, at, :] - column[at, :] * jnp.concatenate([w, w], axis=0)
            if x == 0:
                value = value - solved[0, at, :]
            if x == cx - 1:
                value = value - solved[1, at, :]
            return value

        at, values = solve(fetch, i)
        for x in range(cx):
            block[x, at, :] = values[x]
        return 0

    lax.fori_loop(0, cy // 16, second_solve, 0)

    def inverse_z(rows):
        a, b = split(rows)
        both = mm(jnp.concatenate([a, b], axis=1), sz[...])
        return both[:, :nz] + both[:, nz:]

    def backward(i, _):
        pair_x = jnp.concatenate([block[2 * i], block[2 * i + 1]], axis=1)
        out = dot_left(sy[...], pair_x)
        out = inverse_z(jnp.concatenate([out[:, :nz], out[:, nz:]], axis=0))
        grid[2 * i + 1, pl.ds(8, cy), :] = out[:cy]
        grid[2 * i + 2, pl.ds(8, cy), :] = out[cy:]
        return 0

    lax.fori_loop(0, half, backward, 0, unroll=3)
    copy_out = pltpu.make_async_copy(grid.at[pl.ds(1, cx), pl.ds(8, cy), :], pot_h, osem)
    copy_out.start()
    pair_x = jnp.concatenate([solved[0, :cy], solved[1, :cy]], axis=1)
    out = dot_left(sy[...], pair_x)
    rest = jnp.concatenate([out[:, :nz], out[:, nz:], solved[0, cy:], solved[1, cy:]], axis=0)
    rest = inverse_z(rest)
    grid[0, pl.ds(8, cy), :] = rest[:cy]
    grid[cx + 1, pl.ds(8, cy), :] = rest[cy : 2 * cy]
    pad = 128 - cy
    for e in range(2):
        lines = rest[2 * cy + pad * e : 2 * cy + pad * (e + 1)]
        at = pl.ds(7 if e == 0 else 8 + cy, 1)
        for x in range(cx):
            grid[x + 1, at, :] = lines[x : x + 1]
    for e in range(2):
        lines = rest[2 * cy + pad * e : 2 * cy + pad * (e + 1)]
        for s in range(2):
            grid[(cx + 1) * e, pl.ds(7 if s == 0 else 8 + cy, 1), :] = lines[cx + s : cx + s + 1]

    loads["fold"].wait()
    per_y, per_z = cy // 4, nz // 4
    lanes8 = lax.broadcasted_iota(jnp.int32, (8, 128), 1)
    pick = (
        lax.broadcasted_iota(jnp.int32, (16, 128), 1) // 8 == lax.broadcasted_iota(jnp.int32, (16, 128), 0)
    )
    lane6 = lax.rem(lax.broadcasted_iota(jnp.int32, (6, 128), 1), 8)
    row6 = lax.broadcasted_iota(jnp.int32, (6, 128), 0)
    some = 4

    def gather(i, _):
        cut, odd = [], []
        for c in range(2 * some):
            code = jnp.maximum(ghost[0, 2 * some * i + c], 0)
            ix = code // (per_y * per_z)
            iy = lax.rem(code // per_z, per_y)
            iz = lax.rem(code, per_z)
            rows = grid[pl.ds(4 * ix, 6), pl.ds(7 + 4 * iy, 8), :]
            inside = (lanes8 >= 4 * iz - 1) & (lanes8 <= 4 * iz + 4) & (sub < 6)
            cut.append(jnp.where(inside[None], rows, 0.0).reshape(48, 128))
            odd.append(lax.rem(iz, 2))
        a, b = split(jnp.concatenate(cut, axis=0))
        out = mm(jnp.concatenate([a, b], axis=1), fold[...]).reshape(2 * some * 3, 16, 128)
        out = jnp.sum(jnp.where(pick[None], out, 0.0), axis=1)
        for k in range(some):
            d = some * i + k
            mini = out[6 * k : 6 * k + 6]
            turned = jnp.where(lane6 < 4, pltpu.roll(mini, 124, 1), pltpu.roll(mini, 4, 1))
            which = jnp.where(row6 < 3, odd[2 * k], odd[2 * k + 1])
            mini = jnp.where(which == 1, turned, mini)
            slots = [
                jnp.full((1, 128), ghost[1, 2 * d + c].astype(F32), F32) for c in range(2)
            ]
            s6[pl.ds(pl.multiple_of(8 * d, 8), 8), :] = jnp.concatenate([mini] + slots, axis=0)
        return 0

    lax.fori_loop(0, nf // some, gather, 0, unroll=2)

    ex6 = ("fft", tile(s6), tile(r6), most_rows(r6), x6)
    send(*ex6)
    r6[mine, :] = s6[mine, :]
    sent(*ex4)
    copy_out.wait()
    receive(*ex6)
    blocks[...] = r6[...]
    sent(*ex6)


def patch_kernel(
    blocks, most, change_h, fluid_h, pot_in, weave,
    fine, moved, pot_out,
    fluid, change, force, state, hold, sems,
):
    count = fine.shape[-1]
    nf = blocks.shape[0] // 8
    copies = [
        pltpu.make_async_copy(fluid_h.at[0], fluid.at[0], sems.at[0]),
        pltpu.make_async_copy(pot_in, hold, sems.at[1]),
        pltpu.make_async_copy(change_h, change, sems.at[2]),
        pltpu.make_async_copy(fluid_h.at[pl.ds(1, 4)], fluid.at[pl.ds(1, 4)], sems.at[3]),
    ]
    for c in copies:
        c.start()
    copy_out = pltpu.make_async_copy(hold, pot_out, sems.at[4])
    groups = 128 // count

    lanes = lax.rem(lax.broadcasted_iota(jnp.int32, (nf, 128), 1), count)
    hot = jnp.concatenate(
        [
            jnp.where(blocks[pl.ds(6 + c, nf, stride=8), :] == lanes.astype(F32), 1.0, 0.0)
            for c in range(2)
        ],
        axis=0,
    ).astype(BF16)
    within, outside = [], []
    for t in range(3):
        came = jnp.concatenate([blocks[pl.ds(c * 3 + t, nf, stride=8), :] for c in range(2)], axis=0)
        a, b = split(came.T)
        placed = mm(a, hot) + mm(b, hot)
        a, b = split(placed)
        woven = mm(weave[...], a) + mm(weave[...], b)
        woven = woven.reshape(2, 2, 8, 8, 128)
        within += [woven[0, 0], woven[0, 1]]
        outside += [woven[1, 0], woven[1, 1]]

    z = lax.broadcasted_iota(jnp.int32, (8, 128), 0)
    q = lax.broadcasted_iota(jnp.int32, (8, 128), 1) // count
    bottom, top, zeven = z == 0, z == 7, lax.rem(z, 2) == 0
    zodd = jnp.logical_not(zeven)
    first, final = q == 0, q == 3

    def choose(values, shift, y):
        out = values[shift + 3][y]
        for i in (2, 1, 0):
            out = jnp.where(q == i, values[shift + i][y], out)
        return out

    def along_x(values, r, y):
        if r == 0:
            return 0.25 * choose(values, 0, y) + 0.75 * choose(values, 1, y)
        return 0.75 * choose(values, 1, y) + 0.25 * choose(values, 2, y)

    def between(values, j):
        low = j // 2
        return (
            0.75 * values[low] + 0.25 * values[low + 1]
            if j % 2 == 0
            else 0.25 * values[low] + 0.75 * values[low + 1]
        )

    copies[0].wait()
    scale = 1.0 / (6.0 + SCREEN * FINE_STEP * FINE_STEP)
    layers = {}
    rims = {}
    for r in range(2):
        plane = [along_x(within, r, y) for y in range(6)]
        for jy in range(10):
            value = between(plane, jy)
            if 1 <= jy <= 8:
                state[r, jy - 1] = value
            else:
                rims[r, jy] = value
        plane = [along_x(outside, r, y) for y in range(6)]
        for jy in range(1, 9):
            layers[r, jy - 1] = between(plane, jy)
    ends = (
        [0.75 * within[0][y] + 0.25 * within[1][y] for y in range(6)],
        [0.25 * within[4][y] + 0.75 * within[5][y] for y in range(6)],
    )
    for r in range(2):
        for y in range(8):
            rho = jnp.concatenate(
                [fluid[0, 2 * i + r + 2, y + 2, pl.ds(2, 8), :] for i in range(groups)], axis=1
            )
            side = jnp.where(first if r == 0 else final, between(ends[r], y + 1), 0.0)
            ghost = layers[r, y] + side
            if y == 0:
                ghost = ghost + rims[r, 0]
            if y == 7:
                ghost = ghost + rims[r, 9]
            force[r, y] = (OMEGA * scale) * (ghost - FINE_STEP * FINE_STEP * rho)

    copies[1].wait()
    copy_out.start()

    def beside(r, y, v):
        other = state[1 - r, y]
        if r == 0:
            far = jnp.where(first, 0.0, pltpu.roll(other, count, 1))
        else:
            far = jnp.where(final, 0.0, pltpu.roll(other, 128 - count, 1))
        return other, far

    def sweep(_, carry):
        for colour in (0, 1):
            for r in range(2):
                for y in range(8):
                    v = state[r, y]
                    other, far = beside(r, y, v)
                    near = (other + far) + (
                        jnp.where(bottom, 0.0, pltpu.roll(v, 1, 0)) + jnp.where(top, 0.0, pltpu.roll(v, 7, 0))
                    )
                    if y > 0:
                        near = near + state[r, y - 1]
                    if y < 7:
                        near = near + state[r, y + 1]
                    new = (1.0 - OMEGA) * v + ((OMEGA * scale) * near + force[r, y])
                    mask = zeven if (r + y + colour) % 2 == 0 else zodd
                    state[r, y] = jnp.where(mask, new, v)
        return carry

    lax.fori_loop(0, SWEEPS, sweep, 0)

    copies[2].wait()
    copies[3].wait()
    step = COURANT * FINE_STEP / most[pl.ds(0, 1), pl.ds(0, count)]
    rate = step / FINE_STEP
    for r in range(2):
        for y in range(8):
            v = state[r, y]
            other, far = beside(r, y, v)
            far = far + jnp.where(first if r == 0 else final, between(ends[r], y + 1), 0.0)
            layer = layers[r, y]
            down = state[r, y - 1] if y > 0 else rims[r, 0]
            up = state[r, y + 1] if y < 7 else rims[r, 9]
            pull = (
                far - other if r == 0 else other - far,
                down - up,
                jnp.where(bottom, layer, pltpu.roll(v, 1, 0)) - jnp.where(top, layer, pltpu.roll(v, 7, 0)),
            )
            for i in range(groups):
                x = 2 * i + r
                at = slice(count * i, count * (i + 1))
                fine[x, y] = v[:, at]
                cons = [fluid[k, x + 2, y + 2, pl.ds(2, 8), :] for k in range(5)]
                work = 0.0
                moved[0, x, y] = cons[0] - rate * change[0, x, y]
                for n in range(3):
                    force_n = pull[n][:, at]
                    moved[1 + n, x, y] = cons[1 + n] - rate * change[1 + n, x, y] + step * cons[0] * force_n
                    work = work + cons[1 + n] * force_n
                moved[4, x, y] = cons[4] - rate * change[4, x, y] + step * work
    copy_out.wait()


def root_call(ghost, rho, fluid, nf, ng):
    cx, cy, nz = rho.shape
    kz = nz // ng
    ny = ng * cy
    count = fluid.shape[-1]
    tab = tables(nf, ng, cx, cy, nz)
    consts = [jnp.asarray(tab[n]) for n in NAMES]
    vm = lambda shape, dtype=F32: pltpu.VMEM(shape, dtype)
    anyspace = pl.BlockSpec(memory_space=pl.ANY)
    vspace = pl.BlockSpec(memory_space=pltpu.VMEM)
    dma = pltpu.SemaphoreType.DMA
    local = {n: tab[n].shape for n in NAMES}
    local["inv"] = local["inv"][1:]
    local["pair"] = local["pair"][2:]
    limit = 56 * 1024 * 1024
    potential, blocks, most, change = pl.pallas_call(
        functools.partial(root_kernel, (nf, ng, cx, cy, nz)),
        out_shape=(
            jax.ShapeDtypeStruct((cx, cy, nz), F32),
            jax.ShapeDtypeStruct((nf * 8, 128), F32),
            jax.ShapeDtypeStruct((8, 128), F32),
            jax.ShapeDtypeStruct((5, 8, 8, 8, count), F32),
        ),
        in_specs=[pl.BlockSpec(memory_space=pltpu.SMEM)] + [anyspace] * (2 + len(NAMES)),
        out_specs=(anyspace, vspace, vspace, vspace),
        scratch_shapes=[vm((cx, cy, nz))]
        + [vm(local[n], consts[i].dtype) for i, n in enumerate(NAMES)]
        + [
            vm(fluid.shape), vm((5, 12, 12, 8, count)),
            vm((cx, cy, nz)),
            vm((2, 128, nz)),
            vm((cx, 8, nz)),
            vm((cx + 2, cy + 16, nz)),
            vm((cx, kz, ny)),
            vm((2, nz, 128)), vm((ng, 2, kz, 128)),
            vm((nf * 8, 128)), vm((nf * 8, 128)),
            vm((nf * 8, 128)), vm((nf * 8, 128)),
            vm((ng, 2, kz, 128)), vm((2, ng, kz, 128)),
            vm((nf * 8, 128)), vm((nf * 8, 128)),
            vm((2 * nf, 8, 128)), vm((2 * nf, 8, 128)),
            vm((5, 8, 8, count)),
            dma((14,)), dma,
            dma((2,)), dma((2,)), dma((2,)), dma((2,)), dma((2,)),
        ],
        compiler_params=pltpu.CompilerParams(
            collective_id=0, has_side_effects=True, vmem_limit_bytes=limit
        ),
    )(ghost, rho, fluid, *consts)
    fine, moved, potential = pl.pallas_call(
        patch_kernel,
        out_shape=(
            jax.ShapeDtypeStruct((8, 8, 8, count), F32),
            jax.ShapeDtypeStruct((5, 8, 8, 8, count), F32),
            jax.ShapeDtypeStruct((cx, cy, nz), F32),
        ),
        in_specs=[vspace, vspace, anyspace, anyspace, anyspace, vspace],
        out_specs=(vspace, vspace, anyspace),
        scratch_shapes=[
            vm(fluid.shape), vm((5, 8, 8, 8, count)),
            vm((2, 8, 8, 128)), vm((2, 8, 8, 128)), vm((cx, cy, nz)),
            dma((5,)),
        ],
        compiler_params=pltpu.CompilerParams(vmem_limit_bytes=limit),
    )(blocks, most, change, fluid, potential, jnp.asarray(tab["weave"]))
    return potential, fine, moved


def per_device(root_density, patch_fluid, ghost_list):
    nf = lax.axis_size("fft")
    ng = lax.axis_size("grp")
    return root_call(ghost_list[:, 0], root_density, patch_fluid, nf, ng)


def solution(mesh):
    return jax.shard_map(
        per_device,
        mesh=mesh,
        in_specs=(
            P("fft", "grp", None),
            P(None, None, None, None, ("fft", "grp")),
            P(None, ("fft", "grp"), None),
        ),
        out_specs=(
            P("fft", "grp", None),
            P(None, None, None, ("fft", "grp")),
            P(None, None, None, None, ("fft", "grp")),
        ),
        check_vma=False,
    )
```

```python
import functools

import jax
import jax.numpy as jnp
import ml_dtypes
import numpy as np
from jax import lax
from jax.experimental import pallas as pl
from jax.experimental.pallas import tpu as pltpu
from jax.sharding import PartitionSpec as P

SWEEPS = 8
GAMMA = 5.0 / 3.0
SCREEN = 0.0006
OMEGA = 1.5
COURANT = 0.4
FINE_STEP = 0.5
F32 = jnp.float32
BF16 = jnp.bfloat16


def sine(count):
    index = np.arange(1, count + 1)
    return np.sqrt(2.0 / (count + 1)) * np.sin(
        np.pi * (np.outer(index, index) % (2 * (count + 1))) / (count + 1)
    )


def eigen(count):
    return 4.0 * np.sin(np.pi * np.arange(1, count + 1) / (2 * (count + 1))) ** 2


def halves(table):
    high = table.astype(ml_dtypes.bfloat16)
    low = (table - high.astype(np.float64)).astype(ml_dtypes.bfloat16)
    return np.stack([high, low])


@functools.lru_cache(None)
def tables(nf, ng, cx, cy, nz):
    ny = ng * cy
    kz = nz // ng
    sz, sy, sx, full = sine(nz), sine(cy), sine(cx), sine(ny)
    lam = eigen(cy)[:, None] + eigen(nz)[None, :] + SCREEN
    steps = [1.0 / (2.0 + lam)]
    for _ in range(1, cx // 2):
        steps.append(1.0 / (2.0 + lam - steps[-1]))
    steps.append(1.0 / (1.0 - steps[-1] ** 2))
    edge = np.zeros((ng, 2, ny))
    wide = np.zeros((ng, 128, ny))
    back = np.zeros((ng, 128, ny))
    for d in range(ng):
        if d > 0:
            edge[d, 0] = full[d * cy - 1]
        if d < ng - 1:
            edge[d, 1] = full[(d + 1) * cy]
        wide[d, :cy] = sy @ full[d * cy : (d + 1) * cy]
        back[d, :cy] = wide[d, :cy]
        back[d, cy + cx] = edge[d, 0]
        back[d, cy + cx + 1] = edge[d, 1]
    repeated = np.repeat(edge.reshape(2 * ng, ny), kz, axis=0)
    denom = (
        eigen(cx)[None, :, None, None]
        + eigen(nz).reshape(ng, 1, kz, 1)
        + eigen(ny)[None, None, None, :]
        + SCREEN
    )
    phi = 2.0 * np.arcsinh(np.sqrt(eigen(ny)[None, :] + eigen(nz)[:, None] + SCREEN) / 2.0)

    def ratio(m, n):
        return np.exp(-(n - m) * phi) * np.expm1(-2 * m * phi) / np.expm1(-2 * n * phi)

    pair = np.zeros((ng, nf, 2, 8, 128))
    for i, values in enumerate((ratio(cx - 1, cx), ratio(1, cx))):
        pair[:, :, i, :3] = values.reshape(ng, nf, 3, 128)
    spread = np.zeros((10, 6))
    for j in range(10):
        at = j / 2 + 0.25
        low = int(np.floor(at))
        spread[j, low] += 1 - (at - low)
        spread[j, low + 1] += at - low
    inner = np.zeros((8, 8))
    inner[:, :6] = spread[1:9]
    outer = np.zeros((8, 8))
    outer[0, :6] = spread[0]
    outer[7, :6] = spread[9]
    weave = np.concatenate([np.kron(np.eye(16), inner), np.kron(np.eye(16), outer)])
    lanes = np.arange(128)
    fold = ((lanes[:, None] + 1) % 8 == lanes[None, :] % 8).astype(np.float64)
    column = np.broadcast_to(sy[0][:, None], (cy, 128))
    as32 = lambda t: np.ascontiguousarray(t, dtype=np.float32)
    szh, szl = halves(sz)
    syh, syl = halves(sy)
    return dict(
        sz=np.block([[szh, szl], [szh, np.zeros_like(szh)]]).astype(ml_dtypes.bfloat16),
        sy=np.block([[syh, syh], [syl, np.zeros_like(syl)]]).astype(ml_dtypes.bfloat16),
        sx=as32(sx),
        steps=as32(np.stack(steps)),
        wide=halves(wide.reshape(ng * 128, ny)),
        back=halves(np.ascontiguousarray(back.reshape(ng * 128, ny).T)),
        edge=halves(repeated),
        edget=halves(np.ascontiguousarray(repeated.T)),
        inv=as32(1.0 / denom),
        pair=as32(pair),
        weave=weave.astype(ml_dtypes.bfloat16),
        fold=np.concatenate([fold, fold]).astype(ml_dtypes.bfloat16),
        column=as32(column),
    )


NAMES = (
    "sz", "sy", "sx", "steps", "wide", "back", "edge", "edget", "inv", "pair", "fold", "column",
)


def split(value):
    high = value.astype(BF16)
    return high, (value - high.astype(F32)).astype(BF16)


def mm(a, b):
    return jnp.dot(a, b, preferred_element_type=F32)


def dot_right(value, high, low):
    rows = value.shape[0]
    a, b = split(value)
    main = mm(jnp.concatenate([a, b], axis=0), high)
    return main[:rows] + (main[rows:] + mm(a, low))


def dot_left(both, value):
    rows = both.shape[0] // 2
    a, b = split(value)
    out = mm(both, jnp.concatenate([a, b], axis=0))
    return out[:rows] + out[rows:]


def root_kernel(
    cfg,
    ghost, rho, fluid_h,
    sz_h, sy_h, sx_h, steps_h, wide_h, back_h, edge_h, edget_h, inv_h, pair_h, fold_h, column_h,
    pot_h, blocks, most_out, packed_h,
    src, sz, sy, sx, steps, wide, back, edge, edget, inv, pair, fold, column, fluid, prim,
    block, solved, part, grid, hfield,
    s1, r1, s2, r2, s3, r3, s4, r4, s6, r6, chain, mults, last_face, change, packed,
    tsem, osem, psem, x1, x2, x3, x4, x6,
):
    nf, ng, cx, cy, nz = cfg
    kz = nz // ng
    ny = ng * cy
    half = cx // 2
    f = lax.axis_index("fft")
    g = lax.axis_index("grp")

    quarter = cx // 4
    early = [
        (f"rho{i}", rho.at[pl.ds(quarter * i, quarter)], src.at[pl.ds(quarter * i, quarter)]) for i in range(4)
    ]
    early[1:1] = [("sz", sz_h, sz), ("sy", sy_h, sy)]
    early += [("steps", steps_h, steps), ("column", column_h, column), ("pair", pair_h.at[g, f], pair)]
    late = [
        ("wide", wide_h, wide), ("sx", sx_h, sx), ("edge", edge_h, edge), ("inv", inv_h.at[g], inv),
        ("fluid", fluid_h, fluid), ("edget", edget_h, edget), ("back", back_h, back), ("fold", fold_h, fold),
    ]
    loads = {
        name: pltpu.make_async_copy(a, b, tsem.at[i]) for i, (name, a, b) in enumerate(early + late)
    }
    for name, _, _ in early:
        loads[name].start()

    ny_chips = 4 if nf % 4 == 0 else 1
    nz_chips = nf // ny_chips
    barrier = pltpu.get_barrier_semaphore()

    def grp_partner(k):
        return lax.rem(g + k, ng)

    def fft_partner(k):
        a, b = k // ny_chips, lax.rem(k, ny_chips)
        dz = nz_chips // 2 + ((a + 1) // 2) * (1 - 2 * lax.rem(a, 2))
        dy = ny_chips // 2 + ((b + 1) // 2) * (1 - 2 * lax.rem(b, 2))
        return lax.rem(f // ny_chips + dz, nz_chips) * ny_chips + lax.rem(lax.rem(f, ny_chips) + dy, ny_chips)

    ways = {"grp": (1, ng, grp_partner, g), "fft": (0, nf - 1, fft_partner, f)}

    def hello(axis):
        begin, end, partner, _ = ways[axis]

        def body(k, _):
            pl.semaphore_signal(
                barrier, inc=1, device_id={axis: partner(k)}, device_id_type=pl.DeviceIdType.MESH
            )
            return 0

        lax.fori_loop(begin, end, body, 0, unroll=True)

    hello("fft")
    hello("grp")

    sub = lax.broadcasted_iota(jnp.int32, (8, 128), 0)
    even = lax.rem(sub, 2) == 0

    loads["sz"].wait()
    loads["sy"].wait()

    def forward(i, _):
        rows = src[pl.ds(2 * i, 2)].reshape(2 * cy, nz)
        a, b = split(rows)
        both = mm(jnp.concatenate([a, b], axis=1), sz[...])
        both = both[:, :nz] + both[:, nz:]
        pair_x = jnp.concatenate([both[:cy], both[cy:]], axis=1)
        out = dot_left(sy[...], pair_x)
        block[2 * i] = out[:, :nz]
        block[2 * i + 1] = out[:, nz:]
        return 0

    for part_of in range(4):
        loads[f"rho{part_of}"].wait()
        if part_of == 3:
            for name, _, _ in late:
                loads[name].start()
        lax.fori_loop(part_of * half // 4, (part_of + 1) * half // 4, forward, 0, unroll=True)

    loads["steps"].wait()
    loads["column"].wait()

    def solve(fetch, i):
        at = pl.ds(pl.multiple_of(16 * i, 16), 16)
        low, high = [], []
        for j in range(half):
            m = steps[j, at, :]
            a, b = fetch(j, at), fetch(cx - 1 - j, at)
            if j == 0:
                low.append(-m * a)
                high.append(-m * b)
            else:
                low.append(m * (low[-1] - a))
                high.append(m * (high[-1] - b))
        m, scale = steps[half - 1, at, :], steps[half, at, :]
        a, b = low[-1], high[-1]
        low[-1] = (a + m * b) * scale
        high[-1] = (b + m * a) * scale
        for j in range(half - 2, -1, -1):
            m = steps[j, at, :]
            low[j] = low[j] + m * low[j + 1]
            high[j] = high[j] + m * high[j + 1]
        return at, low + high[::-1]

    part[...] = jnp.zeros_like(part)

    def first(i, _):
        at, values = solve(lambda x, at: block[x, at, :], i)
        col = column[at, :]
        for x in range(cx):
            v = values[x] * col
            part[x] += v[:8] + v[8:]
        solved[0, at, :] = values[0]
        solved[1, at, :] = values[cx - 1]
        return 0

    lax.fori_loop(0, cy // 16, first, 0)
    sums = part[...]
    sign = jnp.where(even, 1.0, -1.0)
    edges = (jnp.sum(sums, axis=1), jnp.sum(sums * sign[None], axis=1))
    for e in range(2):
        solved[e, pl.ds(cy, cx), :] = edges[e]
        solved[e, pl.ds(cy + cx, 8), :] = jnp.zeros((8, 128), F32)
        s1[e] = solved[e].T


    cells = pl.ds(2, 8)

    def cell_values(cons):
        dens = cons[0]
        over = 1.0 / dens
        vel = [m * over for m in cons[1:4]]
        kinetic = 0.5 * (cons[1] * vel[0] + cons[2] * vel[1] + cons[3] * vel[2])
        return [dens] + vel + [(GAMMA - 1.0) * (cons[4] - kinetic)]

    def sound(dens, pres):
        return jnp.sqrt(GAMMA * pres) * lax.rsqrt(dens)

    def make_cells(x, _):
        for y in range(12):
            w = cell_values([fluid[v, x, y, cells, :] for v in range(5)])
            for v in range(5):
                prim[v, x, y] = w[v]
        return 0

    def top_speed():
        def body(x, top):
            for y in range(2, 10):
                w = [prim[v, x + 2, y] for v in range(5)]
                fast = jnp.maximum(jnp.maximum(jnp.abs(w[1]), jnp.abs(w[2])), jnp.abs(w[3]))
                top = jnp.maximum(top, fast + sound(w[0], w[4]))
            return top
        return jnp.max(lax.fori_loop(0, 8, body, jnp.zeros((8, fluid.shape[-1]), F32)))

    def states(before, here, after):
        low, high = [], []
        for a, b, c in zip(before, here, after):
            p, q = b - a, c - b
            half_slope = 0.5 * (
                jnp.maximum(0.0, jnp.minimum(p, q)) + jnp.minimum(0.0, jnp.maximum(p, q))
            )
            low.append(b - half_slope)
            high.append(b + half_slope)
        return low, high

    def side(w, n):
        dens, vel, pres = w[0], w[1:4], w[4]
        energy = pres * (1.0 / (GAMMA - 1.0)) + 0.5 * dens * (
            vel[0] * vel[0] + vel[1] * vel[1] + vel[2] * vel[2]
        )
        mom = [dens * v for v in vel]
        flux = [mom[n]] + [mom[n] * v for v in vel] + [(energy + pres) * vel[n]]
        flux[1 + n] = flux[1 + n] + pres
        return [dens] + mom + [energy], flux, jnp.abs(vel[n]) + sound(dens, pres)

    def face(left, right, n):
        cl, fl, al = side(left, n)
        cr, fr, ar = side(right, n)
        top = jnp.maximum(al, ar)
        return [0.5 * ((a + b) - top * (d - c)) for a, b, c, d in zip(fl, fr, cl, cr)]

    def sweep_line(get, put, n):
        w = [get(0), get(1), get(2)]
        _, high = states(*w)
        flux = None
        for i in range(2, 11):
            w = [w[1], w[2], get(i + 1)]
            low, high_next = states(*w)
            now = face(high, low, n)
            if flux is not None:
                put(i - 3, [b - a for a, b in zip(flux, now)])
            flux, high = now, high_next

    def lines_x(y, _):
        def get(i):
            return [prim[v, i, y + 2] for v in range(5)]

        def put(i, values):
            for v in range(5):
                change[v, i, y] = values[v]

        sweep_line(get, put, 0)
        return 0

    def lines_y(x, _):
        def get(i):
            return [prim[v, x + 2, i] for v in range(5)]

        def put(i, values):
            for v in range(5):
                change[v, x, i] += values[v]

        sweep_line(get, put, 1)
        return 0

    def last_faces(x, _):
        w = [
            cell_values([fluid[v, x + 2, cells, k, :] for v in range(5)]) for k in (8, 9, 10, 11)
        ]
        _, high = states(w[0], w[1], w[2])
        low, _ = states(w[1], w[2], w[3])
        flux = face(high, low, 2)
        for v in range(5):
            last_face[v, x] = flux[v]
        return 0

    def lines_z(x, _):
        row = lax.broadcasted_iota(jnp.int32, (8, fluid.shape[-1]), 0)
        for y in range(8):
            w = [
                cell_values([fluid[v, x + 2, y + 2, pl.ds(k, 8), :] for v in range(5)]) if k != 2
                else [prim[v, x + 2, y + 2] for v in range(5)]
                for k in range(4)
            ]
            _, high = states(w[0], w[1], w[2])
            low, _ = states(w[1], w[2], w[3])
            flux = face(high, low, 2)
            for v in range(5):
                after = jnp.where(row == 7, last_face[v, x, pl.ds(y, 1), :], pltpu.roll(flux[v], 7, 0))
                change[v, x, y] += after - flux[v]
        return 0

    pl.semaphore_wait(barrier, ng + nf - 2)

    def send(axis, source, target, every, sems):
        begin, end, partner, pos = ways[axis]

        def body(k, _):
            to = partner(k)
            pltpu.make_async_remote_copy(
                source(to), target(pos), sems.at[0], sems.at[1], device_id={axis: to},
                device_id_type=pl.DeviceIdType.MESH,
            ).start()
            return 0

        lax.fori_loop(begin, end, body, 0, unroll=True)

    def whole(axis, source, target, every, sems):
        return pltpu.make_async_remote_copy(
            every, every, sems.at[0], sems.at[1], device_id={axis: ways[axis][2](1)},
            device_id_type=pl.DeviceIdType.MESH,
        )

    def receive(*exchange):
        whole(*exchange).wait_recv()

    def sent(*exchange):
        whole(*exchange).wait_send()

    slice1 = lambda d: s1.at[:, pl.ds(pl.multiple_of(d * kz, kz), kz), :]
    ex1 = ("grp", slice1, lambda d: r1.at[d], r1.at[pl.ds(0, ng - 1)], x1)
    send(*ex1)
    r1[g] = s1[:, pl.ds(pl.multiple_of(g * kz, kz), kz), :]

    loads["pair"].wait()
    ca, cb = pair[0], pair[1]
    ca2, cb2 = ca * ca, cb * cb

    def coefficients(i, m):
        m0 = 1.0 / (1.0 - ca2 * m)
        mults[2 * i] = m0
        m1 = 1.0 / (1.0 - cb2 * m0)
        mults[2 * i + 1] = m1
        return m1

    lax.fori_loop(0, nf, coefficients, jnp.zeros((8, 128), F32))
    loads["fluid"].wait()
    lax.fori_loop(0, 12, make_cells, 0)
    most = jnp.full((1, 128), top_speed(), F32)
    loads["wide"].wait()
    loads["sx"].wait()
    loads["edge"].wait()
    loads["inv"].wait()
    receive(*ex1)

    main = jnp.concatenate([r1[d].reshape(2 * kz, 128) for d in range(ng)], axis=1)
    main = dot_right(main, wide[0], wide[1])
    across = r1[...].reshape(ng * 2 * kz, 128).T
    edge_x = across[cy : cy + cx]
    edge_k = jnp.dot(sx[...], edge_x, precision=lax.Precision.HIGHEST, preferred_element_type=F32)
    wide_lane = ng * 2 * kz
    diag = (
        lax.rem(lax.broadcasted_iota(jnp.int32, (kz, wide_lane), 1), kz)
        == lax.broadcasted_iota(jnp.int32, (kz, wide_lane), 0)
    )
    zero = jnp.zeros((kz, wide_lane), F32)
    sums = [jnp.zeros((kz, ny), F32), jnp.zeros((kz, ny), F32)]
    first_row = [float(v) for v in sine(cx)[0]]
    group = cx // 2
    for x0 in range(0, cx, group):
        lhs = jnp.concatenate(
            [jnp.where(diag, jnp.broadcast_to(edge_k[x : x + 1], (kz, wide_lane)), zero) for x in range(x0, x0 + group)],
            axis=0,
        )
        out = dot_right(lhs, edge[0], edge[1])
        for x in range(x0, x0 + group):
            hd = out[(x - x0) * kz : (x - x0 + 1) * kz] * inv[x]
            hfield[x] = hd
            sums[x % 2] = sums[x % 2] + first_row[x] * hd
    rows = (main[:kz] + (sums[0] + sums[1]), main[kz:] + (sums[0] - sums[1]))
    for row in range(2):
        for j in range(6):
            s2[pl.ds((j // 3) * 8 + row * 3 + j % 3, kz, stride=16), :] = rows[row][:, j * 128 : (j + 1) * 128]
    for r in (6, 7):
        s2[pl.ds(r, nf, stride=8), :] = jnp.broadcast_to(most, (nf, 128))

    most_rows = lambda ref: ref.at[pl.ds(0, (nf - 1) * 8), :]
    tile = lambda ref: lambda d: ref.at[pl.ds(pl.multiple_of(d * 8, 8), 8), :]
    ex2 = ("fft", tile(s2), tile(r2), most_rows(r2), x2)
    send(*ex2)
    mine = pl.ds(pl.multiple_of(f * 8, 8), 8)
    r2[mine, :] = s2[mine, :]
    lax.fori_loop(0, 8, lines_x, 0)
    lax.fori_loop(0, 8, lines_y, 0)
    receive(*ex2)
    most = jnp.max(r2[pl.ds(6, nf, stride=8), :], axis=0, keepdims=True)

    last = jnp.zeros((8, 128), F32)
    prev = last
    for d in range(nf):
        msg = r2[8 * d : 8 * d + 8, :]
        other = pltpu.roll(msg, 5, 0)
        m0, m1 = mults[2 * d], mults[2 * d + 1]
        prev = m0 * (msg - cb * other) + (m0 * ca) * prev
        chain[2 * d] = prev
        prev = m1 * (other - cb * msg) + (m1 * cb) * prev
        chain[2 * d + 1] = prev
    chain[2 * nf - 1] = prev
    for j in range(2 * nf - 2, -1, -1):
        prev = chain[j] + (mults[j] * (cb if j % 2 == 0 else ca)) * prev
        chain[j] = prev
    for d in range(nf):
        left = chain[2 * d - 1] if d > 0 else last
        right = chain[2 * d + 2] if d < nf - 1 else last
        s3[8 * d : 8 * d + 8, :] = jnp.where(sub < 3, left, pltpu.roll(right, 3, 0))

    ex3 = ("fft", tile(s3), tile(r3), most_rows(r3), x3)
    send(*ex3)
    r3[mine, :] = s3[mine, :]
    loads["edget"].wait()
    loads["back"].wait()
    lax.fori_loop(0, 8, last_faces, 0)
    lax.fori_loop(0, 8, lines_z, 0)
    receive(*ex3)
    around = [
        jnp.concatenate(
            [r3[pl.ds((j // 3) * 8 + row * 3 + j % 3, kz, stride=16), :] for j in range(6)], axis=1
        )
        for row in range(2)
    ]
    out_rows = dot_right(jnp.concatenate(around, axis=0), back[0], back[1])
    mixed = (around[0] + around[1], around[0] - around[1])
    corr = []
    for x0 in range(0, cx, group):
        lhs = jnp.concatenate(
            [hfield[x] + (first_row[x] * inv[x]) * mixed[x % 2] for x in range(x0, x0 + group)], axis=0
        )
        out = dot_right(lhs, edget[0], edget[1])
        for x in range(group):
            corr.append(jnp.sum(jnp.where(diag, out[x * kz : (x + 1) * kz], zero), axis=0, keepdims=True))
    corr = jnp.concatenate(corr, axis=0)
    corr = jnp.dot(sx[...], corr, precision=lax.Precision.HIGHEST, preferred_element_type=F32)
    blank = jnp.zeros((cx, kz), F32)
    from_left = jnp.concatenate([blank, edge_x[:, :-kz]], axis=1)
    from_right = jnp.concatenate([edge_x[:, kz:], blank], axis=1)
    second = lax.rem(lax.broadcasted_iota(jnp.int32, (cx, wide_lane), 1) // kz, 2) == 1
    sides = corr + jnp.where(second, from_right, from_left)
    sides = jnp.concatenate(
        [jnp.zeros((cy, wide_lane), F32), sides, jnp.zeros((128 - cy - cx, wide_lane), F32)], axis=0
    ).T
    sides = jnp.where(
        lax.broadcasted_iota(jnp.int32, (wide_lane, 128), 1) == 127, jnp.broadcast_to(most, (wide_lane, 128)), sides
    )
    for d in range(ng):
        s4[d] = (out_rows[:, 128 * d : 128 * d + 128] + sides[2 * kz * d : 2 * kz * (d + 1)]).reshape(2, kz, 128)

    ex4 = ("grp", lambda d: s4.at[d], lambda d: r4.at[:, d], r4.at[:, pl.ds(0, ng - 1)], x4)
    send(*ex4)
    r4[:, g] = s4[g]
    sent(*ex1)
    sent(*ex2)
    sent(*ex3)
    receive(*ex4)
    for e in range(2):
        solved[e] = r4[e].reshape(nz, 128).T
    most_out[...] = jnp.full((8, 128), jnp.max(solved[0, pl.ds(127, 1), :]), F32)

    def second_solve(i, _):
        def fetch(x, at):
            va = solved[0, pl.ds(cy + x, 1), :]
            vb = solved[1, pl.ds(cy + x, 1), :]
            w = jnp.where(even, va + vb, va - vb)
            value = block[x, at, :] - column[at, :] * jnp.concatenate([w, w], axis=0)
            if x == 0:
                value = value - solved[0, at, :]
            if x == cx - 1:
                value = value - solved[1, at, :]
            return value

        at, values = solve(fetch, i)
        for x in range(cx):
            block[x, at, :] = values[x]
        return 0

    lax.fori_loop(0, cy // 16, second_solve, 0)

    def inverse_z(rows):
        a, b = split(rows)
        both = mm(jnp.concatenate([a, b], axis=1), sz[...])
        return both[:, :nz] + both[:, nz:]

    def backward(i, _):
        pair_x = jnp.concatenate([block[2 * i], block[2 * i + 1]], axis=1)
        out = dot_left(sy[...], pair_x)
        out = inverse_z(jnp.concatenate([out[:, :nz], out[:, nz:]], axis=0))
        grid[2 * i + 1, pl.ds(8, cy), :] = out[:cy]
        grid[2 * i + 2, pl.ds(8, cy), :] = out[cy:]
        return 0

    lax.fori_loop(0, half, backward, 0, unroll=True)
    copy_out = pltpu.make_async_copy(grid.at[pl.ds(1, cx), pl.ds(8, cy), :], pot_h, osem)
    copy_out.start()
    pair_x = jnp.concatenate([solved[0, :cy], solved[1, :cy]], axis=1)
    out = dot_left(sy[...], pair_x)
    rest = jnp.concatenate([out[:, :nz], out[:, nz:], solved[0, cy:], solved[1, cy:]], axis=0)
    rest = inverse_z(rest)
    grid[0, pl.ds(8, cy), :] = rest[:cy]
    grid[cx + 1, pl.ds(8, cy), :] = rest[cy : 2 * cy]
    pad = 128 - cy
    for e in range(2):
        lines = rest[2 * cy + pad * e : 2 * cy + pad * (e + 1)]
        at = pl.ds(7 if e == 0 else 8 + cy, 1)
        for x in range(cx):
            grid[x + 1, at, :] = lines[x : x + 1]
    for e in range(2):
        lines = rest[2 * cy + pad * e : 2 * cy + pad * (e + 1)]
        for s in range(2):
            grid[(cx + 1) * e, pl.ds(7 if s == 0 else 8 + cy, 1), :] = lines[cx + s : cx + s + 1]

    loads["fold"].wait()
    per_y, per_z = cy // 4, nz // 4
    lanes8 = lax.broadcasted_iota(jnp.int32, (8, 128), 1)
    pick = (
        lax.broadcasted_iota(jnp.int32, (16, 128), 1) // 8 == lax.broadcasted_iota(jnp.int32, (16, 128), 0)
    )
    lane6 = lax.rem(lax.broadcasted_iota(jnp.int32, (6, 128), 1), 8)
    row6 = lax.broadcasted_iota(jnp.int32, (6, 128), 0)
    some = 4

    def gather(i, _):
        cut, odd = [], []
        for c in range(2 * some):
            code = jnp.maximum(ghost[0, 2 * some * i + c], 0)
            ix = code // (per_y * per_z)
            iy = lax.rem(code // per_z, per_y)
            iz = lax.rem(code, per_z)
            rows = grid[pl.ds(4 * ix, 6), pl.ds(7 + 4 * iy, 8), :]
            inside = (lanes8 >= 4 * iz - 1) & (lanes8 <= 4 * iz + 4) & (sub < 6)
            cut.append(jnp.where(inside[None], rows, 0.0).reshape(48, 128))
            odd.append(lax.rem(iz, 2))
        a, b = split(jnp.concatenate(cut, axis=0))
        out = mm(jnp.concatenate([a, b], axis=1), fold[...]).reshape(2 * some * 3, 16, 128)
        out = jnp.sum(jnp.where(pick[None], out, 0.0), axis=1)
        for k in range(some):
            d = some * i + k
            mini = out[6 * k : 6 * k + 6]
            turned = jnp.where(lane6 < 4, pltpu.roll(mini, 124, 1), pltpu.roll(mini, 4, 1))
            which = jnp.where(row6 < 3, odd[2 * k], odd[2 * k + 1])
            mini = jnp.where(which == 1, turned, mini)
            slots = [
                jnp.full((1, 128), ghost[1, 2 * d + c].astype(F32), F32) for c in range(2)
            ]
            s6[pl.ds(pl.multiple_of(8 * d, 8), 8), :] = jnp.concatenate([mini] + slots, axis=0)
        return 0

    lax.fori_loop(0, nf // some, gather, 0, unroll=2)

    ex6 = ("fft", tile(s6), tile(r6), most_rows(r6), x6)
    send(*ex6)
    r6[mine, :] = s6[mine, :]
    width = fluid.shape[-1]
    groups = 128 // width
    rate = COURANT / most_out[pl.ds(0, 1), pl.ds(0, width)]

    def pack(y, _):
        for r in range(2):
            at = [2 * i + r for i in range(groups)]
            cons = [[fluid[v, x + 2, y + 2, cells, :] for x in at] for v in range(5)]
            for v in range(4):
                packed[v, r, y] = jnp.concatenate(cons[v], axis=1)
            for v in range(5):
                packed[4 + v, r, y] = jnp.concatenate(
                    [c - rate * change[v, x, y] for c, x in zip(cons[v], at)], axis=1
                )
        return 0

    lax.fori_loop(0, 8, pack, 0)
    copy_packed = pltpu.make_async_copy(packed, packed_h, psem)
    copy_packed.start()
    sent(*ex4)
    copy_out.wait()
    copy_packed.wait()
    receive(*ex6)
    blocks[...] = r6[...]
    sent(*ex6)


def patch_kernel(
    blocks, most, packed_h, pot_in, weave,
    fine_h, moved_h, pot_out,
    fine, moved, packed, hold, sems,
):
    count = fine.shape[-1]
    nf = blocks.shape[0] // 8
    copy_in = pltpu.make_async_copy(pot_in, hold, sems.at[0])
    needs = [
        pltpu.make_async_copy(packed_h.at[0], packed.at[0], sems.at[8]),
        pltpu.make_async_copy(packed_h.at[pl.ds(1, 8)], packed.at[pl.ds(1, 8)], sems.at[9]),
    ]
    needs[0].start()
    copy_in.start()
    needs[1].start()
    copy_out = pltpu.make_async_copy(hold, pot_out, sems.at[1])
    groups = 128 // count

    lanes = lax.rem(lax.broadcasted_iota(jnp.int32, (nf, 128), 1), count)
    hot = jnp.concatenate(
        [
            jnp.where(blocks[pl.ds(6 + c, nf, stride=8), :] == lanes.astype(F32), 1.0, 0.0)
            for c in range(2)
        ],
        axis=0,
    ).astype(BF16)
    within, outside = [], []
    for t in range(3):
        came = jnp.concatenate([blocks[pl.ds(c * 3 + t, nf, stride=8), :] for c in range(2)], axis=0)
        a, b = split(came.T)
        placed = mm(a, hot) + mm(b, hot)
        a, b = split(placed)
        woven = mm(weave[...], a) + mm(weave[...], b)
        woven = woven.reshape(2, 2, 8, 8, 128)
        within += [woven[0, 0], woven[0, 1]]
        outside += [woven[1, 0], woven[1, 1]]

    z = lax.broadcasted_iota(jnp.int32, (8, 128), 0)
    q = lax.broadcasted_iota(jnp.int32, (8, 128), 1) // count
    bottom, top, zeven = z == 0, z == 7, lax.rem(z, 2) == 0
    zodd = jnp.logical_not(zeven)
    first, final = q == 0, q == 3

    def choose(values, shift, y):
        out = values[shift + 3][y]
        for i in (2, 1, 0):
            out = jnp.where(q == i, values[shift + i][y], out)
        return out

    def along_x(values, r, y):
        if r == 0:
            return 0.25 * choose(values, 0, y) + 0.75 * choose(values, 1, y)
        return 0.75 * choose(values, 1, y) + 0.25 * choose(values, 2, y)

    def between(values, j):
        low = j // 2
        return (
            0.75 * values[low] + 0.25 * values[low + 1]
            if j % 2 == 0
            else 0.25 * values[low] + 0.75 * values[low + 1]
        )

    scale = 1.0 / (6.0 + SCREEN * FINE_STEP * FINE_STEP)
    layers, rims, states, force = {}, {}, {}, {}
    for r in range(2):
        plane = [along_x(within, r, y) for y in range(6)]
        for jy in range(10):
            value = between(plane, jy)
            if 1 <= jy <= 8:
                states[r, jy - 1] = value
            else:
                rims[r, jy] = value
        plane = [along_x(outside, r, y) for y in range(6)]
        for jy in range(1, 9):
            layers[r, jy - 1] = between(plane, jy)
    ends = (
        [0.75 * within[0][y] + 0.25 * within[1][y] for y in range(6)],
        [0.25 * within[4][y] + 0.75 * within[5][y] for y in range(6)],
    )
    keys = [(r, y) for r in range(2) for y in range(8)]
    sides = {
        (r, y): jnp.where(first if r == 0 else final, between(ends[r], y + 1), 0.0) for r, y in keys
    }
    needs[0].wait()
    for r, y in keys:
        ghost = layers[r, y] + sides[r, y]
        if y == 0:
            ghost = ghost + rims[r, 0]
        if y == 7:
            ghost = ghost + rims[r, 9]
        force[r, y] = (OMEGA * scale) * (ghost - FINE_STEP * FINE_STEP * packed[0, r, y])

    copy_in.wait()
    copy_out.start()

    def beside(old, r, y):
        other = old[1 - r, y]
        if r == 0:
            return other, jnp.where(first, 0.0, pltpu.roll(other, count, 1))
        return other, jnp.where(final, 0.0, pltpu.roll(other, 128 - count, 1))

    def sweep(_, carry):
        old = dict(zip(keys, carry))
        for colour in (0, 1):
            new = {}
            for r, y in keys:
                v = old[r, y]
                other, far = beside(old, r, y)
                near = (other + far) + (
                    jnp.where(bottom, 0.0, pltpu.roll(v, 1, 0)) + jnp.where(top, 0.0, pltpu.roll(v, 7, 0))
                )
                if y > 0:
                    near = near + old[r, y - 1]
                if y < 7:
                    near = near + old[r, y + 1]
                value = (1.0 - OMEGA) * v + ((OMEGA * scale) * near + force[r, y])
                mask = zeven if (r + y + colour) % 2 == 0 else zodd
                new[r, y] = jnp.where(mask, value, v)
            old = new
        return tuple(old[k] for k in keys)

    out = lax.fori_loop(0, SWEEPS, sweep, tuple(states[k] for k in keys))
    states = dict(zip(keys, out))

    def spill(target, r, y, value):
        for i in range(groups):
            target[2 * i + r, y] = value[:, count * i : count * (i + 1)]

    copies = [pltpu.make_async_copy(fine, fine_h, sems.at[2])] + [
        pltpu.make_async_copy(moved.at[v], moved_h.at[v], sems.at[3 + v]) for v in range(5)
    ]
    for r, y in keys:
        spill(fine, r, y, states[r, y])
    copies[0].start()

    needs[1].wait()
    for r, y in keys:
        spill(moved.at[0], r, y, packed[4, r, y])
    copies[1].start()
    step = COURANT * FINE_STEP / most[pl.ds(0, 1), :]
    work = {}
    for n in range(3):
        for r, y in keys:
            v = states[r, y]
            if n == 0:
                other, far = beside(states, r, y)
                far = far + sides[r, y]
                pull = far - other if r == 0 else other - far
            elif n == 1:
                down = states[r, y - 1] if y > 0 else rims[r, 0]
                up = states[r, y + 1] if y < 7 else rims[r, 9]
                pull = down - up
            else:
                layer = layers[r, y]
                pull = jnp.where(bottom, layer, pltpu.roll(v, 1, 0)) - jnp.where(top, layer, pltpu.roll(v, 7, 0))
            spill(moved.at[1 + n], r, y, packed[5 + n, r, y] + step * packed[0, r, y] * pull)
            part = packed[1 + n, r, y] * pull
            work[r, y] = part if n == 0 else work[r, y] + part
        copies[2 + n].start()
    for r, y in keys:
        spill(moved.at[4], r, y, packed[8, r, y] + step * work[r, y])
    copies[5].start()
    for c in copies:
        c.wait()
    copy_out.wait()


def root_call(ghost, rho, fluid, nf, ng):
    cx, cy, nz = rho.shape
    kz = nz // ng
    ny = ng * cy
    count = fluid.shape[-1]
    tab = tables(nf, ng, cx, cy, nz)
    consts = [jnp.asarray(tab[n]) for n in NAMES]
    vm = lambda shape, dtype=F32: pltpu.VMEM(shape, dtype)
    anyspace = pl.BlockSpec(memory_space=pl.ANY)
    vspace = pl.BlockSpec(memory_space=pltpu.VMEM)
    dma = pltpu.SemaphoreType.DMA
    local = {n: tab[n].shape for n in NAMES}
    local["inv"] = local["inv"][1:]
    local["pair"] = local["pair"][2:]
    limit = 56 * 1024 * 1024
    potential, blocks, most, packed = pl.pallas_call(
        functools.partial(root_kernel, (nf, ng, cx, cy, nz)),
        out_shape=(
            jax.ShapeDtypeStruct((cx, cy, nz), F32),
            jax.ShapeDtypeStruct((nf * 8, 128), F32),
            jax.ShapeDtypeStruct((8, 128), F32),
            jax.ShapeDtypeStruct((9, 2, 8, 8, 128), F32),
        ),
        in_specs=[pl.BlockSpec(memory_space=pltpu.SMEM)] + [anyspace] * (2 + len(NAMES)),
        out_specs=(anyspace, vspace, vspace, anyspace),
        scratch_shapes=[vm((cx, cy, nz))]
        + [vm(local[n], consts[i].dtype) for i, n in enumerate(NAMES)]
        + [
            vm(fluid.shape), vm((5, 12, 12, 8, count)),
            vm((cx, cy, nz)),
            vm((2, 128, nz)),
            vm((cx, 8, nz)),
            vm((cx + 2, cy + 16, nz)),
            vm((cx, kz, ny)),
            vm((2, nz, 128)), vm((ng, 2, kz, 128)),
            vm((nf * 8, 128)), vm((nf * 8, 128)),
            vm((nf * 8, 128)), vm((nf * 8, 128)),
            vm((ng, 2, kz, 128)), vm((2, ng, kz, 128)),
            vm((nf * 8, 128)), vm((nf * 8, 128)),
            vm((2 * nf, 8, 128)), vm((2 * nf, 8, 128)),
            vm((5, 8, 8, count)),
            vm((5, 8, 8, 8, count)), vm((9, 2, 8, 8, 128)),
            dma((17,)), dma, dma,
            dma((2,)), dma((2,)), dma((2,)), dma((2,)), dma((2,)),
        ],
        compiler_params=pltpu.CompilerParams(
            collective_id=0, has_side_effects=True, vmem_limit_bytes=limit
        ),
    )(ghost, rho, fluid, *consts)
    fine, moved, potential = pl.pallas_call(
        patch_kernel,
        out_shape=(
            jax.ShapeDtypeStruct((8, 8, 8, count), F32),
            jax.ShapeDtypeStruct((5, 8, 8, 8, count), F32),
            jax.ShapeDtypeStruct((cx, cy, nz), F32),
        ),
        in_specs=[vspace, vspace, anyspace, anyspace, vspace],
        out_specs=(anyspace, anyspace, anyspace),
        scratch_shapes=[
            vm((8, 8, 8, count)), vm((5, 8, 8, 8, count)), vm((9, 2, 8, 8, 128)), vm((cx, cy, nz)), dma((10,)),
        ],
        compiler_params=pltpu.CompilerParams(vmem_limit_bytes=limit),
    )(blocks, most, packed, potential, jnp.asarray(tab["weave"]))
    return potential, fine, moved


def per_device(root_density, patch_fluid, ghost_list):
    nf = lax.axis_size("fft")
    ng = lax.axis_size("grp")
    return root_call(ghost_list[:, 0], root_density, patch_fluid, nf, ng)


def solution(mesh):
    return jax.shard_map(
        per_device,
        mesh=mesh,
        in_specs=(
            P("fft", "grp", None),
            P(None, None, None, None, ("fft", "grp")),
            P(None, ("fft", "grp"), None),
        ),
        out_specs=(
            P("fft", "grp", None),
            P(None, None, None, ("fft", "grp")),
            P(None, None, None, None, ("fft", "grp")),
        ),
        check_vma=False,
    )
```

```python
import functools

import jax
import jax.numpy as jnp
import ml_dtypes
import numpy as np
from jax import lax
from jax.experimental import pallas as pl
from jax.experimental.pallas import tpu as pltpu
from jax.sharding import PartitionSpec as P

SWEEPS = 8
GAMMA = 5.0 / 3.0
SCREEN = 0.0006
OMEGA = 1.5
COURANT = 0.4
FINE_STEP = 0.5
F32 = jnp.float32
BF16 = jnp.bfloat16


def sine(count):
    index = np.arange(1, count + 1)
    return np.sqrt(2.0 / (count + 1)) * np.sin(
        np.pi * (np.outer(index, index) % (2 * (count + 1))) / (count + 1)
    )


def eigen(count):
    return 4.0 * np.sin(np.pi * np.arange(1, count + 1) / (2 * (count + 1))) ** 2


def halves(table):
    high = table.astype(ml_dtypes.bfloat16)
    low = (table - high.astype(np.float64)).astype(ml_dtypes.bfloat16)
    return np.stack([high, low])


@functools.lru_cache(None)
def tables(nf, ng, cx, cy, nz):
    ny = ng * cy
    kz = nz // ng
    sz, sy, sx, full = sine(nz), sine(cy), sine(cx), sine(ny)
    lam = eigen(cy)[:, None] + eigen(nz)[None, :] + SCREEN
    steps = [1.0 / (2.0 + lam)]
    for _ in range(1, cx // 2):
        steps.append(1.0 / (2.0 + lam - steps[-1]))
    steps.append(1.0 / (1.0 - steps[-1] ** 2))
    edge = np.zeros((ng, 2, ny))
    wide = np.zeros((ng, 128, ny))
    back = np.zeros((ng, 128, ny))
    for d in range(ng):
        if d > 0:
            edge[d, 0] = full[d * cy - 1]
        if d < ng - 1:
            edge[d, 1] = full[(d + 1) * cy]
        wide[d, :cy] = sy @ full[d * cy : (d + 1) * cy]
        back[d, :cy] = wide[d, :cy]
        back[d, cy + cx] = edge[d, 0]
        back[d, cy + cx + 1] = edge[d, 1]
    repeated = np.repeat(edge.reshape(2 * ng, ny), kz, axis=0)
    denom = (
        eigen(cx)[None, :, None, None]
        + eigen(nz).reshape(ng, 1, kz, 1)
        + eigen(ny)[None, None, None, :]
        + SCREEN
    )
    phi = 2.0 * np.arcsinh(np.sqrt(eigen(ny)[None, :] + eigen(nz)[:, None] + SCREEN) / 2.0)

    def ratio(m, n):
        return np.exp(-(n - m) * phi) * np.expm1(-2 * m * phi) / np.expm1(-2 * n * phi)

    pair = np.zeros((ng, nf, 2, 8, 128))
    for i, values in enumerate((ratio(cx - 1, cx), ratio(1, cx))):
        pair[:, :, i, :3] = values.reshape(ng, nf, 3, 128)
    spread = np.zeros((10, 6))
    for j in range(10):
        at = j / 2 + 0.25
        low = int(np.floor(at))
        spread[j, low] += 1 - (at - low)
        spread[j, low + 1] += at - low
    inner = np.zeros((8, 8))
    inner[:, :6] = spread[1:9]
    outer = np.zeros((8, 8))
    outer[0, :6] = spread[0]
    outer[7, :6] = spread[9]
    weave = np.concatenate([np.kron(np.eye(16), inner), np.kron(np.eye(16), outer)])
    lanes = np.arange(128)
    fold = ((lanes[:, None] + 1) % 8 == lanes[None, :] % 8).astype(np.float64)
    column = np.broadcast_to(sy[0][:, None], (cy, 128))
    as32 = lambda t: np.ascontiguousarray(t, dtype=np.float32)
    szh, szl = halves(sz)
    syh, syl = halves(sy)
    wide_x = np.zeros((cx, 32))
    wide_x[:, :cx] = sx
    xh, xl = halves(np.repeat(wide_x, kz, axis=0))
    sx_rows = np.block([[xh, xh], [xl, np.zeros_like(xl)]]).astype(ml_dtypes.bfloat16)
    tall_x = np.zeros((32, cx * kz))
    tall_x[:cx] = np.repeat(sx, kz, axis=1)
    sx_sums = np.concatenate(halves(tall_x))
    return dict(
        sz=np.block([[szh, szl], [szh, np.zeros_like(szh)]]).astype(ml_dtypes.bfloat16),
        sy=np.block([[syh, syh], [syl, np.zeros_like(syl)]]).astype(ml_dtypes.bfloat16),
        sx=sx_rows,
        sxt=sx_sums,
        steps=as32(np.stack(steps)),
        wide=halves(wide.reshape(ng * 128, ny)),
        back=halves(np.ascontiguousarray(back.reshape(ng * 128, ny).T)),
        edge=halves(repeated),
        edget=halves(np.ascontiguousarray(repeated.T)),
        inv=as32(1.0 / denom),
        pair=as32(pair),
        weave=weave.astype(ml_dtypes.bfloat16),
        fold=np.concatenate([fold, fold]).astype(ml_dtypes.bfloat16),
        column=as32(column),
    )


NAMES = (
    "sz", "sy", "sx", "sxt", "steps", "wide", "back", "edge", "edget", "inv", "pair", "fold", "column",
)


def split(value):
    high = value.astype(BF16)
    return high, (value - high.astype(F32)).astype(BF16)


def mm(a, b):
    return jnp.dot(a, b, preferred_element_type=F32)


def dot_right(value, high, low):
    rows = value.shape[0]
    a, b = split(value)
    main = mm(jnp.concatenate([a, b], axis=0), high)
    return main[:rows] + (main[rows:] + mm(a, low))


def dot_left(both, value):
    rows = both.shape[0] // 2
    a, b = split(value)
    out = mm(both, jnp.concatenate([a, b], axis=0))
    return out[:rows] + out[rows:]


def root_kernel(
    cfg,
    ghost, rho, fluid_h,
    sz_h, sy_h, sx_h, sxt_h, steps_h, wide_h, back_h, edge_h, edget_h, inv_h, pair_h, fold_h, column_h,
    pot_h, blocks, most_out, packed_h,
    src, sz, sy, sx, sxt, steps, wide, back, edge, edget, inv, pair, fold, column, fluid, prim,
    block, solved, part, grid, hfield,
    s1, r1, s2, r2, s3, r3, s4, r4, s6, r6, chain, mults, last_face, change, packed,
    tsem, osem, psem, x1, x2, x3, x4, x6,
):
    nf, ng, cx, cy, nz = cfg
    kz = nz // ng
    ny = ng * cy
    half = cx // 2
    f = lax.axis_index("fft")
    g = lax.axis_index("grp")

    quarter = cx // 4
    early = [
        (f"rho{i}", rho.at[pl.ds(quarter * i, quarter)], src.at[pl.ds(quarter * i, quarter)]) for i in range(4)
    ]
    early[1:1] = [("sz", sz_h, sz), ("sy", sy_h, sy)]
    early += [("steps", steps_h, steps), ("column", column_h, column), ("pair", pair_h.at[g, f], pair)]
    late = [
        ("wide", wide_h, wide), ("sx", sx_h, sx), ("edge", edge_h, edge), ("inv", inv_h.at[g], inv),
        ("fluid", fluid_h, fluid), ("edget", edget_h, edget), ("sxt", sxt_h, sxt), ("back", back_h, back), ("fold", fold_h, fold),
    ]
    loads = {
        name: pltpu.make_async_copy(a, b, tsem.at[i]) for i, (name, a, b) in enumerate(early + late)
    }
    for name, _, _ in early:
        loads[name].start()

    ny_chips = 4 if nf % 4 == 0 else 1
    nz_chips = nf // ny_chips
    barrier = pltpu.get_barrier_semaphore()

    def grp_partner(k):
        return lax.rem(g + k, ng)

    def fft_partner(k):
        a, b = k // ny_chips, lax.rem(k, ny_chips)
        dz = nz_chips // 2 + ((a + 1) // 2) * (1 - 2 * lax.rem(a, 2))
        dy = ny_chips // 2 + ((b + 1) // 2) * (1 - 2 * lax.rem(b, 2))
        return lax.rem(f // ny_chips + dz, nz_chips) * ny_chips + lax.rem(lax.rem(f, ny_chips) + dy, ny_chips)

    ways = {"grp": (1, ng, grp_partner, g), "fft": (0, nf - 1, fft_partner, f)}

    def hello(axis):
        begin, end, partner, _ = ways[axis]

        def body(k, _):
            pl.semaphore_signal(
                barrier, inc=1, device_id={axis: partner(k)}, device_id_type=pl.DeviceIdType.MESH
            )
            return 0

        lax.fori_loop(begin, end, body, 0, unroll=True)

    hello("fft")
    hello("grp")

    sub = lax.broadcasted_iota(jnp.int32, (8, 128), 0)
    even = lax.rem(sub, 2) == 0

    loads["sz"].wait()
    loads["sy"].wait()

    def forward(i, _):
        rows = src[pl.ds(2 * i, 2)].reshape(2 * cy, nz)
        a, b = split(rows)
        both = mm(jnp.concatenate([a, b], axis=1), sz[...])
        both = both[:, :nz] + both[:, nz:]
        pair_x = jnp.concatenate([both[:cy], both[cy:]], axis=1)
        out = dot_left(sy[...], pair_x)
        block[2 * i] = out[:, :nz]
        block[2 * i + 1] = out[:, nz:]
        return 0

    for part_of in range(4):
        loads[f"rho{part_of}"].wait()
        if part_of == 3:
            for name, _, _ in late:
                loads[name].start()
        lax.fori_loop(part_of * half // 4, (part_of + 1) * half // 4, forward, 0, unroll=True)

    loads["steps"].wait()
    loads["column"].wait()

    def solve(fetch, i):
        at = pl.ds(pl.multiple_of(16 * i, 16), 16)
        low, high = [], []
        for j in range(half):
            m = steps[j, at, :]
            a, b = fetch(j, at), fetch(cx - 1 - j, at)
            if j == 0:
                low.append(-m * a)
                high.append(-m * b)
            else:
                low.append(m * (low[-1] - a))
                high.append(m * (high[-1] - b))
        m, scale = steps[half - 1, at, :], steps[half, at, :]
        a, b = low[-1], high[-1]
        low[-1] = (a + m * b) * scale
        high[-1] = (b + m * a) * scale
        for j in range(half - 2, -1, -1):
            m = steps[j, at, :]
            low[j] = low[j] + m * low[j + 1]
            high[j] = high[j] + m * high[j + 1]
        return at, low + high[::-1]

    part[...] = jnp.zeros_like(part)

    def first(i, _):
        at, values = solve(lambda x, at: block[x, at, :], i)
        col = column[at, :]
        for x in range(cx):
            v = values[x] * col
            part[x] += v[:8] + v[8:]
        solved[0, at, :] = values[0]
        solved[1, at, :] = values[cx - 1]
        return 0

    lax.fori_loop(0, cy // 16, first, 0, unroll=2)
    sums = part[...]
    sign = jnp.where(even, 1.0, -1.0)
    edges = (jnp.sum(sums, axis=1), jnp.sum(sums * sign[None], axis=1))
    for e in range(2):
        solved[e, pl.ds(cy, cx), :] = edges[e]
        solved[e, pl.ds(cy + cx, 8), :] = jnp.zeros((8, 128), F32)
        s1[e] = solved[e].T


    cells = pl.ds(2, 8)

    def cell_values(cons):
        dens = cons[0]
        over = 1.0 / dens
        vel = [m * over for m in cons[1:4]]
        kinetic = 0.5 * (cons[1] * vel[0] + cons[2] * vel[1] + cons[3] * vel[2])
        return [dens] + vel + [(GAMMA - 1.0) * (cons[4] - kinetic)]

    def sound(dens, pres):
        return jnp.sqrt(GAMMA * pres) * lax.rsqrt(dens)

    def make_cells(x, _):
        for y in range(12):
            w = cell_values([fluid[v, x, y, cells, :] for v in range(5)])
            for v in range(5):
                prim[v, x, y] = w[v]
        return 0

    def top_speed():
        def body(x, top):
            for y in range(2, 10):
                w = [prim[v, x + 2, y] for v in range(5)]
                fast = jnp.maximum(jnp.maximum(jnp.abs(w[1]), jnp.abs(w[2])), jnp.abs(w[3]))
                top = jnp.maximum(top, fast + sound(w[0], w[4]))
            return top
        return jnp.max(lax.fori_loop(0, 8, body, jnp.zeros((8, fluid.shape[-1]), F32)))

    def states(before, here, after):
        low, high = [], []
        for a, b, c in zip(before, here, after):
            p, q = b - a, c - b
            half_slope = 0.5 * (
                jnp.maximum(0.0, jnp.minimum(p, q)) + jnp.minimum(0.0, jnp.maximum(p, q))
            )
            low.append(b - half_slope)
            high.append(b + half_slope)
        return low, high

    def side(w, n):
        dens, vel, pres = w[0], w[1:4], w[4]
        energy = pres * (1.0 / (GAMMA - 1.0)) + 0.5 * dens * (
            vel[0] * vel[0] + vel[1] * vel[1] + vel[2] * vel[2]
        )
        mom = [dens * v for v in vel]
        flux = [mom[n]] + [mom[n] * v for v in vel] + [(energy + pres) * vel[n]]
        flux[1 + n] = flux[1 + n] + pres
        return [dens] + mom + [energy], flux, jnp.abs(vel[n]) + sound(dens, pres)

    def face(left, right, n):
        cl, fl, al = side(left, n)
        cr, fr, ar = side(right, n)
        top = jnp.maximum(al, ar)
        return [0.5 * ((a + b) - top * (d - c)) for a, b, c, d in zip(fl, fr, cl, cr)]

    def sweep_line(get, put, n):
        w = [get(0), get(1), get(2)]
        _, high = states(*w)
        flux = None
        for i in range(2, 11):
            w = [w[1], w[2], get(i + 1)]
            low, high_next = states(*w)
            now = face(high, low, n)
            if flux is not None:
                put(i - 3, [b - a for a, b in zip(flux, now)])
            flux, high = now, high_next

    def lines_x(y, _):
        def get(i):
            return [prim[v, i, y + 2] for v in range(5)]

        def put(i, values):
            for v in range(5):
                change[v, i, y] = values[v]

        sweep_line(get, put, 0)
        return 0

    def lines_y(x, _):
        def get(i):
            return [prim[v, x + 2, i] for v in range(5)]

        def put(i, values):
            for v in range(5):
                change[v, x, i] += values[v]

        sweep_line(get, put, 1)
        return 0

    def last_faces(x, _):
        w = [
            cell_values([fluid[v, x + 2, cells, k, :] for v in range(5)]) for k in (8, 9, 10, 11)
        ]
        _, high = states(w[0], w[1], w[2])
        low, _ = states(w[1], w[2], w[3])
        flux = face(high, low, 2)
        for v in range(5):
            last_face[v, x] = flux[v]
        return 0

    def lines_z(x, _):
        row = lax.broadcasted_iota(jnp.int32, (8, fluid.shape[-1]), 0)
        for y in range(8):
            w = [
                cell_values([fluid[v, x + 2, y + 2, pl.ds(k, 8), :] for v in range(5)]) if k != 2
                else [prim[v, x + 2, y + 2] for v in range(5)]
                for k in range(4)
            ]
            _, high = states(w[0], w[1], w[2])
            low, _ = states(w[1], w[2], w[3])
            flux = face(high, low, 2)
            for v in range(5):
                after = jnp.where(row == 7, last_face[v, x, pl.ds(y, 1), :], pltpu.roll(flux[v], 7, 0))
                change[v, x, y] += after - flux[v]
        return 0

    pl.semaphore_wait(barrier, ng + nf - 2)

    def send(axis, source, target, every, sems):
        begin, end, partner, pos = ways[axis]

        def body(k, _):
            to = partner(k)
            pltpu.make_async_remote_copy(
                source(to), target(pos), sems.at[0], sems.at[1], device_id={axis: to},
                device_id_type=pl.DeviceIdType.MESH,
            ).start()
            return 0

        lax.fori_loop(begin, end, body, 0, unroll=True)

    def whole(axis, source, target, every, sems):
        return pltpu.make_async_remote_copy(
            every, every, sems.at[0], sems.at[1], device_id={axis: ways[axis][2](1)},
            device_id_type=pl.DeviceIdType.MESH,
        )

    def receive(*exchange):
        whole(*exchange).wait_recv()

    def sent(*exchange):
        whole(*exchange).wait_send()

    slice1 = lambda d: s1.at[:, pl.ds(pl.multiple_of(d * kz, kz), kz), :]
    ex1 = ("grp", slice1, lambda d: r1.at[d], r1.at[pl.ds(0, ng - 1)], x1)
    send(*ex1)
    r1[g] = s1[:, pl.ds(pl.multiple_of(g * kz, kz), kz), :]

    loads["pair"].wait()
    ca, cb = pair[0], pair[1]
    ca2, cb2 = ca * ca, cb * cb

    def coefficients(i, m):
        m0 = 1.0 / (1.0 - ca2 * m)
        mults[2 * i] = m0
        m1 = 1.0 / (1.0 - cb2 * m0)
        mults[2 * i + 1] = m1
        return m1

    lax.fori_loop(0, nf // 2, coefficients, jnp.zeros((8, 128), F32))
    loads["fluid"].wait()
    lax.fori_loop(0, 12, make_cells, 0)
    most = jnp.full((1, 128), top_speed(), F32)
    loads["wide"].wait()
    loads["sx"].wait()
    loads["edge"].wait()
    loads["inv"].wait()
    receive(*ex1)

    main = jnp.concatenate([r1[d].reshape(2 * kz, 128) for d in range(ng)], axis=1)
    main = dot_right(main, wide[0], wide[1])
    across = r1[...].reshape(ng * 2 * kz, 128).T
    edge_x = across[cy : cy + cx]
    edge_k = dot_left(sx[...], across[cy : cy + 32]).reshape(cx, kz, ng * 2 * kz)
    wide_lane = ng * 2 * kz
    diag = (
        lax.rem(lax.broadcasted_iota(jnp.int32, (kz, wide_lane), 1), kz)
        == lax.broadcasted_iota(jnp.int32, (kz, wide_lane), 0)
    )
    sums = [jnp.zeros((kz, ny), F32), jnp.zeros((kz, ny), F32)]
    first_row = [float(v) for v in sine(cx)[0]]
    group = cx // 2
    for x0 in range(0, cx, group):
        lhs = jnp.where(diag[None], edge_k[x0 : x0 + group], 0.0).reshape(group * kz, wide_lane)
        out = dot_right(lhs, edge[0], edge[1])
        for x in range(x0, x0 + group):
            hd = out[(x - x0) * kz : (x - x0 + 1) * kz] * inv[x]
            hfield[x] = hd
            sums[x % 2] = sums[x % 2] + first_row[x] * hd
    rows = (main[:kz] + (sums[0] + sums[1]), main[kz:] + (sums[0] - sums[1]))
    for row in range(2):
        for j in range(6):
            s2[pl.ds((j // 3) * 8 + row * 3 + j % 3, kz, stride=16), :] = rows[row][:, j * 128 : (j + 1) * 128]
    for r in (6, 7):
        s2[pl.ds(r, nf, stride=8), :] = jnp.broadcast_to(most, (nf, 128))

    most_rows = lambda ref: ref.at[pl.ds(0, (nf - 1) * 8), :]
    tile = lambda ref: lambda d: ref.at[pl.ds(pl.multiple_of(d * 8, 8), 8), :]
    ex2 = ("fft", tile(s2), tile(r2), most_rows(r2), x2)
    send(*ex2)
    mine = pl.ds(pl.multiple_of(f * 8, 8), 8)
    r2[mine, :] = s2[mine, :]
    lax.fori_loop(0, 8, lines_x, 0)
    lax.fori_loop(0, 8, lines_y, 0)
    receive(*ex2)
    most = jnp.max(r2[pl.ds(6, nf, stride=8), :], axis=0, keepdims=True)

    last = jnp.zeros((8, 128), F32)

    def right_sides(d):
        msg = r2[8 * d : 8 * d + 8, :]
        other = pltpu.roll(msg, 5, 0)
        return msg - cb * other, other - cb * msg

    up = down = last
    for d in range(nf // 2):
        m0, m1 = mults[2 * d], mults[2 * d + 1]
        ma, mb = m0 * ca, m1 * cb
        e = nf - 1 - d
        p, q = right_sides(d)
        up = m0 * p + ma * up
        chain[2 * d] = up
        up = m1 * q + mb * up
        chain[2 * d + 1] = up
        p, q = right_sides(e)
        down = m0 * q + ma * down
        chain[2 * e + 1] = down
        down = m1 * p + mb * down
        chain[2 * e] = down
    link = mults[nf - 1] * ca
    over = 1.0 / (1.0 - link * link)
    up, down = (up + link * down) * over, (down + link * up) * over
    chain[nf - 1] = up
    chain[nf] = down
    for j in range(nf - 2, -1, -1):
        m = mults[j] * (cb if j % 2 == 0 else ca)
        up = chain[j] + m * up
        chain[j] = up
        down = chain[2 * nf - 1 - j] + m * down
        chain[2 * nf - 1 - j] = down
    for d in range(nf):
        left = chain[2 * d - 1] if d > 0 else last
        right = chain[2 * d + 2] if d < nf - 1 else last
        s3[8 * d : 8 * d + 8, :] = jnp.where(sub < 3, left, pltpu.roll(right, 3, 0))

    ex3 = ("fft", tile(s3), tile(r3), most_rows(r3), x3)
    send(*ex3)
    r3[mine, :] = s3[mine, :]
    loads["edget"].wait()
    loads["back"].wait()
    lax.fori_loop(0, 8, last_faces, 0)
    lax.fori_loop(0, 8, lines_z, 0)
    receive(*ex3)
    around = [
        jnp.concatenate(
            [r3[pl.ds((j // 3) * 8 + row * 3 + j % 3, kz, stride=16), :] for j in range(6)], axis=1
        )
        for row in range(2)
    ]
    out_rows = dot_right(jnp.concatenate(around, axis=0), back[0], back[1])
    mixed = (around[0] + around[1], around[0] - around[1])
    corr = []
    for x0 in range(0, cx, group):
        lhs = jnp.concatenate(
            [hfield[x] + (first_row[x] * inv[x]) * mixed[x % 2] for x in range(x0, x0 + group)], axis=0
        )
        out = dot_right(lhs, edget[0], edget[1])
        corr.append(jnp.where(diag[None], out.reshape(group, kz, wide_lane), 0.0).reshape(group * kz, wide_lane))
    loads["sxt"].wait()
    a, b = split(jnp.concatenate(corr, axis=0))
    main = mm(sxt[...], a)
    corr = (main[:32] + (main[32:] + mm(sxt[pl.ds(0, 32), :], b)))[:cx]
    blank = jnp.zeros((cx, kz), F32)
    from_left = jnp.concatenate([blank, edge_x[:, :-kz]], axis=1)
    from_right = jnp.concatenate([edge_x[:, kz:], blank], axis=1)
    second = lax.rem(lax.broadcasted_iota(jnp.int32, (cx, wide_lane), 1) // kz, 2) == 1
    sides = corr + jnp.where(second, from_right, from_left)
    sides = jnp.concatenate(
        [jnp.zeros((cy, wide_lane), F32), sides, jnp.zeros((128 - cy - cx, wide_lane), F32)], axis=0
    ).T
    sides = jnp.where(
        lax.broadcasted_iota(jnp.int32, (wide_lane, 128), 1) == 127, jnp.broadcast_to(most, (wide_lane, 128)), sides
    )
    for d in range(ng):
        s4[d] = (out_rows[:, 128 * d : 128 * d + 128] + sides[2 * kz * d : 2 * kz * (d + 1)]).reshape(2, kz, 128)

    ex4 = ("grp", lambda d: s4.at[d], lambda d: r4.at[:, d], r4.at[:, pl.ds(0, ng - 1)], x4)
    send(*ex4)
    r4[:, g] = s4[g]
    sent(*ex1)
    sent(*ex2)
    sent(*ex3)
    receive(*ex4)
    for e in range(2):
        solved[e] = r4[e].reshape(nz, 128).T
    most_out[...] = jnp.full((8, 128), jnp.max(solved[0, pl.ds(127, 1), :]), F32)

    for x in range(cx):
        va = solved[0, pl.ds(cy + x, 1), :]
        vb = solved[1, pl.ds(cy + x, 1), :]
        part[x] = jnp.where(even, va + vb, va - vb)

    def second_solve(i, _):
        def fetch(x, at):
            w = part[x]
            value = block[x, at, :] - column[at, :] * jnp.concatenate([w, w], axis=0)
            if x == 0:
                value = value - solved[0, at, :]
            if x == cx - 1:
                value = value - solved[1, at, :]
            return value

        at, values = solve(fetch, i)
        for x in range(cx):
            block[x, at, :] = values[x]
        return 0

    lax.fori_loop(0, cy // 16, second_solve, 0, unroll=2)

    def inverse_z(rows):
        a, b = split(rows)
        both = mm(jnp.concatenate([a, b], axis=1), sz[...])
        return both[:, :nz] + both[:, nz:]

    def backward(i, _):
        pair_x = jnp.concatenate([block[2 * i], block[2 * i + 1]], axis=1)
        out = dot_left(sy[...], pair_x)
        out = inverse_z(jnp.concatenate([out[:, :nz], out[:, nz:]], axis=0))
        grid[2 * i + 1, pl.ds(8, cy), :] = out[:cy]
        grid[2 * i + 2, pl.ds(8, cy), :] = out[cy:]
        return 0

    lax.fori_loop(0, half, backward, 0, unroll=True)
    copy_out = pltpu.make_async_copy(grid.at[pl.ds(1, cx), pl.ds(8, cy), :], pot_h, osem)
    copy_out.start()
    pair_x = jnp.concatenate([solved[0, :cy], solved[1, :cy]], axis=1)
    out = dot_left(sy[...], pair_x)
    rest = jnp.concatenate([out[:, :nz], out[:, nz:], solved[0, cy:], solved[1, cy:]], axis=0)
    rest = inverse_z(rest)
    grid[0, pl.ds(8, cy), :] = rest[:cy]
    grid[cx + 1, pl.ds(8, cy), :] = rest[cy : 2 * cy]
    pad = 128 - cy
    for e in range(2):
        lines = rest[2 * cy + pad * e : 2 * cy + pad * (e + 1)]
        at = pl.ds(7 if e == 0 else 8 + cy, 1)
        for x in range(cx):
            grid[x + 1, at, :] = lines[x : x + 1]
    for e in range(2):
        lines = rest[2 * cy + pad * e : 2 * cy + pad * (e + 1)]
        for s in range(2):
            grid[(cx + 1) * e, pl.ds(7 if s == 0 else 8 + cy, 1), :] = lines[cx + s : cx + s + 1]

    loads["fold"].wait()
    per_y, per_z = cy // 4, nz // 4
    lanes8 = lax.broadcasted_iota(jnp.int32, (8, 128), 1)
    pick = (
        lax.broadcasted_iota(jnp.int32, (16, 128), 1) // 8 == lax.broadcasted_iota(jnp.int32, (16, 128), 0)
    )
    lane6 = lax.rem(lax.broadcasted_iota(jnp.int32, (6, 128), 1), 8)
    row6 = lax.broadcasted_iota(jnp.int32, (6, 128), 0)
    some = 4

    def gather(i, _):
        cut, odd = [], []
        for c in range(2 * some):
            code = jnp.maximum(ghost[0, 2 * some * i + c], 0)
            ix = code // (per_y * per_z)
            iy = lax.rem(code // per_z, per_y)
            iz = lax.rem(code, per_z)
            rows = grid[pl.ds(4 * ix, 6), pl.ds(7 + 4 * iy, 8), :]
            inside = (lanes8 >= 4 * iz - 1) & (lanes8 <= 4 * iz + 4) & (sub < 6)
            cut.append(jnp.where(inside[None], rows, 0.0).reshape(48, 128))
            odd.append(lax.rem(iz, 2))
        a, b = split(jnp.concatenate(cut, axis=0))
        out = mm(jnp.concatenate([a, b], axis=1), fold[...]).reshape(2 * some * 3, 16, 128)
        out = jnp.sum(jnp.where(pick[None], out, 0.0), axis=1)
        for k in range(some):
            d = some * i + k
            mini = out[6 * k : 6 * k + 6]
            turned = jnp.where(lane6 < 4, pltpu.roll(mini, 124, 1), pltpu.roll(mini, 4, 1))
            which = jnp.where(row6 < 3, odd[2 * k], odd[2 * k + 1])
            mini = jnp.where(which == 1, turned, mini)
            slots = [
                jnp.full((1, 128), ghost[1, 2 * d + c].astype(F32), F32) for c in range(2)
            ]
            s6[pl.ds(pl.multiple_of(8 * d, 8), 8), :] = jnp.concatenate([mini] + slots, axis=0)
        return 0

    lax.fori_loop(0, nf // some, gather, 0, unroll=2)

    ex6 = ("fft", tile(s6), tile(r6), most_rows(r6), x6)
    send(*ex6)
    r6[mine, :] = s6[mine, :]
    width = fluid.shape[-1]
    groups = 128 // width
    rate = COURANT / most_out[pl.ds(0, 1), pl.ds(0, width)]

    def pack(y, _):
        for r in range(2):
            at = [2 * i + r for i in range(groups)]
            cons = [[fluid[v, x + 2, y + 2, cells, :] for x in at] for v in range(5)]
            for v in range(4):
                packed[v, r, y] = jnp.concatenate(cons[v], axis=1)
            for v in range(5):
                packed[4 + v, r, y] = jnp.concatenate(
                    [c - rate * change[v, x, y] for c, x in zip(cons[v], at)], axis=1
                )
        return 0

    lax.fori_loop(0, 8, pack, 0)
    copy_packed = pltpu.make_async_copy(packed, packed_h, psem)
    copy_packed.start()
    sent(*ex4)
    copy_out.wait()
    copy_packed.wait()
    receive(*ex6)
    blocks[...] = r6[...]
    sent(*ex6)


def patch_kernel(
    blocks, most, packed_h, pot_in, weave,
    fine_h, moved_h, pot_out,
    fine, moved, packed, hold, sems,
):
    count = fine.shape[-1]
    nf = blocks.shape[0] // 8
    copy_in = pltpu.make_async_copy(pot_in, hold, sems.at[0])
    needs = [
        pltpu.make_async_copy(packed_h.at[0], packed.at[0], sems.at[8]),
        pltpu.make_async_copy(packed_h.at[pl.ds(1, 8)], packed.at[pl.ds(1, 8)], sems.at[9]),
    ]
    needs[0].start()
    copy_in.start()
    needs[1].start()
    copy_out = pltpu.make_async_copy(hold, pot_out, sems.at[1])
    groups = 128 // count

    lanes = lax.rem(lax.broadcasted_iota(jnp.int32, (nf, 128), 1), count)
    hot = jnp.concatenate(
        [
            jnp.where(blocks[pl.ds(6 + c, nf, stride=8), :] == lanes.astype(F32), 1.0, 0.0)
            for c in range(2)
        ],
        axis=0,
    ).astype(BF16)
    within, outside = [], []
    for t in range(3):
        came = jnp.concatenate([blocks[pl.ds(c * 3 + t, nf, stride=8), :] for c in range(2)], axis=0)
        a, b = split(came.T)
        placed = mm(a, hot) + mm(b, hot)
        a, b = split(placed)
        woven = mm(weave[...], a) + mm(weave[...], b)
        woven = woven.reshape(2, 2, 8, 8, 128)
        within += [woven[0, 0], woven[0, 1]]
        outside += [woven[1, 0], woven[1, 1]]

    z = lax.broadcasted_iota(jnp.int32, (8, 128), 0)
    q = lax.broadcasted_iota(jnp.int32, (8, 128), 1) // count
    bottom, top, zeven = z == 0, z == 7, lax.rem(z, 2) == 0
    zodd = jnp.logical_not(zeven)
    first, final = q == 0, q == 3

    def choose(values, shift, y):
        out = values[shift + 3][y]
        for i in (2, 1, 0):
            out = jnp.where(q == i, values[shift + i][y], out)
        return out

    def along_x(values, r, y):
        if r == 0:
            return 0.25 * choose(values, 0, y) + 0.75 * choose(values, 1, y)
        return 0.75 * choose(values, 1, y) + 0.25 * choose(values, 2, y)

    def between(values, j):
        low = j // 2
        return (
            0.75 * values[low] + 0.25 * values[low + 1]
            if j % 2 == 0
            else 0.25 * values[low] + 0.75 * values[low + 1]
        )

    scale = 1.0 / (6.0 + SCREEN * FINE_STEP * FINE_STEP)
    layers, rims, states, force = {}, {}, {}, {}
    for r in range(2):
        plane = [along_x(within, r, y) for y in range(6)]
        for jy in range(10):
            value = between(plane, jy)
            if 1 <= jy <= 8:
                states[r, jy - 1] = value
            else:
                rims[r, jy] = value
        plane = [along_x(outside, r, y) for y in range(6)]
        for jy in range(1, 9):
            layers[r, jy - 1] = between(plane, jy)
    ends = (
        [0.75 * within[0][y] + 0.25 * within[1][y] for y in range(6)],
        [0.25 * within[4][y] + 0.75 * within[5][y] for y in range(6)],
    )
    keys = [(r, y) for r in range(2) for y in range(8)]
    sides = {
        (r, y): jnp.where(first if r == 0 else final, between(ends[r], y + 1), 0.0) for r, y in keys
    }
    needs[0].wait()
    for r, y in keys:
        ghost = layers[r, y] + sides[r, y]
        if y == 0:
            ghost = ghost + rims[r, 0]
        if y == 7:
            ghost = ghost + rims[r, 9]
        force[r, y] = (OMEGA * scale) * (ghost - FINE_STEP * FINE_STEP * packed[0, r, y])

    copy_in.wait()
    copy_out.start()

    def beside(old, r, y):
        other = old[1 - r, y]
        if r == 0:
            return other, jnp.where(first, 0.0, pltpu.roll(other, count, 1))
        return other, jnp.where(final, 0.0, pltpu.roll(other, 128 - count, 1))

    def sweep(_, carry):
        old = dict(zip(keys, carry))
        for colour in (0, 1):
            new = {}
            for r, y in keys:
                v = old[r, y]
                other, far = beside(old, r, y)
                near = (other + far) + (
                    jnp.where(bottom, 0.0, pltpu.roll(v, 1, 0)) + jnp.where(top, 0.0, pltpu.roll(v, 7, 0))
                )
                if y > 0:
                    near = near + old[r, y - 1]
                if y < 7:
                    near = near + old[r, y + 1]
                value = (1.0 - OMEGA) * v + ((OMEGA * scale) * near + force[r, y])
                mask = zeven if (r + y + colour) % 2 == 0 else zodd
                new[r, y] = jnp.where(mask, value, v)
            old = new
        return tuple(old[k] for k in keys)

    out = lax.fori_loop(0, SWEEPS, sweep, tuple(states[k] for k in keys))
    states = dict(zip(keys, out))

    def spill(target, r, y, value):
        for i in range(groups):
            target[2 * i + r, y] = value[:, count * i : count * (i + 1)]

    copies = [pltpu.make_async_copy(fine, fine_h, sems.at[2])] + [
        pltpu.make_async_copy(moved.at[v], moved_h.at[v], sems.at[3 + v]) for v in range(5)
    ]
    for r, y in keys:
        spill(fine, r, y, states[r, y])
    copies[0].start()

    needs[1].wait()
    for r, y in keys:
        spill(moved.at[0], r, y, packed[4, r, y])
    copies[1].start()
    step = COURANT * FINE_STEP / most[pl.ds(0, 1), :]
    work = {}
    for n in range(3):
        for r, y in keys:
            v = states[r, y]
            if n == 0:
                other, far = beside(states, r, y)
                far = far + sides[r, y]
                pull = far - other if r == 0 else other - far
            elif n == 1:
                down = states[r, y - 1] if y > 0 else rims[r, 0]
                up = states[r, y + 1] if y < 7 else rims[r, 9]
                pull = down - up
            else:
                layer = layers[r, y]
                pull = jnp.where(bottom, layer, pltpu.roll(v, 1, 0)) - jnp.where(top, layer, pltpu.roll(v, 7, 0))
            spill(moved.at[1 + n], r, y, packed[5 + n, r, y] + step * packed[0, r, y] * pull)
            part = packed[1 + n, r, y] * pull
            work[r, y] = part if n == 0 else work[r, y] + part
        copies[2 + n].start()
    for r, y in keys:
        spill(moved.at[4], r, y, packed[8, r, y] + step * work[r, y])
    copies[5].start()
    for c in copies:
        c.wait()
    copy_out.wait()


def root_call(ghost, rho, fluid, nf, ng):
    cx, cy, nz = rho.shape
    kz = nz // ng
    ny = ng * cy
    count = fluid.shape[-1]
    tab = tables(nf, ng, cx, cy, nz)
    consts = [jnp.asarray(tab[n]) for n in NAMES]
    vm = lambda shape, dtype=F32: pltpu.VMEM(shape, dtype)
    anyspace = pl.BlockSpec(memory_space=pl.ANY)
    vspace = pl.BlockSpec(memory_space=pltpu.VMEM)
    dma = pltpu.SemaphoreType.DMA
    local = {n: tab[n].shape for n in NAMES}
    local["inv"] = local["inv"][1:]
    local["pair"] = local["pair"][2:]
    limit = 56 * 1024 * 1024
    potential, blocks, most, packed = pl.pallas_call(
        functools.partial(root_kernel, (nf, ng, cx, cy, nz)),
        out_shape=(
            jax.ShapeDtypeStruct((cx, cy, nz), F32),
            jax.ShapeDtypeStruct((nf * 8, 128), F32),
            jax.ShapeDtypeStruct((8, 128), F32),
            jax.ShapeDtypeStruct((9, 2, 8, 8, 128), F32),
        ),
        in_specs=[pl.BlockSpec(memory_space=pltpu.SMEM)] + [anyspace] * (2 + len(NAMES)),
        out_specs=(anyspace, vspace, vspace, anyspace),
        scratch_shapes=[vm((cx, cy, nz))]
        + [vm(local[n], consts[i].dtype) for i, n in enumerate(NAMES)]
        + [
            vm(fluid.shape), vm((5, 12, 12, 8, count)),
            vm((cx, cy, nz)),
            vm((2, 128, nz)),
            vm((cx, 8, nz)),
            vm((cx + 2, cy + 16, nz)),
            vm((cx, kz, ny)),
            vm((2, nz, 128)), vm((ng, 2, kz, 128)),
            vm((nf * 8, 128)), vm((nf * 8, 128)),
            vm((nf * 8, 128)), vm((nf * 8, 128)),
            vm((ng, 2, kz, 128)), vm((2, ng, kz, 128)),
            vm((nf * 8, 128)), vm((nf * 8, 128)),
            vm((2 * nf, 8, 128)), vm((nf, 8, 128)),
            vm((5, 8, 8, count)),
            vm((5, 8, 8, 8, count)), vm((9, 2, 8, 8, 128)),
            dma((18,)), dma, dma,
            dma((2,)), dma((2,)), dma((2,)), dma((2,)), dma((2,)),
        ],
        compiler_params=pltpu.CompilerParams(
            collective_id=0, has_side_effects=True, vmem_limit_bytes=limit
        ),
    )(ghost, rho, fluid, *consts)
    fine, moved, potential = pl.pallas_call(
        patch_kernel,
        out_shape=(
            jax.ShapeDtypeStruct((8, 8, 8, count), F32),
            jax.ShapeDtypeStruct((5, 8, 8, 8, count), F32),
            jax.ShapeDtypeStruct((cx, cy, nz), F32),
        ),
        in_specs=[vspace, vspace, anyspace, anyspace, vspace],
        out_specs=(anyspace, anyspace, anyspace),
        scratch_shapes=[
            vm((8, 8, 8, count)), vm((5, 8, 8, 8, count)), vm((9, 2, 8, 8, 128)), vm((cx, cy, nz)), dma((10,)),
        ],
        compiler_params=pltpu.CompilerParams(vmem_limit_bytes=limit),
    )(blocks, most, packed, potential, jnp.asarray(tab["weave"]))
    return potential, fine, moved


def per_device(root_density, patch_fluid, ghost_list):
    nf = lax.axis_size("fft")
    ng = lax.axis_size("grp")
    return root_call(ghost_list[:, 0], root_density, patch_fluid, nf, ng)


def solution(mesh):
    return jax.shard_map(
        per_device,
        mesh=mesh,
        in_specs=(
            P("fft", "grp", None),
            P(None, None, None, None, ("fft", "grp")),
            P(None, ("fft", "grp"), None),
        ),
        out_specs=(
            P("fft", "grp", None),
            P(None, None, None, ("fft", "grp")),
            P(None, None, None, None, ("fft", "grp")),
        ),
        check_vma=False,
    )
```

```python
import functools

import jax
import jax.numpy as jnp
import ml_dtypes
import numpy as np
from jax import lax
from jax.experimental import pallas as pl
from jax.experimental.pallas import tpu as pltpu
from jax.sharding import PartitionSpec as P

SWEEPS = 8
GAMMA = 5.0 / 3.0
SCREEN = 0.0006
OMEGA = 1.5
COURANT = 0.4
FINE_STEP = 0.5
F32 = jnp.float32
BF16 = jnp.bfloat16


def sine(count):
    index = np.arange(1, count + 1)
    return np.sqrt(2.0 / (count + 1)) * np.sin(
        np.pi * (np.outer(index, index) % (2 * (count + 1))) / (count + 1)
    )


def eigen(count):
    return 4.0 * np.sin(np.pi * np.arange(1, count + 1) / (2 * (count + 1))) ** 2


def halves(table):
    high = table.astype(ml_dtypes.bfloat16)
    low = (table - high.astype(np.float64)).astype(ml_dtypes.bfloat16)
    return np.stack([high, low])


@functools.lru_cache(None)
def tables(nf, ng, cx, cy, nz):
    ny = ng * cy
    kz = nz // ng
    sz, sy, sx, full = sine(nz), sine(cy), sine(cx), sine(ny)
    lam = eigen(cy)[:, None] + eigen(nz)[None, :] + SCREEN
    steps = [1.0 / (2.0 + lam)]
    for _ in range(1, cx // 2):
        steps.append(1.0 / (2.0 + lam - steps[-1]))
    steps.append(1.0 / (1.0 - steps[-1] ** 2))
    edge = np.zeros((ng, 2, ny))
    wide = np.zeros((ng, 128, ny))
    back = np.zeros((ng, 128, ny))
    for d in range(ng):
        if d > 0:
            edge[d, 0] = full[d * cy - 1]
        if d < ng - 1:
            edge[d, 1] = full[(d + 1) * cy]
        wide[d, :cy] = sy @ full[d * cy : (d + 1) * cy]
        back[d, :cy] = wide[d, :cy]
        back[d, cy + cx] = edge[d, 0]
        back[d, cy + cx + 1] = edge[d, 1]
    repeated = np.repeat(edge.reshape(2 * ng, ny), kz, axis=0)
    denom = (
        eigen(cx)[None, :, None, None]
        + eigen(nz).reshape(ng, 1, kz, 1)
        + eigen(ny)[None, None, None, :]
        + SCREEN
    )
    phi = 2.0 * np.arcsinh(np.sqrt(eigen(ny)[None, :] + eigen(nz)[:, None] + SCREEN) / 2.0)

    def ratio(m, n):
        return np.exp(-(n - m) * phi) * np.expm1(-2 * m * phi) / np.expm1(-2 * n * phi)

    pair = np.zeros((ng, nf, 2, 8, 128))
    for i, values in enumerate((ratio(cx - 1, cx), ratio(1, cx))):
        pair[:, :, i, :3] = values.reshape(ng, nf, 3, 128)
    spread = np.zeros((10, 6))
    for j in range(10):
        at = j / 2 + 0.25
        low = int(np.floor(at))
        spread[j, low] += 1 - (at - low)
        spread[j, low + 1] += at - low
    inner = np.zeros((8, 8))
    inner[:, :6] = spread[1:9]
    outer = np.zeros((8, 8))
    outer[0, :6] = spread[0]
    outer[7, :6] = spread[9]
    weave = np.concatenate([np.kron(np.eye(16), inner), np.kron(np.eye(16), outer)])
    lanes = np.arange(128)
    fold = ((lanes[:, None] + 1) % 8 == lanes[None, :] % 8).astype(np.float64)
    column = np.broadcast_to(sy[0][:, None], (cy, 128))
    as32 = lambda t: np.ascontiguousarray(t, dtype=np.float32)
    szh, szl = halves(sz)
    syh, syl = halves(sy)
    wide_x = np.zeros((cx, 32))
    wide_x[:, :cx] = sx
    xh, xl = halves(np.repeat(wide_x, kz, axis=0))
    sx_rows = np.block([[xh, xh], [xl, np.zeros_like(xl)]]).astype(ml_dtypes.bfloat16)
    tall_x = np.zeros((32, cx * kz))
    tall_x[:cx] = np.repeat(sx, kz, axis=1)
    sx_sums = np.concatenate(halves(tall_x))
    return dict(
        sz=np.block([[szh, szl], [szh, np.zeros_like(szh)]]).astype(ml_dtypes.bfloat16),
        sy=np.block([[syh, syh], [syl, np.zeros_like(syl)]]).astype(ml_dtypes.bfloat16),
        sx=sx_rows,
        sxt=sx_sums,
        steps=as32(np.stack(steps)),
        wide=halves(wide.reshape(ng * 128, ny)),
        back=halves(np.ascontiguousarray(back.reshape(ng * 128, ny).T)),
        edge=halves(repeated),
        edget=halves(np.ascontiguousarray(repeated.T)),
        inv=as32(1.0 / denom),
        pair=as32(pair),
        weave=np.concatenate([weave, weave], axis=1).astype(ml_dtypes.bfloat16),
        fold=np.concatenate([fold, fold]).astype(ml_dtypes.bfloat16),
        column=as32(column),
    )


NAMES = (
    "sz", "sy", "sx", "sxt", "steps", "wide", "back", "edge", "edget", "inv", "pair", "fold", "column",
)


def split(value):
    high = value.astype(BF16)
    return high, (value - high.astype(F32)).astype(BF16)


def mm(a, b):
    return jnp.dot(a, b, preferred_element_type=F32)


def dot_right(value, high, low):
    rows = value.shape[0]
    a, b = split(value)
    main = mm(jnp.concatenate([a, b], axis=0), high)
    return main[:rows] + (main[rows:] + mm(a, low))


def dot_left(both, value):
    rows = both.shape[0] // 2
    a, b = split(value)
    out = mm(both, jnp.concatenate([a, b], axis=0))
    return out[:rows] + out[rows:]


def root_kernel(
    cfg,
    ghost, rho, fluid_h,
    sz_h, sy_h, sx_h, sxt_h, steps_h, wide_h, back_h, edge_h, edget_h, inv_h, pair_h, fold_h, column_h,
    pot_h, blocks_h, most_h, packed_h,
    src, sz, sy, sx, sxt, steps, wide, back, edge, edget, inv, pair, fold, column, fluid, prim,
    block, solved, part, grid, hfield,
    s1, r1, s2, r2, s3, r3, s4, r4, s6, most_out, chain, mults, last_face, change, packed,
    tsem, osem, psem, bsem, msem, x1, x2, x3, x4, x6,
):
    nf, ng, cx, cy, nz = cfg
    kz = nz // ng
    ny = ng * cy
    half = cx // 2
    f = lax.axis_index("fft")
    g = lax.axis_index("grp")

    quarter = cx // 4
    early = [
        (f"rho{i}", rho.at[pl.ds(quarter * i, quarter)], src.at[pl.ds(quarter * i, quarter)]) for i in range(4)
    ]
    early[1:1] = [("sz", sz_h, sz), ("sy", sy_h, sy)]
    early += [("steps", steps_h, steps), ("column", column_h, column), ("pair", pair_h.at[g, f], pair)]
    late = [
        ("wide", wide_h, wide), ("sx", sx_h, sx), ("edge", edge_h, edge), ("inv", inv_h.at[g], inv),
        ("fluid", fluid_h, fluid), ("edget", edget_h, edget), ("sxt", sxt_h, sxt), ("back", back_h, back), ("fold", fold_h, fold),
    ]
    loads = {
        name: pltpu.make_async_copy(a, b, tsem.at[i]) for i, (name, a, b) in enumerate(early + late)
    }
    for name, _, _ in early:
        loads[name].start()

    ny_chips = 4 if nf % 4 == 0 else 1
    nz_chips = nf // ny_chips
    barrier = pltpu.get_barrier_semaphore()

    def grp_partner(k):
        return lax.rem(g + k, ng)

    def fft_partner(k):
        a, b = k // ny_chips, lax.rem(k, ny_chips)
        dz = nz_chips // 2 + ((a + 1) // 2) * (1 - 2 * lax.rem(a, 2))
        dy = ny_chips // 2 + ((b + 1) // 2) * (1 - 2 * lax.rem(b, 2))
        return lax.rem(f // ny_chips + dz, nz_chips) * ny_chips + lax.rem(lax.rem(f, ny_chips) + dy, ny_chips)

    ways = {"grp": (1, ng, grp_partner, g), "fft": (0, nf - 1, fft_partner, f)}

    def hello(axis):
        begin, end, partner, _ = ways[axis]

        def body(k, _):
            pl.semaphore_signal(
                barrier, inc=1, device_id={axis: partner(k)}, device_id_type=pl.DeviceIdType.MESH
            )
            return 0

        lax.fori_loop(begin, end, body, 0, unroll=True)

    hello("fft")
    hello("grp")

    sub = lax.broadcasted_iota(jnp.int32, (8, 128), 0)
    even = lax.rem(sub, 2) == 0

    loads["sz"].wait()
    loads["sy"].wait()

    def forward(i, _):
        rows = src[pl.ds(2 * i, 2)].reshape(2 * cy, nz)
        a, b = split(rows)
        both = mm(jnp.concatenate([a, b], axis=1), sz[...])
        both = both[:, :nz] + both[:, nz:]
        pair_x = jnp.concatenate([both[:cy], both[cy:]], axis=1)
        out = dot_left(sy[...], pair_x)
        block[2 * i] = out[:, :nz]
        block[2 * i + 1] = out[:, nz:]
        return 0

    for part_of in range(4):
        loads[f"rho{part_of}"].wait()
        if part_of == 3:
            for name, _, _ in late:
                loads[name].start()
        lax.fori_loop(part_of * half // 4, (part_of + 1) * half // 4, forward, 0, unroll=True)

    loads["steps"].wait()
    loads["column"].wait()

    def solve(fetch, i):
        at = pl.ds(pl.multiple_of(16 * i, 16), 16)
        low, high = [], []
        for j in range(half):
            m = steps[j, at, :]
            a, b = fetch(j, at), fetch(cx - 1 - j, at)
            if j == 0:
                low.append(-m * a)
                high.append(-m * b)
            else:
                low.append(m * (low[-1] - a))
                high.append(m * (high[-1] - b))
        m, scale = steps[half - 1, at, :], steps[half, at, :]
        a, b = low[-1], high[-1]
        low[-1] = (a + m * b) * scale
        high[-1] = (b + m * a) * scale
        for j in range(half - 2, -1, -1):
            m = steps[j, at, :]
            low[j] = low[j] + m * low[j + 1]
            high[j] = high[j] + m * high[j + 1]
        return at, low + high[::-1]

    part[...] = jnp.zeros_like(part)

    def first(i, _):
        at, values = solve(lambda x, at: block[x, at, :], i)
        col = column[at, :]
        for x in range(cx):
            v = values[x] * col
            part[x] += v[:8] + v[8:]
        solved[0, at, :] = values[0]
        solved[1, at, :] = values[cx - 1]
        return 0

    lax.fori_loop(0, cy // 16, first, 0, unroll=2)
    sums = part[...]
    sign = jnp.where(even, 1.0, -1.0)
    edges = (jnp.sum(sums, axis=1), jnp.sum(sums * sign[None], axis=1))
    for e in range(2):
        solved[e, pl.ds(cy, cx), :] = edges[e]
        solved[e, pl.ds(cy + cx, 8), :] = jnp.zeros((8, 128), F32)
        s1[e] = solved[e].T


    cells = pl.ds(2, 8)

    def cell_values(cons):
        dens = cons[0]
        over = 1.0 / dens
        vel = [m * over for m in cons[1:4]]
        kinetic = 0.5 * (cons[1] * vel[0] + cons[2] * vel[1] + cons[3] * vel[2])
        return [dens] + vel + [(GAMMA - 1.0) * (cons[4] - kinetic)]

    def sound(dens, pres):
        return jnp.sqrt(GAMMA * pres) * lax.rsqrt(dens)

    def make_cells(x, _):
        for y in range(12):
            w = cell_values([fluid[v, x, y, cells, :] for v in range(5)])
            for v in range(5):
                prim[v, x, y] = w[v]
        return 0

    def top_speed():
        def body(x, top):
            for y in range(2, 10):
                w = [prim[v, x + 2, y] for v in range(5)]
                fast = jnp.maximum(jnp.maximum(jnp.abs(w[1]), jnp.abs(w[2])), jnp.abs(w[3]))
                top = jnp.maximum(top, fast + sound(w[0], w[4]))
            return top
        return jnp.max(lax.fori_loop(0, 8, body, jnp.zeros((8, fluid.shape[-1]), F32)))

    def states(before, here, after):
        low, high = [], []
        for a, b, c in zip(before, here, after):
            p, q = b - a, c - b
            half_slope = 0.5 * (
                jnp.maximum(0.0, jnp.minimum(p, q)) + jnp.minimum(0.0, jnp.maximum(p, q))
            )
            low.append(b - half_slope)
            high.append(b + half_slope)
        return low, high

    def side(w, n):
        dens, vel, pres = w[0], w[1:4], w[4]
        energy = pres * (1.0 / (GAMMA - 1.0)) + 0.5 * dens * (
            vel[0] * vel[0] + vel[1] * vel[1] + vel[2] * vel[2]
        )
        mom = [dens * v for v in vel]
        flux = [mom[n]] + [mom[n] * v for v in vel] + [(energy + pres) * vel[n]]
        flux[1 + n] = flux[1 + n] + pres
        return [dens] + mom + [energy], flux, jnp.abs(vel[n]) + sound(dens, pres)

    def face(left, right, n):
        cl, fl, al = side(left, n)
        cr, fr, ar = side(right, n)
        top = jnp.maximum(al, ar)
        return [0.5 * ((a + b) - top * (d - c)) for a, b, c, d in zip(fl, fr, cl, cr)]

    def sweep_line(get, put, n):
        w = [get(0), get(1), get(2)]
        _, high = states(*w)
        flux = None
        for i in range(2, 11):
            w = [w[1], w[2], get(i + 1)]
            low, high_next = states(*w)
            now = face(high, low, n)
            if flux is not None:
                put(i - 3, [b - a for a, b in zip(flux, now)])
            flux, high = now, high_next

    def lines_x(y, _):
        def get(i):
            return [prim[v, i, y + 2] for v in range(5)]

        def put(i, values):
            for v in range(5):
                change[v, i, y] = values[v]

        sweep_line(get, put, 0)
        return 0

    def lines_y(x, _):
        def get(i):
            return [prim[v, x + 2, i] for v in range(5)]

        def put(i, values):
            for v in range(5):
                change[v, x, i] += values[v]

        sweep_line(get, put, 1)
        return 0

    def last_faces(x, _):
        w = [
            cell_values([fluid[v, x + 2, cells, k, :] for v in range(5)]) for k in (8, 9, 10, 11)
        ]
        _, high = states(w[0], w[1], w[2])
        low, _ = states(w[1], w[2], w[3])
        flux = face(high, low, 2)
        for v in range(5):
            last_face[v, x] = flux[v]
        return 0

    def lines_z(x, _):
        row = lax.broadcasted_iota(jnp.int32, (8, fluid.shape[-1]), 0)
        for y in range(8):
            w = [
                cell_values([fluid[v, x + 2, y + 2, pl.ds(k, 8), :] for v in range(5)]) if k != 2
                else [prim[v, x + 2, y + 2] for v in range(5)]
                for k in range(4)
            ]
            _, high = states(w[0], w[1], w[2])
            low, _ = states(w[1], w[2], w[3])
            flux = face(high, low, 2)
            for v in range(5):
                after = jnp.where(row == 7, last_face[v, x, pl.ds(y, 1), :], pltpu.roll(flux[v], 7, 0))
                change[v, x, y] += after - flux[v]
        return 0

    pl.semaphore_wait(barrier, ng + nf - 2)

    def send(axis, source, target, every, sems):
        begin, end, partner, pos = ways[axis]

        def body(k, _):
            to = partner(k)
            pltpu.make_async_remote_copy(
                source(to), target(pos), sems.at[0], sems.at[1], device_id={axis: to},
                device_id_type=pl.DeviceIdType.MESH,
            ).start()
            return 0

        lax.fori_loop(begin, end, body, 0, unroll=True)

    def whole(axis, source, target, every, sems):
        return pltpu.make_async_remote_copy(
            every, every, sems.at[0], sems.at[1], device_id={axis: ways[axis][2](1)},
            device_id_type=pl.DeviceIdType.MESH,
        )

    def receive(*exchange):
        whole(*exchange).wait_recv()

    def sent(*exchange):
        whole(*exchange).wait_send()

    slice1 = lambda d: s1.at[:, pl.ds(pl.multiple_of(d * kz, kz), kz), :]
    ex1 = ("grp", slice1, lambda d: r1.at[d], r1.at[pl.ds(0, ng - 1)], x1)
    send(*ex1)
    r1[g] = s1[:, pl.ds(pl.multiple_of(g * kz, kz), kz), :]

    loads["pair"].wait()
    ca, cb = pair[0], pair[1]
    ca2, cb2 = ca * ca, cb * cb

    def coefficients(i, m):
        m0 = 1.0 / (1.0 - ca2 * m)
        mults[2 * i] = m0
        m1 = 1.0 / (1.0 - cb2 * m0)
        mults[2 * i + 1] = m1
        return m1

    lax.fori_loop(0, nf // 2, coefficients, jnp.zeros((8, 128), F32))
    loads["fluid"].wait()
    lax.fori_loop(0, 12, make_cells, 0)
    most = jnp.full((1, 128), top_speed(), F32)
    loads["wide"].wait()
    loads["sx"].wait()
    loads["edge"].wait()
    loads["inv"].wait()
    receive(*ex1)

    main = jnp.concatenate([r1[d].reshape(2 * kz, 128) for d in range(ng)], axis=1)
    main = dot_right(main, wide[0], wide[1])
    across = r1[...].reshape(ng * 2 * kz, 128).T
    edge_x = across[cy : cy + cx]
    edge_k = dot_left(sx[...], across[cy : cy + 32]).reshape(cx, kz, ng * 2 * kz)
    wide_lane = ng * 2 * kz
    diag = (
        lax.rem(lax.broadcasted_iota(jnp.int32, (kz, wide_lane), 1), kz)
        == lax.broadcasted_iota(jnp.int32, (kz, wide_lane), 0)
    )
    sums = [jnp.zeros((kz, ny), F32), jnp.zeros((kz, ny), F32)]
    first_row = [float(v) for v in sine(cx)[0]]
    group = cx // 2
    for x0 in range(0, cx, group):
        lhs = jnp.where(diag[None], edge_k[x0 : x0 + group], 0.0).reshape(group * kz, wide_lane)
        out = dot_right(lhs, edge[0], edge[1])
        for x in range(x0, x0 + group):
            hd = out[(x - x0) * kz : (x - x0 + 1) * kz] * inv[x]
            hfield[x] = hd
            sums[x % 2] = sums[x % 2] + first_row[x] * hd
    rows = (main[:kz] + (sums[0] + sums[1]), main[kz:] + (sums[0] - sums[1]))
    for row in range(2):
        for j in range(6):
            s2[pl.ds((j // 3) * 8 + row * 3 + j % 3, kz, stride=16), :] = rows[row][:, j * 128 : (j + 1) * 128]
    for r in (6, 7):
        s2[pl.ds(r, nf, stride=8), :] = jnp.broadcast_to(most, (nf, 128))

    most_rows = lambda ref: ref.at[pl.ds(0, (nf - 1) * 8), :]
    tile = lambda ref: lambda d: ref.at[pl.ds(pl.multiple_of(d * 8, 8), 8), :]
    ex2 = ("fft", tile(s2), tile(r2), most_rows(r2), x2)
    send(*ex2)
    mine = pl.ds(pl.multiple_of(f * 8, 8), 8)
    r2[mine, :] = s2[mine, :]
    lax.fori_loop(0, 8, lines_x, 0)
    lax.fori_loop(0, 8, lines_y, 0)
    receive(*ex2)
    most = jnp.max(r2[pl.ds(6, nf, stride=8), :], axis=0, keepdims=True)

    last = jnp.zeros((8, 128), F32)

    def right_sides(d):
        msg = r2[8 * d : 8 * d + 8, :]
        other = pltpu.roll(msg, 5, 0)
        return msg - cb * other, other - cb * msg

    up = down = last
    for d in range(nf // 2):
        m0, m1 = mults[2 * d], mults[2 * d + 1]
        ma, mb = m0 * ca, m1 * cb
        e = nf - 1 - d
        p, q = right_sides(d)
        up = m0 * p + ma * up
        chain[2 * d] = up
        up = m1 * q + mb * up
        chain[2 * d + 1] = up
        p, q = right_sides(e)
        down = m0 * q + ma * down
        chain[2 * e + 1] = down
        down = m1 * p + mb * down
        chain[2 * e] = down
    link = mults[nf - 1] * ca
    over = 1.0 / (1.0 - link * link)
    up, down = (up + link * down) * over, (down + link * up) * over
    chain[nf - 1] = up
    chain[nf] = down
    for j in range(nf - 2, -1, -1):
        m = mults[j] * (cb if j % 2 == 0 else ca)
        up = chain[j] + m * up
        chain[j] = up
        down = chain[2 * nf - 1 - j] + m * down
        chain[2 * nf - 1 - j] = down
    for d in range(nf):
        left = chain[2 * d - 1] if d > 0 else last
        right = chain[2 * d + 2] if d < nf - 1 else last
        s3[8 * d : 8 * d + 8, :] = jnp.where(sub < 3, left, pltpu.roll(right, 3, 0))

    ex3 = ("fft", tile(s3), tile(r3), most_rows(r3), x3)
    send(*ex3)
    r3[mine, :] = s3[mine, :]
    loads["edget"].wait()
    loads["back"].wait()
    lax.fori_loop(0, 8, last_faces, 0)
    lax.fori_loop(0, 8, lines_z, 0)
    receive(*ex3)
    around = [
        jnp.concatenate(
            [r3[pl.ds((j // 3) * 8 + row * 3 + j % 3, kz, stride=16), :] for j in range(6)], axis=1
        )
        for row in range(2)
    ]
    out_rows = dot_right(jnp.concatenate(around, axis=0), back[0], back[1])
    mixed = (around[0] + around[1], around[0] - around[1])
    corr = []
    for x0 in range(0, cx, group):
        lhs = jnp.concatenate(
            [hfield[x] + (first_row[x] * inv[x]) * mixed[x % 2] for x in range(x0, x0 + group)], axis=0
        )
        out = dot_right(lhs, edget[0], edget[1])
        corr.append(jnp.where(diag[None], out.reshape(group, kz, wide_lane), 0.0).reshape(group * kz, wide_lane))
    loads["sxt"].wait()
    a, b = split(jnp.concatenate(corr, axis=0))
    main = mm(sxt[...], a)
    corr = (main[:32] + (main[32:] + mm(sxt[pl.ds(0, 32), :], b)))[:cx]
    blank = jnp.zeros((cx, kz), F32)
    from_left = jnp.concatenate([blank, edge_x[:, :-kz]], axis=1)
    from_right = jnp.concatenate([edge_x[:, kz:], blank], axis=1)
    second = lax.rem(lax.broadcasted_iota(jnp.int32, (cx, wide_lane), 1) // kz, 2) == 1
    sides = corr + jnp.where(second, from_right, from_left)
    sides = jnp.concatenate(
        [jnp.zeros((cy, wide_lane), F32), sides, jnp.zeros((128 - cy - cx, wide_lane), F32)], axis=0
    ).T
    sides = jnp.where(
        lax.broadcasted_iota(jnp.int32, (wide_lane, 128), 1) == 127, jnp.broadcast_to(most, (wide_lane, 128)), sides
    )
    for d in range(ng):
        s4[d] = (out_rows[:, 128 * d : 128 * d + 128] + sides[2 * kz * d : 2 * kz * (d + 1)]).reshape(2, kz, 128)

    ex4 = ("grp", lambda d: s4.at[d], lambda d: r4.at[:, d], r4.at[:, pl.ds(0, ng - 1)], x4)
    send(*ex4)
    r4[:, g] = s4[g]
    sent(*ex1)
    sent(*ex2)
    sent(*ex3)
    receive(*ex4)
    for e in range(2):
        solved[e] = r4[e].reshape(nz, 128).T
    most_out[...] = jnp.full((8, 128), jnp.max(solved[0, pl.ds(127, 1), :]), F32)
    copy_most = pltpu.make_async_copy(most_out, most_h, msem)
    copy_most.start()

    for x in range(cx):
        va = solved[0, pl.ds(cy + x, 1), :]
        vb = solved[1, pl.ds(cy + x, 1), :]
        part[x] = jnp.where(even, va + vb, va - vb)

    def second_solve(i, _):
        def fetch(x, at):
            w = part[x]
            value = block[x, at, :] - column[at, :] * jnp.concatenate([w, w], axis=0)
            if x == 0:
                value = value - solved[0, at, :]
            if x == cx - 1:
                value = value - solved[1, at, :]
            return value

        at, values = solve(fetch, i)
        for x in range(cx):
            block[x, at, :] = values[x]
        return 0

    lax.fori_loop(0, cy // 16, second_solve, 0, unroll=2)

    def inverse_z(rows):
        a, b = split(rows)
        both = mm(jnp.concatenate([a, b], axis=1), sz[...])
        return both[:, :nz] + both[:, nz:]

    def backward(i, _):
        pair_x = jnp.concatenate([block[2 * i], block[2 * i + 1]], axis=1)
        out = dot_left(sy[...], pair_x)
        out = inverse_z(jnp.concatenate([out[:, :nz], out[:, nz:]], axis=0))
        grid[2 * i + 1, pl.ds(8, cy), :] = out[:cy]
        grid[2 * i + 2, pl.ds(8, cy), :] = out[cy:]
        return 0

    lax.fori_loop(0, half, backward, 0, unroll=True)
    copy_out = pltpu.make_async_copy(grid.at[pl.ds(1, cx), pl.ds(8, cy), :], pot_h, osem)
    copy_out.start()
    pair_x = jnp.concatenate([solved[0, :cy], solved[1, :cy]], axis=1)
    out = dot_left(sy[...], pair_x)
    rest = jnp.concatenate([out[:, :nz], out[:, nz:], solved[0, cy:], solved[1, cy:]], axis=0)
    rest = inverse_z(rest)
    grid[0, pl.ds(8, cy), :] = rest[:cy]
    grid[cx + 1, pl.ds(8, cy), :] = rest[cy : 2 * cy]
    pad = 128 - cy
    for e in range(2):
        lines = rest[2 * cy + pad * e : 2 * cy + pad * (e + 1)]
        at = pl.ds(7 if e == 0 else 8 + cy, 1)
        for x in range(cx):
            grid[x + 1, at, :] = lines[x : x + 1]
    for e in range(2):
        lines = rest[2 * cy + pad * e : 2 * cy + pad * (e + 1)]
        for s in range(2):
            grid[(cx + 1) * e, pl.ds(7 if s == 0 else 8 + cy, 1), :] = lines[cx + s : cx + s + 1]

    loads["fold"].wait()
    per_y, per_z = cy // 4, nz // 4
    lanes8 = lax.broadcasted_iota(jnp.int32, (8, 128), 1)
    pick = (
        lax.broadcasted_iota(jnp.int32, (16, 128), 1) // 8 == lax.broadcasted_iota(jnp.int32, (16, 128), 0)
    )
    lane6 = lax.rem(lax.broadcasted_iota(jnp.int32, (6, 128), 1), 8)
    row6 = lax.broadcasted_iota(jnp.int32, (6, 128), 0)
    some = 4

    def gather(i, _):
        cut, odd = [], []
        for c in range(2 * some):
            code = jnp.maximum(ghost[0, 2 * some * i + c], 0)
            ix = code // (per_y * per_z)
            iy = lax.rem(code // per_z, per_y)
            iz = lax.rem(code, per_z)
            rows = grid[pl.ds(4 * ix, 6), pl.ds(7 + 4 * iy, 8), :]
            inside = (lanes8 >= 4 * iz - 1) & (lanes8 <= 4 * iz + 4) & (sub < 6)
            cut.append(jnp.where(inside[None], rows, 0.0).reshape(48, 128))
            odd.append(lax.rem(iz, 2))
        a, b = split(jnp.concatenate(cut, axis=0))
        out = mm(jnp.concatenate([a, b], axis=1), fold[...]).reshape(2 * some * 3, 16, 128)
        out = jnp.sum(jnp.where(pick[None], out, 0.0), axis=1)
        for k in range(some):
            d = some * i + k
            mini = out[6 * k : 6 * k + 6]
            turned = jnp.where(lane6 < 4, pltpu.roll(mini, 124, 1), pltpu.roll(mini, 4, 1))
            which = jnp.where(row6 < 3, odd[2 * k], odd[2 * k + 1])
            mini = jnp.where(which == 1, turned, mini)
            slots = [
                jnp.full((1, 128), ghost[1, 2 * d + c].astype(F32), F32) for c in range(2)
            ]
            s6[pl.ds(pl.multiple_of(8 * d, 8), 8), :] = jnp.concatenate([mini] + slots, axis=0)
        return 0

    lax.fori_loop(0, nf // some, gather, 0, unroll=2)

    ex6 = ("fft", tile(s6), tile(blocks_h), most_rows(blocks_h), x6)
    send(*ex6)
    copy_mine = pltpu.make_async_copy(s6.at[mine, :], blocks_h.at[mine, :], bsem)
    copy_mine.start()
    width = fluid.shape[-1]
    groups = 128 // width
    rate = COURANT / most_out[pl.ds(0, 1), pl.ds(0, width)]

    def pack(y, _):
        for r in range(2):
            at = [2 * i + r for i in range(groups)]
            cons = [[fluid[v, x + 2, y + 2, cells, :] for x in at] for v in range(5)]
            for v in range(4):
                packed[v, r, y] = jnp.concatenate(cons[v], axis=1)
            for v in range(5):
                packed[4 + v, r, y] = jnp.concatenate(
                    [c - rate * change[v, x, y] for c, x in zip(cons[v], at)], axis=1
                )
        return 0

    lax.fori_loop(0, 8, pack, 0)
    copy_packed = pltpu.make_async_copy(packed, packed_h, psem)
    copy_packed.start()
    sent(*ex4)
    copy_out.wait()
    copy_packed.wait()
    copy_most.wait()
    copy_mine.wait()
    sent(*ex6)
    receive(*ex6)


def patch_kernel(
    blocks, most, packed_h, pot_in, weave,
    fine_h, moved_h, pot_out,
    fine, moved, packed, hold, sems,
):
    count = fine.shape[-1]
    nf = blocks.shape[0] // 8
    copy_in = pltpu.make_async_copy(pot_in, hold, sems.at[0])
    needs = [
        pltpu.make_async_copy(packed_h.at[0], packed.at[0], sems.at[8]),
        pltpu.make_async_copy(packed_h.at[pl.ds(1, 8)], packed.at[pl.ds(1, 8)], sems.at[9]),
    ]
    needs[0].start()
    copy_in.start()
    needs[1].start()
    copy_out = pltpu.make_async_copy(hold, pot_out, sems.at[1])
    groups = 128 // count

    lanes = lax.rem(lax.broadcasted_iota(jnp.int32, (nf, 128), 1), count)
    hot = jnp.concatenate(
        [
            jnp.where(blocks[pl.ds(6 + c, nf, stride=8), :] == lanes.astype(F32), 1.0, 0.0)
            for c in (0, 1, 0, 1)
        ],
        axis=0,
    ).astype(BF16)
    within, outside = [], []
    for t in range(3):
        came = jnp.concatenate([blocks[pl.ds(c * 3 + t, nf, stride=8), :] for c in range(2)], axis=0)
        placed = mm(jnp.concatenate(split(came.T), axis=1), hot)
        woven = mm(weave[...], jnp.concatenate(split(placed), axis=0))
        woven = woven.reshape(2, 2, 8, 8, 128)
        within += [woven[0, 0], woven[0, 1]]
        outside += [woven[1, 0], woven[1, 1]]

    z = lax.broadcasted_iota(jnp.int32, (8, 128), 0)
    q = lax.broadcasted_iota(jnp.int32, (8, 128), 1) // count
    bottom, top, zeven = z == 0, z == 7, lax.rem(z, 2) == 0
    zodd = jnp.logical_not(zeven)
    first, final = q == 0, q == 3

    def choose(values, shift, y):
        out = values[shift + 3][y]
        for i in (2, 1, 0):
            out = jnp.where(q == i, values[shift + i][y], out)
        return out

    def along_x(values, r, y):
        if r == 0:
            return 0.25 * choose(values, 0, y) + 0.75 * choose(values, 1, y)
        return 0.75 * choose(values, 1, y) + 0.25 * choose(values, 2, y)

    def between(values, j):
        low = j // 2
        return (
            0.75 * values[low] + 0.25 * values[low + 1]
            if j % 2 == 0
            else 0.25 * values[low] + 0.75 * values[low + 1]
        )

    scale = 1.0 / (6.0 + SCREEN * FINE_STEP * FINE_STEP)
    layers, rims, states, force = {}, {}, {}, {}
    for r in range(2):
        plane = [along_x(within, r, y) for y in range(6)]
        for jy in range(10):
            value = between(plane, jy)
            if 1 <= jy <= 8:
                states[r, jy - 1] = value
            else:
                rims[r, jy] = value
        plane = [along_x(outside, r, y) for y in range(6)]
        for jy in range(1, 9):
            layers[r, jy - 1] = between(plane, jy)
    ends = (
        [0.75 * within[0][y] + 0.25 * within[1][y] for y in range(6)],
        [0.25 * within[4][y] + 0.75 * within[5][y] for y in range(6)],
    )
    keys = [(r, y) for r in range(2) for y in range(8)]
    sides = {
        (r, y): jnp.where(first if r == 0 else final, between(ends[r], y + 1), 0.0) for r, y in keys
    }
    needs[0].wait()
    for r, y in keys:
        ghost = layers[r, y] + sides[r, y]
        if y == 0:
            ghost = ghost + rims[r, 0]
        if y == 7:
            ghost = ghost + rims[r, 9]
        force[r, y] = (OMEGA * scale) * (ghost - FINE_STEP * FINE_STEP * packed[0, r, y])

    copy_in.wait()
    copy_out.start()

    def beside(old, r, y):
        other = old[1 - r, y]
        if r == 0:
            return other, jnp.where(first, 0.0, pltpu.roll(other, count, 1))
        return other, jnp.where(final, 0.0, pltpu.roll(other, 128 - count, 1))

    weight = OMEGA * scale
    from_below = jnp.where(bottom, 0.0, weight)
    from_above = jnp.where(top, 0.0, weight)
    from_left = jnp.where(first, 0.0, weight)
    from_right = jnp.where(final, 0.0, weight)

    def sweep(_, carry):
        old = dict(zip(keys, carry))
        for colour in (0, 1):
            new = {}
            for r, y in keys:
                v = old[r, y]
                other = old[1 - r, y]
                far = pltpu.roll(other, count if r == 0 else 128 - count, 1)
                near = other
                if y > 0:
                    near = near + old[r, y - 1]
                if y < 7:
                    near = near + old[r, y + 1]
                value = ((1.0 - OMEGA) * v + force[r, y]) + weight * near
                value = value + (from_below * pltpu.roll(v, 1, 0) + from_above * pltpu.roll(v, 7, 0))
                value = value + (from_left if r == 0 else from_right) * far
                mask = zeven if (r + y + colour) % 2 == 0 else zodd
                new[r, y] = jnp.where(mask, value, v)
            old = new
        return tuple(old[k] for k in keys)

    out = lax.fori_loop(0, SWEEPS, sweep, tuple(states[k] for k in keys))
    states = dict(zip(keys, out))

    def spill(target, r, y, value):
        for i in range(groups):
            target[2 * i + r, y] = value[:, count * i : count * (i + 1)]

    copies = [pltpu.make_async_copy(fine, fine_h, sems.at[2])] + [
        pltpu.make_async_copy(moved.at[v], moved_h.at[v], sems.at[3 + v]) for v in range(5)
    ]
    for r, y in keys:
        spill(fine, r, y, states[r, y])
    copies[0].start()

    needs[1].wait()
    for r, y in keys:
        spill(moved.at[0], r, y, packed[4, r, y])
    copies[1].start()
    step = COURANT * FINE_STEP / most[pl.ds(0, 1), :]
    work = {}
    for n in range(3):
        for r, y in keys:
            v = states[r, y]
            if n == 0:
                other, far = beside(states, r, y)
                far = far + sides[r, y]
                pull = far - other if r == 0 else other - far
            elif n == 1:
                down = states[r, y - 1] if y > 0 else rims[r, 0]
                up = states[r, y + 1] if y < 7 else rims[r, 9]
                pull = down - up
            else:
                layer = layers[r, y]
                pull = jnp.where(bottom, layer, pltpu.roll(v, 1, 0)) - jnp.where(top, layer, pltpu.roll(v, 7, 0))
            spill(moved.at[1 + n], r, y, packed[5 + n, r, y] + step * packed[0, r, y] * pull)
            part = packed[1 + n, r, y] * pull
            work[r, y] = part if n == 0 else work[r, y] + part
        copies[2 + n].start()
    for r, y in keys:
        spill(moved.at[4], r, y, packed[8, r, y] + step * work[r, y])
    copies[5].start()
    for c in copies:
        c.wait()
    copy_out.wait()


def root_call(ghost, rho, fluid, nf, ng):
    cx, cy, nz = rho.shape
    kz = nz // ng
    ny = ng * cy
    count = fluid.shape[-1]
    tab = tables(nf, ng, cx, cy, nz)
    consts = [jnp.asarray(tab[n]) for n in NAMES]
    vm = lambda shape, dtype=F32: pltpu.VMEM(shape, dtype)
    anyspace = pl.BlockSpec(memory_space=pl.ANY)
    vspace = pl.BlockSpec(memory_space=pltpu.VMEM)
    dma = pltpu.SemaphoreType.DMA
    local = {n: tab[n].shape for n in NAMES}
    local["inv"] = local["inv"][1:]
    local["pair"] = local["pair"][2:]
    limit = 56 * 1024 * 1024
    potential, blocks, most, packed = pl.pallas_call(
        functools.partial(root_kernel, (nf, ng, cx, cy, nz)),
        out_shape=(
            jax.ShapeDtypeStruct((cx, cy, nz), F32),
            jax.ShapeDtypeStruct((nf * 8, 128), F32),
            jax.ShapeDtypeStruct((8, 128), F32),
            jax.ShapeDtypeStruct((9, 2, 8, 8, 128), F32),
        ),
        in_specs=[pl.BlockSpec(memory_space=pltpu.SMEM)] + [anyspace] * (2 + len(NAMES)),
        out_specs=(anyspace,) * 4,
        scratch_shapes=[vm((cx, cy, nz))]
        + [vm(local[n], consts[i].dtype) for i, n in enumerate(NAMES)]
        + [
            vm(fluid.shape), vm((5, 12, 12, 8, count)),
            vm((cx, cy, nz)),
            vm((2, 128, nz)),
            vm((cx, 8, nz)),
            vm((cx + 2, cy + 16, nz)),
            vm((cx, kz, ny)),
            vm((2, nz, 128)), vm((ng, 2, kz, 128)),
            vm((nf * 8, 128)), vm((nf * 8, 128)),
            vm((nf * 8, 128)), vm((nf * 8, 128)),
            vm((ng, 2, kz, 128)), vm((2, ng, kz, 128)),
            vm((nf * 8, 128)), vm((8, 128)),
            vm((2 * nf, 8, 128)), vm((nf, 8, 128)),
            vm((5, 8, 8, count)),
            vm((5, 8, 8, 8, count)), vm((9, 2, 8, 8, 128)),
            dma((18,)), dma, dma, dma, dma,
            dma((2,)), dma((2,)), dma((2,)), dma((2,)), dma((2,)),
        ],
        compiler_params=pltpu.CompilerParams(
            collective_id=0, has_side_effects=True, vmem_limit_bytes=limit
        ),
    )(ghost, rho, fluid, *consts)
    fine, moved, potential = pl.pallas_call(
        patch_kernel,
        out_shape=(
            jax.ShapeDtypeStruct((8, 8, 8, count), F32),
            jax.ShapeDtypeStruct((5, 8, 8, 8, count), F32),
            jax.ShapeDtypeStruct((cx, cy, nz), F32),
        ),
        in_specs=[vspace, vspace, anyspace, anyspace, vspace],
        out_specs=(anyspace, anyspace, anyspace),
        scratch_shapes=[
            vm((8, 8, 8, count)), vm((5, 8, 8, 8, count)), vm((9, 2, 8, 8, 128)), vm((cx, cy, nz)), dma((10,)),
        ],
        compiler_params=pltpu.CompilerParams(vmem_limit_bytes=limit),
    )(blocks, most, packed, potential, jnp.asarray(tab["weave"]))
    return potential, fine, moved


def per_device(root_density, patch_fluid, ghost_list):
    nf = lax.axis_size("fft")
    ng = lax.axis_size("grp")
    return root_call(ghost_list[:, 0], root_density, patch_fluid, nf, ng)


def solution(mesh):
    return jax.shard_map(
        per_device,
        mesh=mesh,
        in_specs=(
            P("fft", "grp", None),
            P(None, None, None, None, ("fft", "grp")),
            P(None, ("fft", "grp"), None),
        ),
        out_specs=(
            P("fft", "grp", None),
            P(None, None, None, ("fft", "grp")),
            P(None, None, None, None, ("fft", "grp")),
        ),
        check_vma=False,
    )
```

```python
import functools

import jax
import jax.numpy as jnp
import ml_dtypes
import numpy as np
from jax import lax
from jax.experimental import pallas as pl
from jax.experimental.pallas import tpu as pltpu
from jax.sharding import PartitionSpec as P

SWEEPS = 8
GAMMA = 5.0 / 3.0
SCREEN = 0.0006
OMEGA = 1.5
COURANT = 0.4
FINE_STEP = 0.5
F32 = jnp.float32
BF16 = jnp.bfloat16


def sine(count):
    index = np.arange(1, count + 1)
    return np.sqrt(2.0 / (count + 1)) * np.sin(
        np.pi * (np.outer(index, index) % (2 * (count + 1))) / (count + 1)
    )


def eigen(count):
    return 4.0 * np.sin(np.pi * np.arange(1, count + 1) / (2 * (count + 1))) ** 2


def halves(table):
    high = table.astype(ml_dtypes.bfloat16)
    low = (table - high.astype(np.float64)).astype(ml_dtypes.bfloat16)
    return np.stack([high, low])


@functools.lru_cache(None)
def tables(nf, ng, cx, cy, nz):
    ny = ng * cy
    kz = nz // ng
    sz, sy, sx, full = sine(nz), sine(cy), sine(cx), sine(ny)
    lam = eigen(cy)[:, None] + eigen(nz)[None, :] + SCREEN
    steps = [1.0 / (2.0 + lam)]
    for _ in range(1, cx // 2):
        steps.append(1.0 / (2.0 + lam - steps[-1]))
    steps.append(1.0 / (1.0 - steps[-1] ** 2))
    edge = np.zeros((ng, 2, ny))
    wide = np.zeros((ng, 128, ny))
    back = np.zeros((ng, 128, ny))
    for d in range(ng):
        if d > 0:
            edge[d, 0] = full[d * cy - 1]
        if d < ng - 1:
            edge[d, 1] = full[(d + 1) * cy]
        wide[d, :cy] = sy @ full[d * cy : (d + 1) * cy]
        back[d, :cy] = wide[d, :cy]
        back[d, cy + cx] = edge[d, 0]
        back[d, cy + cx + 1] = edge[d, 1]
    repeated = np.repeat(edge.reshape(2 * ng, ny), kz, axis=0)
    denom = (
        eigen(cx)[None, :, None, None]
        + eigen(nz).reshape(ng, 1, kz, 1)
        + eigen(ny)[None, None, None, :]
        + SCREEN
    )
    phi = 2.0 * np.arcsinh(np.sqrt(eigen(ny)[None, :] + eigen(nz)[:, None] + SCREEN) / 2.0)

    def ratio(m, n):
        return np.exp(-(n - m) * phi) * np.expm1(-2 * m * phi) / np.expm1(-2 * n * phi)

    pair = np.zeros((ng, nf, 2, 8, 128))
    for i, values in enumerate((ratio(cx - 1, cx), ratio(1, cx))):
        pair[:, :, i, :3] = values.reshape(ng, nf, 3, 128)
    spread = np.zeros((10, 6))
    for j in range(10):
        at = j / 2 + 0.25
        low = int(np.floor(at))
        spread[j, low] += 1 - (at - low)
        spread[j, low + 1] += at - low
    inner = np.zeros((8, 8))
    inner[:, :6] = spread[1:9]
    outer = np.zeros((8, 8))
    outer[0, :6] = spread[0]
    outer[7, :6] = spread[9]
    weave = np.concatenate([np.kron(np.eye(16), inner), np.kron(np.eye(16), outer)])
    lanes = np.arange(128)
    fold = ((lanes[:, None] + 1) % 8 == lanes[None, :] % 8).astype(np.float64)
    column = np.broadcast_to(sy[0][:, None], (cy, 128))
    as32 = lambda t: np.ascontiguousarray(t, dtype=np.float32)
    szh, szl = halves(sz)
    syh, syl = halves(sy)
    wide_x = np.zeros((cx, 32))
    wide_x[:, :cx] = sx
    xh, xl = halves(np.repeat(wide_x, kz, axis=0))
    sx_rows = np.block([[xh, xh], [xl, np.zeros_like(xl)]]).astype(ml_dtypes.bfloat16)
    tall_x = np.zeros((32, cx * kz))
    tall_x[:cx] = np.repeat(sx, kz, axis=1)
    sx_sums = np.concatenate(halves(tall_x))
    return dict(
        sz=np.block([[szh, szl], [szh, np.zeros_like(szh)]]).astype(ml_dtypes.bfloat16),
        sy=np.block([[syh, syh], [syl, np.zeros_like(syl)]]).astype(ml_dtypes.bfloat16),
        sx=sx_rows,
        sxt=sx_sums,
        steps=as32(np.stack(steps)),
        wide=halves(wide.reshape(ng * 128, ny)),
        back=halves(np.ascontiguousarray(back.reshape(ng * 128, ny).T)),
        edge=halves(repeated),
        edget=halves(np.ascontiguousarray(repeated.T)),
        inv=as32(1.0 / denom),
        pair=as32(pair),
        weave=np.concatenate([weave, weave], axis=1).astype(ml_dtypes.bfloat16),
        fold=np.concatenate([fold, fold]).astype(ml_dtypes.bfloat16),
        column=as32(column),
    )


NAMES = (
    "sz", "sy", "sx", "sxt", "steps", "wide", "back", "edge", "edget", "inv", "pair", "fold", "column",
)


def split(value):
    high = value.astype(BF16)
    return high, (value - high.astype(F32)).astype(BF16)


def mm(a, b):
    return jnp.dot(a, b, preferred_element_type=F32)


def dot_right(value, high, low):
    rows = value.shape[0]
    a, b = split(value)
    main = mm(jnp.concatenate([a, b], axis=0), high)
    return main[:rows] + (main[rows:] + mm(a, low))


def dot_left(both, value):
    rows = both.shape[0] // 2
    a, b = split(value)
    out = mm(both, jnp.concatenate([a, b], axis=0))
    return out[:rows] + out[rows:]


def root_kernel(
    cfg,
    ghost, rho, fluid_h,
    sz_h, sy_h, sx_h, sxt_h, steps_h, wide_h, back_h, edge_h, edget_h, inv_h, pair_h, fold_h, column_h,
    pot_h, blocks_h, most_h, packed_h,
    src, sz, sy, sx, sxt, steps, wide, back, edge, edget, inv, pair, fold, column, fluid, prim,
    block, solved, part, grid, hfield,
    s1, r1, s2, r2, s3, r3, s4, r4, s6, most_out, chain, mults, last_face, change, packed,
    tsem, osem, psem, bsem, msem, x1, x2, x3, x4, x6,
):
    nf, ng, cx, cy, nz = cfg
    kz = nz // ng
    ny = ng * cy
    half = cx // 2
    f = lax.axis_index("fft")
    g = lax.axis_index("grp")

    quarter = cx // 4
    early = [
        (f"rho{i}", rho.at[pl.ds(quarter * i, quarter)], src.at[pl.ds(quarter * i, quarter)]) for i in range(4)
    ]
    early[1:1] = [("sz", sz_h, sz), ("sy", sy_h, sy)]
    early += [("steps", steps_h, steps), ("column", column_h, column), ("pair", pair_h.at[g, f], pair)]
    late = [
        ("wide", wide_h, wide), ("sx", sx_h, sx), ("edge", edge_h, edge), ("inv", inv_h.at[g], inv),
        ("fluid", fluid_h, fluid), ("edget", edget_h, edget), ("sxt", sxt_h, sxt), ("back", back_h, back), ("fold", fold_h, fold),
    ]
    loads = {
        name: pltpu.make_async_copy(a, b, tsem.at[i]) for i, (name, a, b) in enumerate(early + late)
    }
    for name, _, _ in early:
        loads[name].start()

    ny_chips = 4 if nf % 4 == 0 else 1
    nz_chips = nf // ny_chips
    barrier = pltpu.get_barrier_semaphore()

    def grp_partner(k):
        return lax.rem(g + k, ng)

    def fft_partner(k):
        a, b = k // ny_chips, lax.rem(k, ny_chips)
        dz = nz_chips // 2 + ((a + 1) // 2) * (1 - 2 * lax.rem(a, 2))
        dy = ny_chips // 2 + ((b + 1) // 2) * (1 - 2 * lax.rem(b, 2))
        return lax.rem(f // ny_chips + dz, nz_chips) * ny_chips + lax.rem(lax.rem(f, ny_chips) + dy, ny_chips)

    ways = {"grp": (1, ng, grp_partner, g), "fft": (0, nf - 1, fft_partner, f)}

    def hello(axis):
        begin, end, partner, _ = ways[axis]

        def body(k, _):
            pl.semaphore_signal(
                barrier, inc=1, device_id={axis: partner(k)}, device_id_type=pl.DeviceIdType.MESH
            )
            return 0

        lax.fori_loop(begin, end, body, 0, unroll=True)

    hello("fft")
    hello("grp")

    sub = lax.broadcasted_iota(jnp.int32, (8, 128), 0)
    even = lax.rem(sub, 2) == 0

    loads["sz"].wait()
    loads["sy"].wait()

    def forward(i, _):
        rows = src[pl.ds(2 * i, 2)].reshape(2 * cy, nz)
        a, b = split(rows)
        both = mm(jnp.concatenate([a, b], axis=1), sz[...])
        both = both[:, :nz] + both[:, nz:]
        pair_x = jnp.concatenate([both[:cy], both[cy:]], axis=1)
        out = dot_left(sy[...], pair_x)
        block[2 * i] = out[:, :nz]
        block[2 * i + 1] = out[:, nz:]
        return 0

    for part_of in range(4):
        loads[f"rho{part_of}"].wait()
        if part_of == 3:
            for name, _, _ in late:
                loads[name].start()
        lax.fori_loop(part_of * half // 4, (part_of + 1) * half // 4, forward, 0, unroll=True)

    loads["steps"].wait()
    loads["column"].wait()

    def solve(fetch, i):
        at = pl.ds(pl.multiple_of(16 * i, 16), 16)
        low, high = [], []
        for j in range(half):
            m = steps[j, at, :]
            a, b = fetch(j, at), fetch(cx - 1 - j, at)
            if j == 0:
                low.append(-m * a)
                high.append(-m * b)
            else:
                low.append(m * (low[-1] - a))
                high.append(m * (high[-1] - b))
        m, scale = steps[half - 1, at, :], steps[half, at, :]
        a, b = low[-1], high[-1]
        low[-1] = (a + m * b) * scale
        high[-1] = (b + m * a) * scale
        for j in range(half - 2, -1, -1):
            m = steps[j, at, :]
            low[j] = low[j] + m * low[j + 1]
            high[j] = high[j] + m * high[j + 1]
        return at, low + high[::-1]

    part[...] = jnp.zeros_like(part)

    def first(i, _):
        at, values = solve(lambda x, at: block[x, at, :], i)
        col = column[at, :]
        for x in range(cx):
            v = values[x] * col
            part[x] += v[:8] + v[8:]
        solved[0, at, :] = values[0]
        solved[1, at, :] = values[cx - 1]
        return 0

    lax.fori_loop(0, cy // 16, first, 0, unroll=2)
    sums = part[...]
    sign = jnp.where(even, 1.0, -1.0)
    edges = (jnp.sum(sums, axis=1), jnp.sum(sums * sign[None], axis=1))
    for e in range(2):
        solved[e, pl.ds(cy, cx), :] = edges[e]
        solved[e, pl.ds(cy + cx, 8), :] = jnp.zeros((8, 128), F32)
        s1[e] = solved[e].T


    cells = pl.ds(2, 8)

    def cell_values(cons):
        dens = cons[0]
        over = 1.0 / dens
        vel = [m * over for m in cons[1:4]]
        kinetic = 0.5 * (cons[1] * vel[0] + cons[2] * vel[1] + cons[3] * vel[2])
        return [dens] + vel + [(GAMMA - 1.0) * (cons[4] - kinetic)]

    def sound(dens, pres):
        return jnp.sqrt(GAMMA * pres) * lax.rsqrt(dens)

    def make_cells(x, _):
        for y in range(12):
            w = cell_values([fluid[v, x, y, cells, :] for v in range(5)])
            for v in range(5):
                prim[v, x, y] = w[v]
        return 0

    def top_speed():
        def body(x, top):
            for y in range(2, 10):
                w = [prim[v, x + 2, y] for v in range(5)]
                fast = jnp.maximum(jnp.maximum(jnp.abs(w[1]), jnp.abs(w[2])), jnp.abs(w[3]))
                top = jnp.maximum(top, fast + sound(w[0], w[4]))
            return top
        return jnp.max(lax.fori_loop(0, 8, body, jnp.zeros((8, fluid.shape[-1]), F32)))

    def states(before, here, after):
        low, high = [], []
        for a, b, c in zip(before, here, after):
            p, q = b - a, c - b
            half_slope = 0.5 * (
                jnp.maximum(0.0, jnp.minimum(p, q)) + jnp.minimum(0.0, jnp.maximum(p, q))
            )
            low.append(b - half_slope)
            high.append(b + half_slope)
        return low, high

    def side(w, n):
        dens, vel, pres = w[0], w[1:4], w[4]
        energy = pres * (1.0 / (GAMMA - 1.0)) + 0.5 * dens * (
            vel[0] * vel[0] + vel[1] * vel[1] + vel[2] * vel[2]
        )
        mom = [dens * v for v in vel]
        flux = [mom[n]] + [mom[n] * v for v in vel] + [(energy + pres) * vel[n]]
        flux[1 + n] = flux[1 + n] + pres
        return [dens] + mom + [energy], flux, jnp.abs(vel[n]) + sound(dens, pres)

    def face(left, right, n):
        cl, fl, al = side(left, n)
        cr, fr, ar = side(right, n)
        top = jnp.maximum(al, ar)
        return [0.5 * ((a + b) - top * (d - c)) for a, b, c, d in zip(fl, fr, cl, cr)]

    def sweep_line(get, put, n):
        w = [get(0), get(1), get(2)]
        _, high = states(*w)
        flux = None
        for i in range(2, 11):
            w = [w[1], w[2], get(i + 1)]
            low, high_next = states(*w)
            now = face(high, low, n)
            if flux is not None:
                put(i - 3, [b - a for a, b in zip(flux, now)])
            flux, high = now, high_next

    def lines_x(y, _):
        def get(i):
            return [prim[v, i, y + 2] for v in range(5)]

        def put(i, values):
            for v in range(5):
                change[v, i, y] = values[v]

        sweep_line(get, put, 0)
        return 0

    def lines_y(x, _):
        def get(i):
            return [prim[v, x + 2, i] for v in range(5)]

        def put(i, values):
            for v in range(5):
                change[v, x, i] += values[v]

        sweep_line(get, put, 1)
        return 0

    def last_faces(x, _):
        w = [
            cell_values([fluid[v, x + 2, cells, k, :] for v in range(5)]) for k in (8, 9, 10, 11)
        ]
        _, high = states(w[0], w[1], w[2])
        low, _ = states(w[1], w[2], w[3])
        flux = face(high, low, 2)
        for v in range(5):
            last_face[v, x] = flux[v]
        return 0

    def lines_z(x, _):
        row = lax.broadcasted_iota(jnp.int32, (8, fluid.shape[-1]), 0)
        for y in range(8):
            w = [
                cell_values([fluid[v, x + 2, y + 2, pl.ds(k, 8), :] for v in range(5)]) if k != 2
                else [prim[v, x + 2, y + 2] for v in range(5)]
                for k in range(4)
            ]
            _, high = states(w[0], w[1], w[2])
            low, _ = states(w[1], w[2], w[3])
            flux = face(high, low, 2)
            for v in range(5):
                after = jnp.where(row == 7, last_face[v, x, pl.ds(y, 1), :], pltpu.roll(flux[v], 7, 0))
                change[v, x, y] += after - flux[v]
        return 0

    pl.semaphore_wait(barrier, ng + nf - 2)

    def send(axis, source, target, every, sems):
        begin, end, partner, pos = ways[axis]

        def body(k, _):
            to = partner(k)
            pltpu.make_async_remote_copy(
                source(to), target(pos), sems.at[0], sems.at[1], device_id={axis: to},
                device_id_type=pl.DeviceIdType.MESH,
            ).start()
            return 0

        lax.fori_loop(begin, end, body, 0, unroll=True)

    def whole(axis, source, target, every, sems):
        return pltpu.make_async_remote_copy(
            every, every, sems.at[0], sems.at[1], device_id={axis: ways[axis][2](1)},
            device_id_type=pl.DeviceIdType.MESH,
        )

    def receive(*exchange):
        whole(*exchange).wait_recv()

    def sent(*exchange):
        whole(*exchange).wait_send()

    slice1 = lambda d: s1.at[:, pl.ds(pl.multiple_of(d * kz, kz), kz), :]
    ex1 = ("grp", slice1, lambda d: r1.at[d], r1.at[pl.ds(0, ng - 1)], x1)
    send(*ex1)
    r1[g] = s1[:, pl.ds(pl.multiple_of(g * kz, kz), kz), :]

    loads["pair"].wait()
    ca, cb = pair[0], pair[1]
    ca2, cb2 = ca * ca, cb * cb

    def coefficients(i, m):
        m0 = 1.0 / (1.0 - ca2 * m)
        mults[2 * i] = m0
        m1 = 1.0 / (1.0 - cb2 * m0)
        mults[2 * i + 1] = m1
        return m1

    lax.fori_loop(0, nf // 2, coefficients, jnp.zeros((8, 128), F32))
    loads["fluid"].wait()
    lax.fori_loop(0, 12, make_cells, 0)
    most = jnp.full((1, 128), top_speed(), F32)
    loads["wide"].wait()
    loads["sx"].wait()
    loads["edge"].wait()
    loads["inv"].wait()
    receive(*ex1)

    main = jnp.concatenate([r1[d].reshape(2 * kz, 128) for d in range(ng)], axis=1)
    main = dot_right(main, wide[0], wide[1])
    across = r1[...].reshape(ng * 2 * kz, 128).T
    edge_x = across[cy : cy + cx]
    edge_k = dot_left(sx[...], across[cy : cy + 32]).reshape(cx, kz, ng * 2 * kz)
    wide_lane = ng * 2 * kz
    diag = (
        lax.rem(lax.broadcasted_iota(jnp.int32, (kz, wide_lane), 1), kz)
        == lax.broadcasted_iota(jnp.int32, (kz, wide_lane), 0)
    )
    sums = [jnp.zeros((kz, ny), F32), jnp.zeros((kz, ny), F32)]
    first_row = [float(v) for v in sine(cx)[0]]
    group = cx // 2
    for x0 in range(0, cx, group):
        lhs = jnp.where(diag[None], edge_k[x0 : x0 + group], 0.0).reshape(group * kz, wide_lane)
        out = dot_right(lhs, edge[0], edge[1])
        for x in range(x0, x0 + group):
            hd = out[(x - x0) * kz : (x - x0 + 1) * kz] * inv[x]
            hfield[x] = hd
            sums[x % 2] = sums[x % 2] + first_row[x] * hd
    rows = (main[:kz] + (sums[0] + sums[1]), main[kz:] + (sums[0] - sums[1]))
    for row in range(2):
        for j in range(6):
            s2[pl.ds((j // 3) * 8 + row * 3 + j % 3, kz, stride=16), :] = rows[row][:, j * 128 : (j + 1) * 128]
    for r in (6, 7):
        s2[pl.ds(r, nf, stride=8), :] = jnp.broadcast_to(most, (nf, 128))

    most_rows = lambda ref: ref.at[pl.ds(0, (nf - 1) * 8), :]
    tile = lambda ref: lambda d: ref.at[pl.ds(pl.multiple_of(d * 8, 8), 8), :]
    ex2 = ("fft", tile(s2), tile(r2), most_rows(r2), x2)
    send(*ex2)
    mine = pl.ds(pl.multiple_of(f * 8, 8), 8)
    r2[mine, :] = s2[mine, :]
    lax.fori_loop(0, 8, lines_x, 0)
    lax.fori_loop(0, 8, lines_y, 0)
    receive(*ex2)
    most = jnp.max(r2[pl.ds(6, nf, stride=8), :], axis=0, keepdims=True)

    last = jnp.zeros((8, 128), F32)

    def right_sides(d):
        msg = r2[8 * d : 8 * d + 8, :]
        other = pltpu.roll(msg, 5, 0)
        return msg - cb * other, other - cb * msg

    up = down = last
    for d in range(nf // 2):
        m0, m1 = mults[2 * d], mults[2 * d + 1]
        ma, mb = m0 * ca, m1 * cb
        e = nf - 1 - d
        p, q = right_sides(d)
        up = m0 * p + ma * up
        chain[2 * d] = up
        up = m1 * q + mb * up
        chain[2 * d + 1] = up
        p, q = right_sides(e)
        down = m0 * q + ma * down
        chain[2 * e + 1] = down
        down = m1 * p + mb * down
        chain[2 * e] = down
    link = mults[nf - 1] * ca
    over = 1.0 / (1.0 - link * link)
    up, down = (up + link * down) * over, (down + link * up) * over
    chain[nf - 1] = up
    chain[nf] = down
    for j in range(nf - 2, -1, -1):
        m = mults[j] * (cb if j % 2 == 0 else ca)
        up = chain[j] + m * up
        chain[j] = up
        down = chain[2 * nf - 1 - j] + m * down
        chain[2 * nf - 1 - j] = down
    for d in range(nf):
        left = chain[2 * d - 1] if d > 0 else last
        right = chain[2 * d + 2] if d < nf - 1 else last
        s3[8 * d : 8 * d + 8, :] = jnp.where(sub < 3, left, pltpu.roll(right, 3, 0))

    ex3 = ("fft", tile(s3), tile(r3), most_rows(r3), x3)
    send(*ex3)
    r3[mine, :] = s3[mine, :]
    loads["edget"].wait()
    loads["back"].wait()
    lax.fori_loop(0, 8, last_faces, 0)
    lax.fori_loop(0, 8, lines_z, 0)
    receive(*ex3)
    around = [
        jnp.concatenate(
            [r3[pl.ds((j // 3) * 8 + row * 3 + j % 3, kz, stride=16), :] for j in range(6)], axis=1
        )
        for row in range(2)
    ]
    out_rows = dot_right(jnp.concatenate(around, axis=0), back[0], back[1])
    mixed = (around[0] + around[1], around[0] - around[1])
    corr = []
    for x0 in range(0, cx, group):
        lhs = jnp.concatenate(
            [hfield[x] + (first_row[x] * inv[x]) * mixed[x % 2] for x in range(x0, x0 + group)], axis=0
        )
        out = dot_right(lhs, edget[0], edget[1])
        corr.append(jnp.where(diag[None], out.reshape(group, kz, wide_lane), 0.0).reshape(group * kz, wide_lane))
    loads["sxt"].wait()
    a, b = split(jnp.concatenate(corr, axis=0))
    main = mm(sxt[...], a)
    corr = (main[:32] + (main[32:] + mm(sxt[pl.ds(0, 32), :], b)))[:cx]
    blank = jnp.zeros((cx, kz), F32)
    from_left = jnp.concatenate([blank, edge_x[:, :-kz]], axis=1)
    from_right = jnp.concatenate([edge_x[:, kz:], blank], axis=1)
    second = lax.rem(lax.broadcasted_iota(jnp.int32, (cx, wide_lane), 1) // kz, 2) == 1
    sides = corr + jnp.where(second, from_right, from_left)
    sides = jnp.concatenate(
        [jnp.zeros((cy, wide_lane), F32), sides, jnp.zeros((128 - cy - cx, wide_lane), F32)], axis=0
    ).T
    sides = jnp.where(
        lax.broadcasted_iota(jnp.int32, (wide_lane, 128), 1) == 127, jnp.broadcast_to(most, (wide_lane, 128)), sides
    )
    for d in range(ng):
        s4[d] = (out_rows[:, 128 * d : 128 * d + 128] + sides[2 * kz * d : 2 * kz * (d + 1)]).reshape(2, kz, 128)

    ex4 = ("grp", lambda d: s4.at[d], lambda d: r4.at[:, d], r4.at[:, pl.ds(0, ng - 1)], x4)
    send(*ex4)
    r4[:, g] = s4[g]
    sent(*ex1)
    sent(*ex2)
    sent(*ex3)
    receive(*ex4)
    for e in range(2):
        solved[e] = r4[e].reshape(nz, 128).T
    most_out[...] = jnp.full((8, 128), jnp.max(solved[0, pl.ds(127, 1), :]), F32)
    copy_most = pltpu.make_async_copy(most_out, most_h, msem)
    copy_most.start()

    for x in range(cx):
        va = solved[0, pl.ds(cy + x, 1), :]
        vb = solved[1, pl.ds(cy + x, 1), :]
        part[x] = jnp.where(even, va + vb, va - vb)

    def second_solve(i, _):
        def fetch(x, at):
            w = part[x]
            value = block[x, at, :] - column[at, :] * jnp.concatenate([w, w], axis=0)
            if x == 0:
                value = value - solved[0, at, :]
            if x == cx - 1:
                value = value - solved[1, at, :]
            return value

        at, values = solve(fetch, i)
        for x in range(cx):
            block[x, at, :] = values[x]
        return 0

    lax.fori_loop(0, cy // 16, second_solve, 0, unroll=2)

    def inverse_z(rows):
        a, b = split(rows)
        both = mm(jnp.concatenate([a, b], axis=1), sz[...])
        return both[:, :nz] + both[:, nz:]

    def backward(i, _):
        pair_x = jnp.concatenate([block[2 * i], block[2 * i + 1]], axis=1)
        out = dot_left(sy[...], pair_x)
        out = inverse_z(jnp.concatenate([out[:, :nz], out[:, nz:]], axis=0))
        grid[2 * i + 1, pl.ds(8, cy), :] = out[:cy]
        grid[2 * i + 2, pl.ds(8, cy), :] = out[cy:]
        return 0

    lax.fori_loop(0, half, backward, 0, unroll=True)
    copy_out = pltpu.make_async_copy(grid.at[pl.ds(1, cx), pl.ds(8, cy), :], pot_h, osem)
    copy_out.start()
    pair_x = jnp.concatenate([solved[0, :cy], solved[1, :cy]], axis=1)
    out = dot_left(sy[...], pair_x)
    rest = jnp.concatenate([out[:, :nz], out[:, nz:], solved[0, cy:], solved[1, cy:]], axis=0)
    rest = inverse_z(rest)
    grid[0, pl.ds(8, cy), :] = rest[:cy]
    grid[cx + 1, pl.ds(8, cy), :] = rest[cy : 2 * cy]
    pad = 128 - cy
    for e in range(2):
        lines = rest[2 * cy + pad * e : 2 * cy + pad * (e + 1)]
        at = pl.ds(7 if e == 0 else 8 + cy, 1)
        for x in range(cx):
            grid[x + 1, at, :] = lines[x : x + 1]
    for e in range(2):
        lines = rest[2 * cy + pad * e : 2 * cy + pad * (e + 1)]
        for s in range(2):
            grid[(cx + 1) * e, pl.ds(7 if s == 0 else 8 + cy, 1), :] = lines[cx + s : cx + s + 1]

    loads["fold"].wait()
    per_y, per_z = cy // 4, nz // 4
    lanes8 = lax.broadcasted_iota(jnp.int32, (8, 128), 1)
    pick = (
        lax.broadcasted_iota(jnp.int32, (16, 128), 1) // 8 == lax.broadcasted_iota(jnp.int32, (16, 128), 0)
    )
    lane6 = lax.rem(lax.broadcasted_iota(jnp.int32, (6, 128), 1), 8)
    row6 = lax.broadcasted_iota(jnp.int32, (6, 128), 0)
    some = 4

    def gather(i, _):
        cut, odd = [], []
        for c in range(2 * some):
            code = jnp.maximum(ghost[0, 2 * some * i + c], 0)
            ix = code // (per_y * per_z)
            iy = lax.rem(code // per_z, per_y)
            iz = lax.rem(code, per_z)
            rows = grid[pl.ds(4 * ix, 6), pl.ds(7 + 4 * iy, 8), :]
            inside = (lanes8 >= 4 * iz - 1) & (lanes8 <= 4 * iz + 4) & (sub < 6)
            cut.append(jnp.where(inside[None], rows, 0.0).reshape(48, 128))
            odd.append(lax.rem(iz, 2))
        a, b = split(jnp.concatenate(cut, axis=0))
        out = mm(jnp.concatenate([a, b], axis=1), fold[...]).reshape(2 * some * 3, 16, 128)
        out = jnp.sum(jnp.where(pick[None], out, 0.0), axis=1)
        for k in range(some):
            d = some * i + k
            mini = out[6 * k : 6 * k + 6]
            turned = jnp.where(lane6 < 4, pltpu.roll(mini, 124, 1), pltpu.roll(mini, 4, 1))
            which = jnp.where(row6 < 3, odd[2 * k], odd[2 * k + 1])
            mini = jnp.where(which == 1, turned, mini)
            slots = [
                jnp.full((1, 128), ghost[1, 2 * d + c].astype(F32), F32) for c in range(2)
            ]
            s6[pl.ds(pl.multiple_of(8 * d, 8), 8), :] = jnp.concatenate([mini] + slots, axis=0)
        return 0

    lax.fori_loop(0, nf // some, gather, 0, unroll=2)

    ex6 = ("fft", tile(s6), tile(blocks_h), most_rows(blocks_h), x6)
    send(*ex6)
    copy_mine = pltpu.make_async_copy(s6.at[mine, :], blocks_h.at[mine, :], bsem)
    copy_mine.start()
    width = fluid.shape[-1]
    groups = 128 // width
    rate = COURANT / most_out[pl.ds(0, 1), pl.ds(0, width)]

    def pack(y, _):
        for r in range(2):
            at = [2 * i + r for i in range(groups)]
            cons = [[fluid[v, x + 2, y + 2, cells, :] for x in at] for v in range(5)]
            for v in range(4):
                packed[v, r, y] = jnp.concatenate(cons[v], axis=1)
            for v in range(5):
                packed[4 + v, r, y] = jnp.concatenate(
                    [c - rate * change[v, x, y] for c, x in zip(cons[v], at)], axis=1
                )
        return 0

    lax.fori_loop(0, 8, pack, 0)
    copy_packed = pltpu.make_async_copy(packed, packed_h, psem)
    copy_packed.start()
    sent(*ex4)
    copy_out.wait()
    copy_packed.wait()
    copy_most.wait()
    copy_mine.wait()
    sent(*ex6)
    receive(*ex6)


def patch_kernel(
    blocks, most, packed_h, pot_in, weave,
    fine_h, moved_h, pot_out,
    fine, moved, packed, hold, sems,
):
    count = fine.shape[-1]
    nf = blocks.shape[0] // 8
    copy_in = pltpu.make_async_copy(pot_in, hold, sems.at[0])
    needs = [
        pltpu.make_async_copy(packed_h.at[0], packed.at[0], sems.at[8]),
        pltpu.make_async_copy(packed_h.at[pl.ds(1, 8)], packed.at[pl.ds(1, 8)], sems.at[9]),
    ]
    needs[0].start()
    copy_in.start()
    needs[1].start()
    copy_out = pltpu.make_async_copy(hold, pot_out, sems.at[1])
    groups = 128 // count

    lanes = lax.rem(lax.broadcasted_iota(jnp.int32, (nf, 128), 1), count)
    hot = jnp.concatenate(
        [
            jnp.where(blocks[pl.ds(6 + c, nf, stride=8), :] == lanes.astype(F32), 1.0, 0.0)
            for c in (0, 1, 0, 1)
        ],
        axis=0,
    ).astype(BF16)
    within, outside = [], []
    for t in range(3):
        came = jnp.concatenate([blocks[pl.ds(c * 3 + t, nf, stride=8), :] for c in range(2)], axis=0)
        placed = mm(jnp.concatenate(split(came.T), axis=1), hot)
        woven = mm(weave[...], jnp.concatenate(split(placed), axis=0))
        woven = woven.reshape(2, 2, 8, 8, 128)
        within += [woven[0, 0], woven[0, 1]]
        outside += [woven[1, 0], woven[1, 1]]

    z = lax.broadcasted_iota(jnp.int32, (8, 128), 0)
    q = lax.broadcasted_iota(jnp.int32, (8, 128), 1) // count
    bottom, top, zeven = z == 0, z == 7, lax.rem(z, 2) == 0
    zodd = jnp.logical_not(zeven)
    first, final = q == 0, q == 3

    def choose(values, shift, y):
        out = values[shift + 3][y]
        for i in (2, 1, 0):
            out = jnp.where(q == i, values[shift + i][y], out)
        return out

    def along_x(values, r, y):
        if r == 0:
            return 0.25 * choose(values, 0, y) + 0.75 * choose(values, 1, y)
        return 0.75 * choose(values, 1, y) + 0.25 * choose(values, 2, y)

    def between(values, j):
        low = j // 2
        return (
            0.75 * values[low] + 0.25 * values[low + 1]
            if j % 2 == 0
            else 0.25 * values[low] + 0.75 * values[low + 1]
        )

    scale = 1.0 / (6.0 + SCREEN * FINE_STEP * FINE_STEP)
    layers, rims, states, force = {}, {}, {}, {}
    for r in range(2):
        plane = [along_x(within, r, y) for y in range(6)]
        for jy in range(10):
            value = between(plane, jy)
            if 1 <= jy <= 8:
                states[r, jy - 1] = value
            else:
                rims[r, jy] = value
        plane = [along_x(outside, r, y) for y in range(6)]
        for jy in range(1, 9):
            layers[r, jy - 1] = between(plane, jy)
    ends = (
        [0.75 * within[0][y] + 0.25 * within[1][y] for y in range(6)],
        [0.25 * within[4][y] + 0.75 * within[5][y] for y in range(6)],
    )
    keys = [(r, y) for r in range(2) for y in range(8)]
    sides = {
        (r, y): jnp.where(first if r == 0 else final, between(ends[r], y + 1), 0.0) for r, y in keys
    }
    needs[0].wait()
    for r, y in keys:
        ghost = layers[r, y] + sides[r, y]
        if y == 0:
            ghost = ghost + rims[r, 0]
        if y == 7:
            ghost = ghost + rims[r, 9]
        force[r, y] = (OMEGA * scale) * (ghost - FINE_STEP * FINE_STEP * packed[0, r, y])

    copy_in.wait()
    copy_out.start()
    needs[1].wait()

    def spill(target, r, y, value):
        for i in range(groups):
            target[2 * i + r, y] = value[:, count * i : count * (i + 1)]

    copies = [pltpu.make_async_copy(fine, fine_h, sems.at[2])] + [
        pltpu.make_async_copy(moved.at[v], moved_h.at[v], sems.at[3 + v]) for v in range(5)
    ]
    for r, y in keys:
        spill(moved.at[0], r, y, packed[4, r, y])
    copies[1].start()

    def beside(old, r, y):
        other = old[1 - r, y]
        if r == 0:
            return other, jnp.where(first, 0.0, pltpu.roll(other, count, 1))
        return other, jnp.where(final, 0.0, pltpu.roll(other, 128 - count, 1))

    weight = OMEGA * scale
    from_below = jnp.where(bottom, 0.0, weight)
    from_above = jnp.where(top, 0.0, weight)
    from_left = jnp.where(first, 0.0, weight)
    from_right = jnp.where(final, 0.0, weight)

    def sweep(_, carry):
        old = dict(zip(keys, carry))
        for colour in (0, 1):
            new = {}
            for r, y in keys:
                v = old[r, y]
                other = old[1 - r, y]
                far = pltpu.roll(other, count if r == 0 else 128 - count, 1)
                near = other
                if y > 0:
                    near = near + old[r, y - 1]
                if y < 7:
                    near = near + old[r, y + 1]
                value = ((1.0 - OMEGA) * v + force[r, y]) + weight * near
                value = value + (from_below * pltpu.roll(v, 1, 0) + from_above * pltpu.roll(v, 7, 0))
                value = value + (from_left if r == 0 else from_right) * far
                mask = zeven if (r + y + colour) % 2 == 0 else zodd
                new[r, y] = jnp.where(mask, value, v)
            old = new
        return tuple(old[k] for k in keys)

    out = lax.fori_loop(0, SWEEPS, sweep, tuple(states[k] for k in keys))
    states = dict(zip(keys, out))

    for r, y in keys:
        spill(fine, r, y, states[r, y])
    copies[0].start()

    step = COURANT * FINE_STEP / most[pl.ds(0, 1), :]
    work = {}
    for n in range(3):
        for r, y in keys:
            v = states[r, y]
            if n == 0:
                other, far = beside(states, r, y)
                far = far + sides[r, y]
                pull = far - other if r == 0 else other - far
            elif n == 1:
                down = states[r, y - 1] if y > 0 else rims[r, 0]
                up = states[r, y + 1] if y < 7 else rims[r, 9]
                pull = down - up
            else:
                layer = layers[r, y]
                pull = jnp.where(bottom, layer, pltpu.roll(v, 1, 0)) - jnp.where(top, layer, pltpu.roll(v, 7, 0))
            spill(moved.at[1 + n], r, y, packed[5 + n, r, y] + step * packed[0, r, y] * pull)
            part = packed[1 + n, r, y] * pull
            work[r, y] = part if n == 0 else work[r, y] + part
        copies[2 + n].start()
    for r, y in keys:
        spill(moved.at[4], r, y, packed[8, r, y] + step * work[r, y])
    copies[5].start()
    for c in copies:
        c.wait()
    copy_out.wait()


def root_call(ghost, rho, fluid, nf, ng):
    cx, cy, nz = rho.shape
    kz = nz // ng
    ny = ng * cy
    count = fluid.shape[-1]
    tab = tables(nf, ng, cx, cy, nz)
    consts = [jnp.asarray(tab[n]) for n in NAMES]
    vm = lambda shape, dtype=F32: pltpu.VMEM(shape, dtype)
    anyspace = pl.BlockSpec(memory_space=pl.ANY)
    vspace = pl.BlockSpec(memory_space=pltpu.VMEM)
    dma = pltpu.SemaphoreType.DMA
    local = {n: tab[n].shape for n in NAMES}
    local["inv"] = local["inv"][1:]
    local["pair"] = local["pair"][2:]
    limit = 56 * 1024 * 1024
    potential, blocks, most, packed = pl.pallas_call(
        functools.partial(root_kernel, (nf, ng, cx, cy, nz)),
        out_shape=(
            jax.ShapeDtypeStruct((cx, cy, nz), F32),
            jax.ShapeDtypeStruct((nf * 8, 128), F32),
            jax.ShapeDtypeStruct((8, 128), F32),
            jax.ShapeDtypeStruct((9, 2, 8, 8, 128), F32),
        ),
        in_specs=[pl.BlockSpec(memory_space=pltpu.SMEM)] + [anyspace] * (2 + len(NAMES)),
        out_specs=(anyspace,) * 4,
        scratch_shapes=[vm((cx, cy, nz))]
        + [vm(local[n], consts[i].dtype) for i, n in enumerate(NAMES)]
        + [
            vm(fluid.shape), vm((5, 12, 12, 8, count)),
            vm((cx, cy, nz)),
            vm((2, 128, nz)),
            vm((cx, 8, nz)),
            vm((cx + 2, cy + 16, nz)),
            vm((cx, kz, ny)),
            vm((2, nz, 128)), vm((ng, 2, kz, 128)),
            vm((nf * 8, 128)), vm((nf * 8, 128)),
            vm((nf * 8, 128)), vm((nf * 8, 128)),
            vm((ng, 2, kz, 128)), vm((2, ng, kz, 128)),
            vm((nf * 8, 128)), vm((8, 128)),
            vm((2 * nf, 8, 128)), vm((nf, 8, 128)),
            vm((5, 8, 8, count)),
            vm((5, 8, 8, 8, count)), vm((9, 2, 8, 8, 128)),
            dma((18,)), dma, dma, dma, dma,
            dma((2,)), dma((2,)), dma((2,)), dma((2,)), dma((2,)),
        ],
        compiler_params=pltpu.CompilerParams(
            collective_id=0, has_side_effects=True, vmem_limit_bytes=limit
        ),
    )(ghost, rho, fluid, *consts)
    fine, moved, potential = pl.pallas_call(
        patch_kernel,
        out_shape=(
            jax.ShapeDtypeStruct((8, 8, 8, count), F32),
            jax.ShapeDtypeStruct((5, 8, 8, 8, count), F32),
            jax.ShapeDtypeStruct((cx, cy, nz), F32),
        ),
        in_specs=[vspace, vspace, anyspace, anyspace, vspace],
        out_specs=(anyspace, anyspace, anyspace),
        scratch_shapes=[
            vm((8, 8, 8, count)), vm((5, 8, 8, 8, count)), vm((9, 2, 8, 8, 128)), vm((cx, cy, nz)), dma((10,)),
        ],
        compiler_params=pltpu.CompilerParams(vmem_limit_bytes=limit),
    )(blocks, most, packed, potential, jnp.asarray(tab["weave"]))
    return potential, fine, moved


def per_device(root_density, patch_fluid, ghost_list):
    nf = lax.axis_size("fft")
    ng = lax.axis_size("grp")
    return root_call(ghost_list[:, 0], root_density, patch_fluid, nf, ng)


def solution(mesh):
    return jax.shard_map(
        per_device,
        mesh=mesh,
        in_specs=(
            P("fft", "grp", None),
            P(None, None, None, None, ("fft", "grp")),
            P(None, ("fft", "grp"), None),
        ),
        out_specs=(
            P("fft", "grp", None),
            P(None, None, None, ("fft", "grp")),
            P(None, None, None, None, ("fft", "grp")),
        ),
        check_vma=False,
    )
```
